256 devices in a mesh: tm: 32 (over z, x), rep: 8 (over y, core).
Axes of the slice: x: 4, y: 4, z: 8, core: 2. Of those that a mesh axis runs over, the one named last changes fastest.
Arguments:
- video: bfloat16 [8, 32, 32, 16, 256], P('rep', 'tm'), may hold values from -6 to 6
- cotangent: bfloat16 [8, 32, 32, 16, 256], P('rep', 'tm'), may hold values from -24 to 24
- w_spat1: bfloat16 [3, 3, 256, 256], replicated, may hold values from -0.125 to 0.125
- w_spat2: bfloat16 [3, 3, 256, 256], replicated, may hold values from -0.125 to 0.125
- w_time1: bfloat16 [3, 256, 256], replicated, may hold values from -0.21875 to 0.21875
- w_time2: bfloat16 [3, 256, 256], replicated, may hold values from -0.21875 to 0.21875
Outputs:
- grad_input: bfloat16 [8, 32, 32, 16, 256], P('rep', 'tm')
- grad_spat1: float32 [3, 3, 256, 256], replicated
- grad_spat2: float32 [3, 3, 256, 256], replicated
- grad_time1: float32 [3, 256, 256], replicated
- grad_time2: float32 [3, 256, 256], replicated
The draws below stay inside these ranges and needn't reach their ends.
All inputs are finite; a program needn't handle non-finite values.
Results may differ from the reference program's by a relative error of at most 0.02.
Values may be sent and summed in bfloat16 or wider, within the bound.
No kernel may reach another device: no remote copies, remote signals or barrier semaphores. Data moves between devices by JAX's collectives and lax.ppermute only.
A program may use at most 64 MiB of HBM per device.

```python
import math
import jax
import jax.numpy as jnp
from jax import lax

CH = 256
ROWS = 32
COLS = 16
FRAMES = 32
VIDEOS = 8


def block_scale(stream_key, extent, cuts, least, high):
    loudness = 1.0
    for axis_at, blocks in cuts:
        steps = jax.random.uniform(jax.random.fold_in(jax.random.fold_in(stream_key, 6), axis_at), (blocks,), jnp.float32, least / len(cuts), high / len(cuts))
        loudness = loudness * jnp.repeat(jnp.exp(steps), extent[axis_at] // blocks).reshape((-1,) + (1,) * (len(extent) - 1 - axis_at))
    return loudness


def scatter_about(own_key, shape, deviation, reach, split=(), kind=jnp.bfloat16):
    entries = deviation * jax.random.normal(own_key, shape, jnp.float32)
    if split:
        entries = entries * block_scale(own_key, shape, split, -0.22, 0.18)
    return jnp.clip(entries, -reach, reach).astype(kind)


def setup_inputs(seed: int = 0) -> dict:
    seeds = jax.random.split(jax.random.key(seed), 7)
    return {
        "video": scatter_about(seeds[0], (VIDEOS, FRAMES, ROWS, COLS, CH), 1.0, 6.0, ((0, 8), (1, 32))),
        "cotangent": scatter_about(seeds[1], (VIDEOS, FRAMES, ROWS, COLS, CH), 4.0, 24.0, ((0, 8), (1, 32))),
        "w_spat1": scatter_about(seeds[2], (3, 3, CH, CH), (9 * CH) ** -0.5, 0.125),
        "w_spat2": scatter_about(seeds[3], (3, 3, CH, CH), (9 * CH) ** -0.5, 0.125),
        "w_time1": scatter_about(seeds[4], (3, CH, CH), (3 * CH) ** -0.5, 0.21875),
        "w_time2": scatter_about(seeds[5], (3, CH, CH), (3 * CH) ** -0.5, 0.21875),
    }


def matmul(left, right):
    return jnp.dot(left, right, preferred_element_type=jnp.float32)

def matmul_nt(left, right):
    return lax.dot_general(left, right, (((1,), (1,)), ((), ())), preferred_element_type=jnp.float32)

def matmul_tn(left, right):
    return lax.dot_general(left, right, (((0,), (0,)), ((), ())), preferred_element_type=jnp.float32)

def padded_slab(values):
    return jnp.pad(values, ((0, 0), (1, 1), (1, 1), (0, 0)))

def spatial_conv(values, weight):
    frames, rows, cols, channels = values.shape
    padded = padded_slab(values)
    total = jnp.zeros((frames * rows * cols, channels), jnp.float32)
    for row_tap in range(3):
        for col_tap in range(3):
            window = padded[:, row_tap:row_tap + rows, col_tap:col_tap + cols, :].reshape(-1, channels)
            total = total + matmul(window, weight[row_tap, col_tap])
    return total.reshape(values.shape)

def spatial_back(grads, weight):
    frames, rows, cols, channels = grads.shape
    padded = padded_slab(grads)
    total = jnp.zeros((frames * rows * cols, channels), jnp.float32)
    for row_tap in range(3):
        for col_tap in range(3):
            window = padded[:, 2 - row_tap:2 - row_tap + rows, 2 - col_tap:2 - col_tap + cols, :].reshape(-1, channels)
            total = total + matmul_nt(window, weight[row_tap, col_tap])
    return total.reshape(grads.shape)

def spatial_grad(values, grads):
    frames, rows, cols, channels = values.shape
    padded = padded_slab(values)
    grad_rows = grads.reshape(-1, channels)
    taps = []
    for row_tap in range(3):
        for col_tap in range(3):
            window = padded[:, row_tap:row_tap + rows, col_tap:col_tap + cols, :].reshape(-1, channels)
            taps.append(matmul_tn(window, grad_rows))
    return jnp.stack(taps).reshape(3, 3, channels, channels)

def frames_behind(values):
    count = values.shape[0]
    padded = jnp.pad(values, ((2, 0), (0, 0), (0, 0), (0, 0)))
    return [values, padded[1:1 + count], padded[0:count]]

def frames_ahead(values):
    count = values.shape[0]
    padded = jnp.pad(values, ((0, 2), (0, 0), (0, 0), (0, 0)))
    return [values, padded[1:1 + count], padded[2:2 + count]]

def silu_slope(pre):
    sigma = jax.nn.sigmoid(pre)
    return sigma * (1.0 + pre * (1.0 - sigma))

def time_block(behind, cot_ahead, w_time1, w_time2, ahead_fn):
    shape = behind[0].shape
    channels = shape[-1]
    time_pre = jnp.zeros((behind[0].size // channels, channels), jnp.float32)
    time_back = jnp.zeros_like(time_pre)
    for offset in range(3):
        time_pre = time_pre + matmul(behind[offset].reshape(-1, channels), w_time1[offset])
        time_back = time_back + matmul_nt(cot_ahead[offset].reshape(-1, channels), w_time2[offset])
    time_act = jax.nn.silu(time_pre).astype(jnp.bfloat16)
    time_grad = (time_back * silu_slope(time_pre)).astype(jnp.bfloat16)
    grad_second = jnp.stack([matmul_tn(time_act, cot_ahead[offset].reshape(-1, channels)) for offset in range(3)])
    grad_first = jnp.stack([matmul_tn(behind[offset].reshape(-1, channels), time_grad) for offset in range(3)])
    grad_ahead = ahead_fn(time_grad.reshape(shape))
    act_back = jnp.zeros_like(time_pre)
    for offset in range(3):
        act_back = act_back + matmul_nt(grad_ahead[offset].reshape(-1, channels), w_time1[offset])
    return (act_back.astype(jnp.bfloat16).reshape(shape), grad_first, grad_second)

def reference(video, cotangent, w_spat1, w_spat2, w_time1, w_time2):

    def one_video(pair):
        frames, cot = pair
        first_pre = spatial_conv(frames, w_spat1)
        first_act = jax.nn.silu(first_pre).astype(jnp.bfloat16)
        second_pre = spatial_conv(first_act, w_spat2)
        second_act = jax.nn.silu(second_pre).astype(jnp.bfloat16)
        act_back, grad_first, grad_second = time_block(frames_behind(second_act), frames_ahead(cot), w_time1, w_time2, frames_ahead)
        second_grad = (act_back.astype(jnp.float32) * silu_slope(second_pre)).astype(jnp.bfloat16)
        first_back = spatial_back(second_grad, w_spat2)
        first_grad = (first_back * silu_slope(first_pre)).astype(jnp.bfloat16)
        grad_input = spatial_back(first_grad, w_spat1).astype(jnp.bfloat16)
        return (grad_input, spatial_grad(frames, first_grad), spatial_grad(first_act, second_grad), grad_first, grad_second)
    grad_input, spat_one, spat_two, time_one, time_two = lax.map(one_video, (video, cotangent))
    scale = 1.0 / math.sqrt(VIDEOS * FRAMES * ROWS * COLS)
    return (grad_input, lax.optimization_barrier(jnp.sum(spat_one, 0)) * scale, lax.optimization_barrier(jnp.sum(spat_two, 0)) * scale, lax.optimization_barrier(jnp.sum(time_one, 0)) * scale, lax.optimization_barrier(jnp.sum(time_two, 0)) * scale)
```

```python
import math

import jax
import jax.numpy as jnp
from jax import lax
from jax.sharding import Mesh
from jax.sharding import PartitionSpec as P


def matmul(left, right):
    return jnp.dot(left, right, preferred_element_type=jnp.float32)


def matmul_nt(left, right):
    return lax.dot_general(
        left, right, (((1,), (1,)), ((), ())), preferred_element_type=jnp.float32
    )


def matmul_tn(left, right):
    return lax.dot_general(
        left, right, (((0,), (0,)), ((), ())), preferred_element_type=jnp.float32
    )


def padded_slab(values):
    return jnp.pad(values, ((0, 0), (1, 1), (1, 1), (0, 0)))


def spatial_conv(values, weight):
    frames, rows, cols, channels = values.shape
    padded = padded_slab(values)
    total = jnp.zeros((frames * rows * cols, channels), jnp.float32)
    for row_tap in range(3):
        for col_tap in range(3):
            window = padded[:, row_tap : row_tap + rows, col_tap : col_tap + cols, :].reshape(
                -1, channels
            )
            total = total + matmul(window, weight[row_tap, col_tap])
    return total.reshape(values.shape)


def spatial_back(grads, weight):
    frames, rows, cols, channels = grads.shape
    padded = padded_slab(grads)
    total = jnp.zeros((frames * rows * cols, channels), jnp.float32)
    for row_tap in range(3):
        for col_tap in range(3):
            window = padded[
                :, 2 - row_tap : 2 - row_tap + rows, 2 - col_tap : 2 - col_tap + cols, :
            ].reshape(-1, channels)
            total = total + matmul_nt(window, weight[row_tap, col_tap])
    return total.reshape(grads.shape)


def spatial_grad(values, grads):
    frames, rows, cols, channels = values.shape
    padded = padded_slab(values)
    grad_rows = grads.reshape(-1, channels)
    taps = []
    for row_tap in range(3):
        for col_tap in range(3):
            window = padded[:, row_tap : row_tap + rows, col_tap : col_tap + cols, :].reshape(
                -1, channels
            )
            taps.append(matmul_tn(window, grad_rows))
    return jnp.stack(taps).reshape(3, 3, channels, channels)


def frames_behind(values):
    count = values.shape[0]
    padded = jnp.pad(values, ((2, 0), (0, 0), (0, 0), (0, 0)))
    return [values, padded[1 : 1 + count], padded[0:count]]


def frames_ahead(values):
    count = values.shape[0]
    padded = jnp.pad(values, ((0, 2), (0, 0), (0, 0), (0, 0)))
    return [values, padded[1 : 1 + count], padded[2 : 2 + count]]


def silu_slope(pre):
    sigma = jax.nn.sigmoid(pre)
    return sigma * (1.0 + pre * (1.0 - sigma))


def time_block(behind, cot_ahead, w_time1, w_time2, ahead_fn):
    shape = behind[0].shape
    channels = shape[-1]
    time_pre = jnp.zeros((behind[0].size // channels, channels), jnp.float32)
    time_back = jnp.zeros_like(time_pre)
    for offset in range(3):
        time_pre = time_pre + matmul(behind[offset].reshape(-1, channels), w_time1[offset])
        time_back = time_back + matmul_nt(cot_ahead[offset].reshape(-1, channels), w_time2[offset])
    time_act = jax.nn.silu(time_pre).astype(jnp.bfloat16)
    time_grad = (time_back * silu_slope(time_pre)).astype(jnp.bfloat16)
    grad_second = jnp.stack(
        [matmul_tn(time_act, cot_ahead[offset].reshape(-1, channels)) for offset in range(3)]
    )
    grad_first = jnp.stack(
        [matmul_tn(behind[offset].reshape(-1, channels), time_grad) for offset in range(3)]
    )
    grad_ahead = ahead_fn(time_grad.reshape(shape))
    act_back = jnp.zeros_like(time_pre)
    for offset in range(3):
        act_back = act_back + matmul_nt(grad_ahead[offset].reshape(-1, channels), w_time1[offset])
    return (act_back.astype(jnp.bfloat16).reshape(shape), grad_first, grad_second)


def scatter_sum(values, axes, count):
    parts = values.reshape(count, -1, values.shape[-1])
    arrived = lax.all_to_all(parts, axes, 0, 0, tiled=True)
    return jnp.sum(arrived.astype(jnp.float32), axis=0).astype(jnp.bfloat16)


def gather_all(values, axes, count):
    copies = jnp.broadcast_to(values[None], (count,) + values.shape)
    arrived = lax.all_to_all(copies, axes, 0, 0, tiled=True)
    return arrived.reshape(-1, values.shape[-1])


def total_over_devices(values):
    values = scatter_sum(values, "core", 2)
    values = scatter_sum(values, ("x", "y"), 16)
    values = scatter_sum(values, "z", 8)
    values = gather_all(values, "z", 8)
    values = gather_all(values, ("x", "y"), 16)
    return gather_all(values, "core", 2)


def body(video, cotangent, w_spat1, w_spat2, w_time1, w_time2):
    frame_block = video[0]
    cot_block = cotangent[0]
    cot_ahead = frames_ahead(
        lax.all_to_all(cot_block, ("z", "x"), split_axis=1, concat_axis=0, tiled=True)
    )
    first_pre = spatial_conv(frame_block, w_spat1)
    first_act = jax.nn.silu(first_pre).astype(jnp.bfloat16)
    second_pre = spatial_conv(first_act, w_spat2)
    second_act = jax.nn.silu(second_pre).astype(jnp.bfloat16)
    tall_act = lax.all_to_all(second_act, ("z", "x"), split_axis=1, concat_axis=0, tiled=True)
    tall_back, grad_first, grad_second = time_block(
        frames_behind(tall_act), cot_ahead, w_time1, w_time2, frames_ahead
    )
    act_back = lax.all_to_all(tall_back, ("z", "x"), split_axis=0, concat_axis=1, tiled=True)
    second_grad = (act_back.astype(jnp.float32) * silu_slope(second_pre)).astype(jnp.bfloat16)
    first_back = spatial_back(second_grad, w_spat2)
    first_grad = (first_back * silu_slope(first_pre)).astype(jnp.bfloat16)
    grad_input = spatial_back(first_grad, w_spat1).astype(jnp.bfloat16)
    spat_one = spatial_grad(frame_block, first_grad)
    spat_two = spatial_grad(first_act, second_grad)
    scale = 1.0 / math.sqrt(256 * 512)
    channels = grad_first.shape[-1]
    stacked = jnp.concatenate(
        [part.reshape(-1, channels) for part in (spat_one, spat_two, grad_first, grad_second)]
    )
    summed = total_over_devices((stacked * scale).astype(jnp.bfloat16)).astype(jnp.float32)
    taps = summed.reshape(-1, channels, channels)
    spat_shape = spat_one.shape
    return (
        grad_input[None],
        taps[0:9].reshape(spat_shape),
        taps[9:18].reshape(spat_shape),
        taps[18:21],
        taps[21:24],
    )


def solution(mesh):
    fine = Mesh(mesh.devices.reshape(8, 4, 4, 2), ("z", "x", "y", "core"))
    frames = P(("y", "core"), ("z", "x"), None, None, None)
    return jax.shard_map(
        body,
        mesh=fine,
        in_specs=(frames, frames, P(), P(), P(), P()),
        out_specs=(frames, P(), P(), P(), P()),
        check_vma=False,
    )
```

```python
import math

import jax
import jax.numpy as jnp
from jax import lax
from jax.experimental import pallas as pl
from jax.experimental.pallas import tpu as pltpu
from jax.sharding import Mesh
from jax.sharding import PartitionSpec as P

CH = 256
COLS = 16
PIX = 512
PAD = PIX + 2 * COLS
SCALE = 1.0 / math.sqrt(131072)
BF = jnp.bfloat16
F32 = jnp.float32
VMEM = pl.BlockSpec(memory_space=pltpu.VMEM)
SMEM = pl.BlockSpec(memory_space=pltpu.SMEM)


def dot_nn(left, right):
    return lax.dot_general(left, right, (((1,), (0,)), ((), ())), preferred_element_type=F32)


def dot_nt(left, right):
    return lax.dot_general(left, right, (((1,), (1,)), ((), ())), preferred_element_type=F32)


def dot_tn(left, right):
    return lax.dot_general(left, right, (((0,), (0,)), ((), ())), preferred_element_type=F32)


def call(kernel, outs, ins, scratch=(), flops=0):
    specs = [SMEM if value.dtype == jnp.int32 else VMEM for value in ins]
    moved = sum(value.size * value.dtype.itemsize for value in ins)
    return pl.pallas_call(
        kernel,
        out_shape=[jax.ShapeDtypeStruct(shape, kind) for shape, kind in outs],
        in_specs=specs,
        out_specs=[VMEM] * len(outs),
        scratch_shapes=list(scratch),
        cost_estimate=pl.CostEstimate(flops=flops, bytes_accessed=moved, transcendentals=0),
        compiler_params=pltpu.CompilerParams(vmem_limit_bytes=40 * 1024 * 1024),
    )(*ins)


def fill_windows(wide, values):
    edge = jnp.zeros((COLS, 3 * CH), BF)
    wide[0:COLS, :] = edge
    wide[COLS + PIX : PAD, :] = edge
    column = lax.broadcasted_iota(jnp.int32, (PIX, CH), 0) & (COLS - 1)
    full = values.astype(F32)
    before = jnp.where(column == 0, 0.0, pltpu.roll(full, 1, 0))
    after = jnp.where(column == COLS - 1, 0.0, pltpu.roll(full, PIX - 1, 0))
    wide[COLS : COLS + PIX, 0:CH] = before.astype(BF)
    wide[COLS : COLS + PIX, CH : 2 * CH] = values.astype(BF)
    wide[COLS : COLS + PIX, 2 * CH : 3 * CH] = after.astype(BF)


def conv_from(wide, weight):
    total = None
    for tap in range(3):
        term = dot_nn(
            wide[tap * COLS : tap * COLS + PIX, :], weight[tap * 3 * CH : (tap + 1) * 3 * CH, :]
        )
        total = term if total is None else total + term
    return total


def back_from(wide, weight):
    total = None
    for tap in range(3):
        for side in range(3):
            at = (tap * 3 + side) * CH
            term = dot_nt(
                wide[(2 - tap) * COLS : (2 - tap) * COLS + PIX, (2 - side) * CH : (3 - side) * CH],
                weight[at : at + CH, :],
            )
            total = term if total is None else total + term
    return total


def silu_pair(pre):
    sigma = jax.nn.sigmoid(pre)
    act = pre * sigma
    return act, sigma * (1.0 + pre * (1.0 - sigma))


def forward_kernel(core, video, w1, w2, act2, slope1, slope2, keep, send, wide):
    values = video[...]
    fill_windows(wide, values)
    act, slope = silu_pair(conv_from(wide, w1))
    slope1[...] = slope
    first = act.astype(BF)

    @pl.when(core[0] == 0)
    def _():
        keep[...] = first
        send[...] = values

    @pl.when(core[0] != 0)
    def _():
        keep[...] = values
        send[...] = first

    fill_windows(wide, first)
    act, slope = silu_pair(conv_from(wide, w2))
    slope2[...] = slope
    act2[...] = act.astype(BF)


def ahead_sum(padded, weight):
    total = None
    for step in range(3):
        term = dot_nt(padded[step * COLS : step * COLS + PIX, :], weight[step * CH : (step + 1) * CH, :])
        total = term if total is None else total + term
    return total


def time_back_kernel(cot, wt2, back, padded):
    padded[0:PIX, :] = cot[...]
    padded[PIX:PAD, :] = jnp.zeros((2 * COLS, CH), BF)
    back[...] = ahead_sum(padded, wt2)


def time_kernel(core, act, cot, back, wt1, act_back, keep, send, padded):
    padded[0 : 2 * COLS, :] = jnp.zeros((2 * COLS, CH), BF)
    padded[2 * COLS : PAD, :] = act[...]
    pre = None
    for step in range(3):
        at = (2 - step) * COLS
        term = dot_nn(padded[at : at + PIX, :], wt1[step * CH : (step + 1) * CH, :])
        pre = term if pre is None else pre + term
    value, slope = silu_pair(pre)
    time_act = value.astype(BF)
    time_grad = (back[...] * slope).astype(BF)

    @pl.when(core[0] == 0)
    def _():
        keep[0] = act[...]
        keep[1] = time_grad
        send[0] = time_act
        send[1] = cot[...]

    @pl.when(core[0] != 0)
    def _():
        keep[0] = time_act
        keep[1] = cot[...]
        send[0] = act[...]
        send[1] = time_grad

    padded[0:PIX, :] = time_grad
    padded[PIX:PAD, :] = jnp.zeros((2 * COLS, CH), BF)
    act_back[...] = ahead_sum(padded, wt1).astype(BF)


def time_weights_kernel(keep, recv, out):
    for step in range(3):
        rows = PIX - step * COLS
        total = dot_tn(keep[0, 0:rows, :], keep[1, step * COLS : PIX, :])
        total = total + dot_tn(recv[0, 0:rows, :], recv[1, step * COLS : PIX, :])
        out[step * CH : (step + 1) * CH, :] = (total * SCALE).astype(BF)


def backward_kernel(core, act_back, slope1, slope2, w2, first_grad, keep, send, wide):
    second = (act_back[...].astype(F32) * slope2[...]).astype(BF)
    fill_windows(wide, second)
    first = (back_from(wide, w2) * slope1[...]).astype(BF)
    first_grad[...] = first

    @pl.when(core[0] == 0)
    def _():
        keep[...] = second
        send[...] = first

    @pl.when(core[0] != 0)
    def _():
        keep[...] = first
        send[...] = second


def space_weights_kernel(keep_x, recv_x, keep_g, recv_g, time_part, out, wide, other):
    fill_windows(wide, keep_x[...])
    fill_windows(other, recv_x[...])
    for tap in range(3):
        for side in range(3):
            rows = slice(tap * COLS, tap * COLS + PIX)
            lanes = slice(side * CH, (side + 1) * CH)
            total = dot_tn(wide[rows, lanes], keep_g[...])
            total = total + dot_tn(other[rows, lanes], recv_g[...])
            at = (tap * 3 + side) * CH
            out[at : at + CH, :] = (total * SCALE).astype(BF)
    out[9 * CH : 12 * CH, :] = time_part[...]


def input_kernel(first_grad, w1, out, wide):
    fill_windows(wide, first_grad[...])
    out[...] = back_from(wide, w1).astype(BF)


def swap_cores(values):
    return lax.ppermute(values, "core", [(0, 1), (1, 0)])


def swap_frames(values):
    blocks = values.reshape(PIX // COLS, COLS, CH)
    return lax.all_to_all(blocks, ("z", "x"), 0, 0, tiled=True).reshape(PIX, CH)


def scatter_sum(values, axes, count):
    parts = values.reshape(count, -1, CH)
    arrived = lax.all_to_all(parts, axes, 0, 0, tiled=True)
    return jnp.sum(arrived.astype(F32), axis=0).astype(BF)


def gather_all(values, axes, count):
    copies = jnp.broadcast_to(values[None], (count,) + values.shape)
    return lax.all_to_all(copies, axes, 0, 0, tiled=True).reshape(-1, CH)


def body(video, cotangent, w_spat1, w_spat2, w_time1, w_time2):
    core = lax.axis_index("core").astype(jnp.int32).reshape(1)
    w1, w2, wt1, wt2 = (w.reshape(-1, CH) for w in (w_spat1, w_spat2, w_time1, w_time2))
    slab, slab32 = ((PIX, CH), BF), ((PIX, CH), F32)
    pair = ((2, PIX, CH), BF)
    wide, tall = pltpu.VMEM((PAD, 3 * CH), BF), pltpu.VMEM((PAD, CH), BF)
    conv_flops, time_flops = 2 * PIX * 9 * CH * CH, 2 * PIX * 3 * CH * CH

    cot = swap_frames(cotangent.reshape(PIX, CH))
    second_act, slope1, slope2, keep_x, send_x = call(
        forward_kernel,
        [slab, slab32, slab32, slab, slab],
        (core, video.reshape(PIX, CH), w1, w2),
        [wide],
        2 * conv_flops,
    )
    act = swap_frames(second_act)
    recv_x = swap_cores(send_x)
    (time_back,) = call(time_back_kernel, [slab32], (cot, wt2), [tall], time_flops)
    act_back, keep_t, send_t = call(
        time_kernel, [slab, pair, pair], (core, act, cot, time_back, wt1), [tall], 2 * time_flops
    )
    act_back = swap_frames(act_back)
    recv_t = swap_cores(send_t)
    (time_part,) = call(
        time_weights_kernel, [((3 * CH, CH), BF)], (keep_t, recv_t), (), 2 * time_flops
    )
    first_grad, keep_g, send_g = call(
        backward_kernel, [slab, slab, slab], (core, act_back, slope1, slope2, w2), [wide], conv_flops
    )
    recv_g = swap_cores(send_g)
    (part,) = call(
        space_weights_kernel,
        [((12 * CH, CH), BF)],
        (keep_x, recv_x, keep_g, recv_g, time_part),
        [wide, wide],
        2 * conv_flops,
    )
    (grad_input,) = call(input_kernel, [slab], (first_grad, w1), [wide], conv_flops)

    part = scatter_sum(part, ("x", "y"), 16)
    part = scatter_sum(part, "z", 8)
    part = gather_all(part, "z", 8)
    part = gather_all(part, ("x", "y"), 16)
    peer = swap_cores(part)
    low = jnp.where(core[0] == 0, part, peer).astype(F32).reshape(12, CH, CH)
    high = jnp.where(core[0] == 0, peer, part).astype(F32).reshape(12, CH, CH)
    return (
        grad_input.reshape(video.shape),
        high[0:9].reshape(w_spat1.shape),
        low[0:9].reshape(w_spat2.shape),
        low[9:12],
        high[9:12],
    )


def solution(mesh):
    fine = Mesh(mesh.devices.reshape(8, 4, 4, 2), ("z", "x", "y", "core"))
    frames = P(("y", "core"), ("z", "x"), None, None, None)
    return jax.shard_map(
        body,
        mesh=fine,
        in_specs=(frames, frames, P(), P(), P(), P()),
        out_specs=(frames, P(), P(), P(), P()),
        check_vma=False,
    )
```

```python
import functools
import math

import jax
import jax.numpy as jnp
from jax import lax
from jax.experimental import pallas as pl
from jax.experimental.pallas import tpu as pltpu
from jax.sharding import Mesh
from jax.sharding import PartitionSpec as P

CH = 256
COLS = 16
PIX = 512
PAD = PIX + 2 * COLS
SCALE = 1.0 / math.sqrt(131072)
BF = jnp.bfloat16
F32 = jnp.float32
VMEM = pl.BlockSpec(memory_space=pltpu.VMEM)
SMEM = pl.BlockSpec(memory_space=pltpu.SMEM)
HBM = pl.BlockSpec(memory_space=pl.ANY)
QUARTER = 384
SIXTEENTH = 96


def dot_nn(left, right):
    return lax.dot_general(left, right, (((1,), (0,)), ((), ())), preferred_element_type=F32)


def dot_nt(left, right):
    return lax.dot_general(left, right, (((1,), (1,)), ((), ())), preferred_element_type=F32)


def dot_tn(left, right):
    return lax.dot_general(left, right, (((0,), (0,)), ((), ())), preferred_element_type=F32)


def call(kernel, outs, ins, scratch=(), flops=0, out_space=VMEM, aliases=None):
    specs = [SMEM if value.dtype == jnp.int32 else VMEM for value in ins]
    for at in aliases or {}:
        specs[at] = out_space
    moved = sum(value.size * value.dtype.itemsize for value in ins)
    return pl.pallas_call(
        kernel,
        out_shape=[jax.ShapeDtypeStruct(shape, kind) for shape, kind in outs],
        in_specs=specs,
        out_specs=[out_space] * len(outs),
        input_output_aliases=aliases or {},
        scratch_shapes=list(scratch),
        cost_estimate=pl.CostEstimate(flops=flops, bytes_accessed=moved, transcendentals=0),
        compiler_params=pltpu.CompilerParams(vmem_limit_bytes=40 * 1024 * 1024),
    )(*ins)


def fill_windows(wide, values):
    edge = jnp.zeros((COLS, 3 * CH), BF)
    wide[0:COLS, :] = edge
    wide[COLS + PIX : PAD, :] = edge
    column = lax.broadcasted_iota(jnp.int32, (PIX, CH), 0) & (COLS - 1)
    full = values.astype(F32)
    before = jnp.where(column == 0, 0.0, pltpu.roll(full, 1, 0))
    after = jnp.where(column == COLS - 1, 0.0, pltpu.roll(full, PIX - 1, 0))
    wide[COLS : COLS + PIX, 0:CH] = before.astype(BF)
    wide[COLS : COLS + PIX, CH : 2 * CH] = values.astype(BF)
    wide[COLS : COLS + PIX, 2 * CH : 3 * CH] = after.astype(BF)


def conv_from(wide, weight):
    total = None
    for tap in range(3):
        term = dot_nn(
            wide[tap * COLS : tap * COLS + PIX, :], weight[tap * 3 * CH : (tap + 1) * 3 * CH, :]
        )
        total = term if total is None else total + term
    return total


def back_from(wide, weight):
    total = None
    for tap in range(3):
        for side in range(3):
            at = (tap * 3 + side) * CH
            term = dot_nt(
                wide[(2 - tap) * COLS : (2 - tap) * COLS + PIX, (2 - side) * CH : (3 - side) * CH],
                weight[at : at + CH, :],
            )
            total = term if total is None else total + term
    return total


def silu_pair(pre):
    sigma = jax.nn.sigmoid(pre)
    act = pre * sigma
    return act, sigma * (1.0 + pre * (1.0 - sigma))


def forward_kernel(pos, video, w1, w2, act2, slope1, slope2, keep, send, wide):
    values = video[...]
    fill_windows(wide, values)
    act, slope = silu_pair(conv_from(wide, w1))
    slope1[...] = slope
    first = act.astype(BF)

    @pl.when(pos[0] == 0)
    def _():
        keep[...] = first
        send[...] = values

    @pl.when(pos[0] != 0)
    def _():
        keep[...] = values
        send[...] = first

    fill_windows(wide, first)
    act, slope = silu_pair(conv_from(wide, w2))
    slope2[...] = slope
    act2[...] = act.astype(BF)


def ahead_sum(padded, weight):
    total = None
    for step in range(3):
        term = dot_nt(padded[step * COLS : step * COLS + PIX, :], weight[step * CH : (step + 1) * CH, :])
        total = term if total is None else total + term
    return total


def time_back_kernel(cot, wt2, back, padded):
    padded[0:PIX, :] = cot[...]
    padded[PIX:PAD, :] = jnp.zeros((2 * COLS, CH), BF)
    back[...] = ahead_sum(padded, wt2)


def time_kernel(pos, act, cot, back, wt1, act_back, keep, send, padded):
    padded[0 : 2 * COLS, :] = jnp.zeros((2 * COLS, CH), BF)
    padded[2 * COLS : PAD, :] = act[...]
    pre = None
    for step in range(3):
        at = (2 - step) * COLS
        term = dot_nn(padded[at : at + PIX, :], wt1[step * CH : (step + 1) * CH, :])
        pre = term if pre is None else pre + term
    value, slope = silu_pair(pre)
    time_act = value.astype(BF)
    time_grad = (back[...] * slope).astype(BF)

    @pl.when(pos[0] == 0)
    def _():
        keep[0] = act[...]
        keep[1] = time_grad
        send[0] = time_act
        send[1] = cot[...]

    @pl.when(pos[0] != 0)
    def _():
        keep[0] = time_act
        keep[1] = cot[...]
        send[0] = act[...]
        send[1] = time_grad

    padded[0:PIX, :] = time_grad
    padded[PIX:PAD, :] = jnp.zeros((2 * COLS, CH), BF)
    act_back[...] = ahead_sum(padded, wt1).astype(BF)


def time_weights_kernel(keep, recv, out):
    for step in range(3):
        rows = PIX - step * COLS
        total = dot_tn(keep[0, 0:rows, :], keep[1, step * COLS : PIX, :])
        total = total + dot_tn(recv[0, 0:rows, :], recv[1, step * COLS : PIX, :])
        out[step * CH : (step + 1) * CH, :] = (total * SCALE).astype(BF)


def backward_kernel(pos, act_back, slope1, slope2, w2, first_grad, keep, send, wide):
    second = (act_back[...].astype(F32) * slope2[...]).astype(BF)
    fill_windows(wide, second)
    first = (back_from(wide, w2) * slope1[...]).astype(BF)
    first_grad[...] = first

    @pl.when(pos[0] == 0)
    def _():
        keep[...] = second
        send[...] = first

    @pl.when(pos[0] != 0)
    def _():
        keep[...] = first
        send[...] = second


def chunk(at, rows):
    return pl.ds(pl.multiple_of(at * rows, rows), rows)


def space_weights_kernel(pos, keep_x, recv_x, keep_g, recv_g, time_part, *rest):
    first, second = rest[0:4], rest[4:8]
    out, wide, other = rest[8:]
    fill_windows(wide, keep_x[...])
    fill_windows(other, recv_x[...])
    for tap in range(3):
        for side in range(3):
            rows = slice(tap * COLS, tap * COLS + PIX)
            lanes = slice(side * CH, (side + 1) * CH)
            total = dot_tn(wide[rows, lanes], keep_g[...])
            total = total + dot_tn(other[rows, lanes], recv_g[...])
            at = (tap * 3 + side) * CH
            out[at : at + CH, :] = (total * SCALE).astype(BF)
    out[9 * CH : 12 * CH, :] = time_part[...]
    for step in range(4):
        first[step][...] = out[chunk((pos[2] + step) & 3, QUARTER), :]
        second[step][...] = out[chunk(4 + ((pos[1] + step) & 3), QUARTER), :]


def add_up(parts):
    total = parts[0][...].astype(F32)
    for part in parts[1:]:
        total = total + part[...].astype(F32)
    return total.astype(BF)


def add_quarters_kernel(pos, *refs):
    first, second = refs[8:12], refs[12:16]
    low, high = refs[16:]
    low[...] = add_up(refs[0:4])
    high[...] = add_up(refs[4:8])
    for step in range(4):
        first[step][...] = low[chunk((pos[1] + step) & 3, SIXTEENTH), :]
        second[step][...] = high[chunk((pos[2] + step) & 3, SIXTEENTH), :]


def add_sixteenths_kernel(*refs):
    out = refs[8]
    out[0:SIXTEENTH, :] = add_up(refs[0:4])
    out[SIXTEENTH : 2 * SIXTEENTH, :] = add_up(refs[4:8])


def join_sixteenths_kernel(pos, *refs):
    low, high = refs[8:]
    for step in range(4):
        low[chunk((pos[1] - step) & 3, SIXTEENTH), :] = refs[step][...]
        high[chunk((pos[2] - step) & 3, SIXTEENTH), :] = refs[4 + step][...]


def join_quarters_kernel(pos, *refs):
    out = refs[8]
    for step in range(4):
        out[chunk((pos[2] - step) & 3, QUARTER), :] = refs[step][...]
        out[chunk(4 + ((pos[1] - step) & 3), QUARTER), :] = refs[4 + step][...]


def spread_kernel(owner, pos, half, *refs):
    spat1, spat2, time1, time2, stage, sems = refs[-6:]
    targets = [(spat2, time1), (spat1, time2)]

    def copies(at):
        space, time = targets[at]
        rows = 3 * CH
        for piece in range(3):
            part = pl.ds(piece * rows, rows)
            yield pltpu.make_async_copy(stage.at[part], space.at[part], sems.at[piece])
        yield pltpu.make_async_copy(stage.at[pl.ds(3 * rows, rows)], time, sems.at[3])

    for at in range(2):

        @pl.when((pos[0] ^ owner) == at)
        def _():
            for piece, copy in enumerate(copies(at)):
                rows = slice(piece * 3 * CH, (piece + 1) * 3 * CH)
                stage[rows, :] = half[rows, :].astype(F32)
                copy.start()
            for copy in copies(at):
                copy.wait()


def input_kernel(first_grad, w1, out, wide):
    fill_windows(wide, first_grad[...])
    out[...] = back_from(wide, w1).astype(BF)


def swap_cores(values):
    return lax.ppermute(values, "core", [(0, 1), (1, 0)])


def swap_frames(values):
    blocks = values.reshape(PIX // COLS, COLS, CH)
    return lax.all_to_all(blocks, ("z", "x"), 0, 0, tiled=True).reshape(PIX, CH)


def ring(values, axis, step):
    return lax.ppermute(values, axis, [(at, (at + step) % 4) for at in range(4)])


def exchange(own, axis):
    return [own[0]] + [ring(own[step], axis, step) for step in (1, 3, 2)]


def ordered(parts):
    return [parts[0], parts[1], parts[3], parts[2]]


def body(video, cotangent, w_spat1, w_spat2, w_time1, w_time2):
    axes = ("core", "x", "y", "z")
    pos = jnp.stack([lax.axis_index(axis) for axis in axes]).astype(jnp.int32)
    w1, w2, wt1, wt2 = (w.reshape(-1, CH) for w in (w_spat1, w_spat2, w_time1, w_time2))
    slab, slab32 = ((PIX, CH), BF), ((PIX, CH), F32)
    pair = ((2, PIX, CH), BF)
    wide, tall = pltpu.VMEM((PAD, 3 * CH), BF), pltpu.VMEM((PAD, CH), BF)
    conv_flops, time_flops = 2 * PIX * 9 * CH * CH, 2 * PIX * 3 * CH * CH

    cot = swap_frames(cotangent.reshape(PIX, CH))
    second_act, slope1, slope2, keep_x, send_x = call(
        forward_kernel,
        [slab, slab32, slab32, slab, slab],
        (pos, video.reshape(PIX, CH), w1, w2),
        [wide],
        2 * conv_flops,
    )
    act = swap_frames(second_act)
    recv_x = swap_cores(send_x)
    (time_back,) = call(time_back_kernel, [slab32], (cot, wt2), [tall], time_flops)
    act_back, keep_t, send_t = call(
        time_kernel, [slab, pair, pair], (pos, act, cot, time_back, wt1), [tall], 2 * time_flops
    )
    act_back = swap_frames(act_back)
    recv_t = swap_cores(send_t)
    (time_part,) = call(
        time_weights_kernel, [((3 * CH, CH), BF)], (keep_t, recv_t), (), 2 * time_flops
    )
    first_grad, keep_g, send_g = call(
        backward_kernel, [slab, slab, slab], (pos, act_back, slope1, slope2, w2), [wide], conv_flops
    )
    recv_g = swap_cores(send_g)
    quarter, sixteenth = ((QUARTER, CH), BF), ((SIXTEENTH, CH), BF)
    parts = call(
        space_weights_kernel,
        [quarter] * 8,
        (pos, keep_x, recv_x, keep_g, recv_g, time_part),
        [pltpu.VMEM((12 * CH, CH), BF), wide, wide],
        2 * conv_flops,
    )
    parts = ordered(exchange(parts[0:4], "y")) + ordered(exchange(parts[4:8], "x"))
    (grad_input,) = call(input_kernel, [slab], (first_grad, w1), [wide], conv_flops)
    parts = call(
        add_quarters_kernel,
        [sixteenth] * 8,
        (pos, *parts),
        [pltpu.VMEM((QUARTER, CH), BF), pltpu.VMEM((QUARTER, CH), BF)],
    )
    parts = ordered(exchange(parts[0:4], "x")) + ordered(exchange(parts[4:8], "y"))
    (part,) = call(add_sixteenths_kernel, [((2 * SIXTEENTH, CH), BF)], tuple(parts))
    part = lax.all_to_all(part.reshape(8, -1, CH), "z", 0, 0, tiled=True)
    part = jnp.sum(part.astype(F32), axis=0).astype(BF)
    part = lax.all_to_all(jnp.broadcast_to(part[None], (8,) + part.shape), "z", 0, 0, tiled=True)
    part = part.reshape(2 * SIXTEENTH, CH)
    low, high = part[0:SIXTEENTH], part[SIXTEENTH:]
    parts = ordered(exchange([low] * 4, "x")) + ordered(exchange([high] * 4, "y"))
    low, high = call(join_sixteenths_kernel, [quarter] * 2, (pos, *parts))
    parts = ordered(exchange([low] * 4, "y")) + ordered(exchange([high] * 4, "x"))
    (part,) = call(join_quarters_kernel, [((12 * CH, CH), BF)], (pos, *parts))
    peer = swap_cores(part)
    space, time = ((9 * CH, CH), F32), ((3 * CH, CH), F32)
    grads = [space, space, time, time]
    scratch = [pltpu.VMEM((12 * CH, CH), F32), pltpu.SemaphoreType.DMA((4,))]
    outs = call(functools.partial(spread_kernel, 0), grads, (pos, part), scratch, 0, HBM)
    outs = call(
        functools.partial(spread_kernel, 1),
        grads,
        (pos, peer, *outs),
        scratch,
        0,
        HBM,
        {2: 0, 3: 1, 4: 2, 5: 3},
    )
    return (
        grad_input.reshape(video.shape),
        outs[0].reshape(w_spat1.shape),
        outs[1].reshape(w_spat2.shape),
        outs[2].reshape(w_time1.shape),
        outs[3].reshape(w_time2.shape),
    )


def solution(mesh):
    fine = Mesh(mesh.devices.reshape(8, 4, 4, 2), ("z", "x", "y", "core"))
    frames = P(("y", "core"), ("z", "x"), None, None, None)
    return jax.shard_map(
        body,
        mesh=fine,
        in_specs=(frames, frames, P(), P(), P(), P()),
        out_specs=(frames, P(), P(), P(), P()),
        check_vma=False,
    )
```

```python
import functools
import math

import jax
import jax.numpy as jnp
from jax import lax
from jax.experimental import pallas as pl
from jax.experimental.pallas import tpu as pltpu
from jax.sharding import Mesh
from jax.sharding import PartitionSpec as P

CH = 256
COLS = 16
PIX = 512
PAD = PIX + 2 * COLS
SCALE = 1.0 / math.sqrt(131072)
BF = jnp.bfloat16
F32 = jnp.float32
VMEM = pl.BlockSpec(memory_space=pltpu.VMEM)
SMEM = pl.BlockSpec(memory_space=pltpu.SMEM)
HBM = pl.BlockSpec(memory_space=pltpu.HBM)


def dot_nn(left, right):
    return lax.dot_general(left, right, (((1,), (0,)), ((), ())), preferred_element_type=F32)


def dot_nt(left, right):
    return lax.dot_general(left, right, (((1,), (1,)), ((), ())), preferred_element_type=F32)


def dot_tn(left, right):
    return lax.dot_general(left, right, (((0,), (0,)), ((), ())), preferred_element_type=F32)


def call(kernel, outs, ins, scratch=(), flops=0, hbm_in=(), hbm_out=(), aliases=None, vmem=40):
    specs = [SMEM if value.dtype == jnp.int32 else VMEM for value in ins]
    for at in hbm_in:
        specs[at] = HBM
    moved = sum(value.size * value.dtype.itemsize for value in ins)
    return pl.pallas_call(
        kernel,
        out_shape=[jax.ShapeDtypeStruct(shape, kind) for shape, kind in outs],
        in_specs=specs,
        out_specs=[HBM if at in hbm_out else VMEM for at in range(len(outs))],
        scratch_shapes=list(scratch),
        input_output_aliases=aliases or {},
        cost_estimate=pl.CostEstimate(flops=flops, bytes_accessed=moved, transcendentals=0),
        compiler_params=pltpu.CompilerParams(vmem_limit_bytes=vmem * 1024 * 1024),
    )(*ins)


def start_by_core(pos, sems, first, pairs):
    for at, (even, odd, target) in enumerate(pairs):

        @pl.when(pos[0] == 0)
        def _():
            pltpu.make_async_copy(even, target, sems.at[first + at]).start()

        @pl.when(pos[0] != 0)
        def _():
            pltpu.make_async_copy(odd, target, sems.at[first + at]).start()


def wait_by_core(sems, first, pairs):
    for at, (even, _, target) in enumerate(pairs):
        pltpu.make_async_copy(even, target, sems.at[first + at]).wait()


def fill_windows(wide, values):
    edge = jnp.zeros((COLS, 3 * CH), BF)
    wide[0:COLS, :] = edge
    wide[COLS + PIX : PAD, :] = edge
    column = lax.broadcasted_iota(jnp.int32, (PIX, CH), 0) & (COLS - 1)
    full = values.astype(F32)
    before = jnp.where(column == 0, 0.0, pltpu.roll(full, 1, 0))
    after = jnp.where(column == COLS - 1, 0.0, pltpu.roll(full, PIX - 1, 0))
    wide[COLS : COLS + PIX, 0:CH] = before.astype(BF)
    wide[COLS : COLS + PIX, CH : 2 * CH] = values.astype(BF)
    wide[COLS : COLS + PIX, 2 * CH : 3 * CH] = after.astype(BF)


def conv_from(wide, weight):
    total = None
    for tap in range(3):
        term = dot_nn(
            wide[tap * COLS : tap * COLS + PIX, :], weight[tap * 3 * CH : (tap + 1) * 3 * CH, :]
        )
        total = term if total is None else total + term
    return total


def back_from(wide, weight):
    total = None
    for tap in range(3):
        for side in range(3):
            at = (tap * 3 + side) * CH
            term = dot_nt(
                wide[(2 - tap) * COLS : (2 - tap) * COLS + PIX, (2 - side) * CH : (3 - side) * CH],
                weight[at : at + CH, :],
            )
            total = term if total is None else total + term
    return total


def silu_pair(pre):
    sigma = jax.nn.sigmoid(pre)
    act = pre * sigma
    return act, sigma * (1.0 + pre * (1.0 - sigma))


def forward_kernel(pos, video_at, cot_at, w1_at, w2_at, both, slope1, slope2, keep, send, *rest):
    video, first, w1, w2, wide, sems = rest
    rows = PIX // COLS
    loads = [
        pltpu.make_async_copy(source, target, sems.at[at])
        for at, (source, target) in enumerate(
            [(video_at, video), (w1_at, w1), (w2_at, w2), (cot_at, both.at[:, COLS : 2 * COLS, :])]
        )
    ]
    for load in loads:
        load.start()
    loads[0].wait()
    fill_windows(wide, video[...])
    loads[1].wait()
    act, slope = silu_pair(conv_from(wide, w1))
    first[...] = act.astype(BF)
    stores = [(first, video, keep), (video, first, send)]
    start_by_core(pos, sems, 4, stores)
    slope1[...] = slope
    fill_windows(wide, first[...])
    loads[2].wait()
    act, slope = silu_pair(conv_from(wide, w2))
    slope2[...] = slope
    both[:, 0:COLS, :] = act.astype(BF).reshape(rows, COLS, CH)
    loads[3].wait()
    wait_by_core(sems, 4, stores)


def ahead_sum(padded, weight):
    total = None
    for step in range(3):
        term = dot_nt(padded[step * COLS : step * COLS + PIX, :], weight[step * CH : (step + 1) * CH, :])
        total = term if total is None else total + term
    return total


def time_kernel(pos, both_at, wt1_at, wt2_at, act_back, keep, send, *rest):
    act, cot, wt1, wt2, time_act, time_grad, behind, ahead, sems = rest
    loads = [
        pltpu.make_async_copy(source, target, sems.at[at])
        for at, (source, target) in enumerate(
            [
                (both_at.at[:, COLS : 2 * COLS, :], cot),
                (wt2_at, wt2),
                (both_at.at[:, 0:COLS, :], act),
                (wt1_at, wt1),
            ]
        )
    ]
    for load in loads:
        load.start()
    edge = jnp.zeros((2 * COLS, CH), BF)
    loads[0].wait()
    ahead[0:PIX, :] = cot[...].reshape(PIX, CH)
    ahead[PIX:PAD, :] = edge
    loads[1].wait()
    back = ahead_sum(ahead, wt2)
    loads[2].wait()
    behind[0 : 2 * COLS, :] = edge
    behind[2 * COLS : PAD, :] = act[...].reshape(PIX, CH)
    loads[3].wait()
    pre = None
    for step in range(3):
        at = (2 - step) * COLS
        term = dot_nn(behind[at : at + PIX, :], wt1[step * CH : (step + 1) * CH, :])
        pre = term if pre is None else pre + term
    value, slope = silu_pair(pre)
    grad = (back * slope).astype(BF)
    time_act[...] = value.astype(BF).reshape(PIX // COLS, COLS, CH)
    time_grad[...] = grad.reshape(PIX // COLS, COLS, CH)
    stores = [
        (act, time_act, keep.at[0]),
        (time_grad, cot, keep.at[1]),
        (time_act, act, send.at[0]),
        (cot, time_grad, send.at[1]),
    ]
    start_by_core(pos, sems, 4, stores)
    ahead[0:PIX, :] = grad
    act_back[...] = ahead_sum(ahead, wt1).astype(BF)
    wait_by_core(sems, 4, stores)


def time_weights_kernel(keep, recv, out):
    for step in range(3):
        rows = PIX - step * COLS
        total = dot_tn(keep[0, 0:rows, :], keep[1, step * COLS : PIX, :])
        total = total + dot_tn(recv[0, 0:rows, :], recv[1, step * COLS : PIX, :])
        out[step * CH : (step + 1) * CH, :] = (total * SCALE).astype(BF)


def backward_kernel(pos, act_back, slope1, slope2, w2, first_grad, keep, send, wide):
    second = (act_back[...].astype(F32) * slope2[...]).astype(BF)
    fill_windows(wide, second)
    first = (back_from(wide, w2) * slope1[...]).astype(BF)
    first_grad[...] = first

    @pl.when(pos[0] == 0)
    def _():
        keep[...] = second
        send[...] = first

    @pl.when(pos[0] != 0)
    def _():
        keep[...] = first
        send[...] = second


def space_weights_kernel(keep_x, recv_x, keep_g, recv_g, time_part, out, wide, other):
    fill_windows(wide, keep_x[...])
    fill_windows(other, recv_x[...])
    for tap in range(3):
        for side in range(3):
            rows = slice(tap * COLS, tap * COLS + PIX)
            lanes = slice(side * CH, (side + 1) * CH)
            total = dot_tn(wide[rows, lanes], keep_g[...])
            total = total + dot_tn(other[rows, lanes], recv_g[...])
            at = (tap * 3 + side) * CH
            out[at : at + CH, :] = (total * SCALE).astype(BF)
    out[9 * CH : 12 * CH, :] = time_part[...]


def spread_kernel(owner, pos, half, *refs):
    spat1, spat2, time1, time2, stage, sems = refs[-6:]
    targets = [(spat2, time1), (spat1, time2)]

    def copies(at):
        space, time = targets[at]
        rows = 3 * CH
        for piece in range(3):
            part = pl.ds(piece * rows, rows)
            yield pltpu.make_async_copy(stage.at[part], space.at[part], sems.at[piece])
        yield pltpu.make_async_copy(stage.at[pl.ds(3 * rows, rows)], time, sems.at[3])

    for at in range(2):

        @pl.when((pos[0] ^ owner) == at)
        def _():
            for piece, copy in enumerate(copies(at)):
                rows = slice(piece * 3 * CH, (piece + 1) * 3 * CH)
                stage[rows, :] = half[rows, :].astype(F32)
                copy.start()
            for copy in copies(at):
                copy.wait()


def input_kernel(first_grad, w1, out, wide):
    fill_windows(wide, first_grad[...])
    out[...] = back_from(wide, w1).astype(BF)


def swap_cores(values):
    return lax.ppermute(values, "core", [(0, 1), (1, 0)])


def swap_frames(values):
    blocks = values.reshape(PIX // COLS, COLS, CH)
    return lax.all_to_all(blocks, ("z", "x"), 0, 0, tiled=True).reshape(PIX, CH)


def scatter_sum(values, axes, count):
    parts = values.reshape(count, -1, CH)
    arrived = lax.all_to_all(parts, axes, 0, 0, tiled=True)
    return jnp.sum(arrived.astype(F32), axis=0).astype(BF)


def gather_all(values, axes, count):
    copies = jnp.broadcast_to(values[None], (count,) + values.shape)
    return lax.all_to_all(copies, axes, 0, 0, tiled=True).reshape(-1, CH)


def body(video, cotangent, w_spat1, w_spat2, w_time1, w_time2):
    pos = lax.axis_index("core").astype(jnp.int32).reshape(1)
    w1, w2, wt1, wt2 = (w.reshape(-1, CH) for w in (w_spat1, w_spat2, w_time1, w_time2))
    rows = PIX // COLS
    slab, slab32 = ((PIX, CH), BF), ((PIX, CH), F32)
    pair = ((2, rows, COLS, CH), BF)
    wide, tall = pltpu.VMEM((PAD, 3 * CH), BF), pltpu.VMEM((PAD, CH), BF)
    frame, lines = pltpu.VMEM((PIX, CH), BF), pltpu.VMEM((rows, COLS, CH), BF)
    space, time = pltpu.VMEM((9 * CH, CH), BF), pltpu.VMEM((3 * CH, CH), BF)
    conv_flops, time_flops = 2 * PIX * 9 * CH * CH, 2 * PIX * 3 * CH * CH

    both, slope1, slope2, keep_x, send_x = call(
        forward_kernel,
        [((rows, 2 * COLS, CH), BF), slab32, slab32, slab, slab],
        (pos, video.reshape(PIX, CH), cotangent.reshape(rows, COLS, CH), w1, w2),
        [frame, frame, space, space, wide, pltpu.SemaphoreType.DMA((6,))],
        2 * conv_flops,
        (1, 2, 3, 4),
        (3, 4),
        vmem=62,
    )
    both = lax.all_to_all(both, ("z", "x"), 0, 0, tiled=True)
    recv_x = swap_cores(send_x)
    act_back, keep_t, send_t = call(
        time_kernel,
        [slab, pair, pair],
        (pos, both, wt1, wt2),
        [lines, lines, time, time, lines, lines, tall, tall, pltpu.SemaphoreType.DMA((8,))],
        3 * time_flops,
        (1, 2, 3),
        (1, 2),
        vmem=62,
    )
    act_back = swap_frames(act_back)
    recv_t = swap_cores(send_t)
    keep_t, recv_t = keep_t.reshape(2, PIX, CH), recv_t.reshape(2, PIX, CH)
    (time_part,) = call(
        time_weights_kernel, [((3 * CH, CH), BF)], (keep_t, recv_t), (), 2 * time_flops
    )
    first_grad, keep_g, send_g = call(
        backward_kernel, [slab, slab, slab], (pos, act_back, slope1, slope2, w2), [wide], conv_flops
    )
    recv_g = swap_cores(send_g)
    (part,) = call(
        space_weights_kernel,
        [((12 * CH, CH), BF)],
        (keep_x, recv_x, keep_g, recv_g, time_part),
        [wide, wide],
        2 * conv_flops,
    )

    part = lax.all_to_all(part.reshape(16, -1, CH), ("x", "y"), 0, 0, tiled=True)
    part = jnp.sum(part.astype(F32), axis=0).astype(BF)
    part = scatter_sum(part, "z", 8)
    part = gather_all(part, "z", 8)
    part = gather_all(part, ("x", "y"), 16)
    peer = swap_cores(part)
    part, first_grad = lax.optimization_barrier((part, first_grad))
    (grad_input,) = call(input_kernel, [slab], (first_grad, w1), [wide], conv_flops)
    grads = [((9 * CH, CH), F32)] * 2 + [((3 * CH, CH), F32)] * 2
    scratch = [pltpu.VMEM((12 * CH, CH), F32), pltpu.SemaphoreType.DMA((4,))]
    outs = call(
        functools.partial(spread_kernel, 0), grads, (pos, part), scratch, 0, (), (0, 1, 2, 3)
    )
    outs = call(
        functools.partial(spread_kernel, 1),
        grads,
        (pos, peer, *outs),
        scratch,
        0,
        (2, 3, 4, 5),
        (0, 1, 2, 3),
        {2: 0, 3: 1, 4: 2, 5: 3},
    )
    return (
        grad_input.reshape(video.shape),
        outs[0].reshape(w_spat1.shape),
        outs[1].reshape(w_spat2.shape),
        outs[2].reshape(w_time1.shape),
        outs[3].reshape(w_time2.shape),
    )


def solution(mesh):
    fine = Mesh(mesh.devices.reshape(8, 4, 4, 2), ("z", "x", "y", "core"))
    frames = P(("y", "core"), ("z", "x"), None, None, None)
    return jax.shard_map(
        body,
        mesh=fine,
        in_specs=(frames, frames, P(), P(), P(), P()),
        out_specs=(frames, P(), P(), P(), P()),
        check_vma=False,
    )
```

```python
import functools
import math

import jax
import jax.numpy as jnp
from jax import lax
from jax.experimental import pallas as pl
from jax.experimental.pallas import tpu as pltpu
from jax.sharding import Mesh
from jax.sharding import PartitionSpec as P

CH = 256
COLS = 16
PIX = 512
PAD = PIX + 2 * COLS
FRAME_AXES = ("zh", "zl", "x")
SCALE = 1.0 / math.sqrt(131072)
BF = jnp.bfloat16
F32 = jnp.float32
VMEM = pl.BlockSpec(memory_space=pltpu.VMEM)
SMEM = pl.BlockSpec(memory_space=pltpu.SMEM)
HBM = pl.BlockSpec(memory_space=pltpu.HBM)


def dot_nn(left, right):
    return lax.dot_general(left, right, (((1,), (0,)), ((), ())), preferred_element_type=F32)


def dot_nt(left, right):
    return lax.dot_general(left, right, (((1,), (1,)), ((), ())), preferred_element_type=F32)


def dot_tn(left, right):
    return lax.dot_general(left, right, (((0,), (0,)), ((), ())), preferred_element_type=F32)


def call(kernel, outs, ins, scratch=(), flops=0, hbm_in=(), hbm_out=(), aliases=None, vmem=40):
    specs = [SMEM if value.dtype == jnp.int32 else VMEM for value in ins]
    for at in hbm_in:
        specs[at] = HBM
    moved = sum(value.size * value.dtype.itemsize for value in ins)
    return pl.pallas_call(
        kernel,
        out_shape=[jax.ShapeDtypeStruct(shape, kind) for shape, kind in outs],
        in_specs=specs,
        out_specs=[HBM if at in hbm_out else VMEM for at in range(len(outs))],
        scratch_shapes=list(scratch),
        input_output_aliases=aliases or {},
        cost_estimate=pl.CostEstimate(flops=flops, bytes_accessed=moved, transcendentals=0),
        compiler_params=pltpu.CompilerParams(vmem_limit_bytes=vmem * 1024 * 1024),
    )(*ins)


def start_by_core(pos, sems, first, pairs):
    for at, (even, odd, target) in enumerate(pairs):

        @pl.when(pos[0] == 0)
        def _():
            pltpu.make_async_copy(even, target, sems.at[first + at]).start()

        @pl.when(pos[0] != 0)
        def _():
            pltpu.make_async_copy(odd, target, sems.at[first + at]).start()


def wait_by_core(sems, first, pairs):
    for at, (even, _, target) in enumerate(pairs):
        pltpu.make_async_copy(even, target, sems.at[first + at]).wait()


def fill_windows(wide, values):
    edge = jnp.zeros((COLS, 3 * CH), BF)
    wide[0:COLS, :] = edge
    wide[COLS + PIX : PAD, :] = edge
    column = lax.broadcasted_iota(jnp.int32, (PIX, CH), 0) & (COLS - 1)
    full = values.astype(F32)
    before = jnp.where(column == 0, 0.0, pltpu.roll(full, 1, 0))
    after = jnp.where(column == COLS - 1, 0.0, pltpu.roll(full, PIX - 1, 0))
    wide[COLS : COLS + PIX, 0:CH] = before.astype(BF)
    wide[COLS : COLS + PIX, CH : 2 * CH] = values.astype(BF)
    wide[COLS : COLS + PIX, 2 * CH : 3 * CH] = after.astype(BF)


def conv_from(wide, weight):
    total = None
    for tap in range(3):
        term = dot_nn(
            wide[tap * COLS : tap * COLS + PIX, :], weight[tap * 3 * CH : (tap + 1) * 3 * CH, :]
        )
        total = term if total is None else total + term
    return total


def back_from(wide, weight):
    total = None
    for tap in range(3):
        for side in range(3):
            at = (tap * 3 + side) * CH
            term = dot_nt(
                wide[(2 - tap) * COLS : (2 - tap) * COLS + PIX, (2 - side) * CH : (3 - side) * CH],
                weight[at : at + CH, :],
            )
            total = term if total is None else total + term
    return total


def silu_pair(pre):
    sigma = jax.nn.sigmoid(pre)
    act = pre * sigma
    return act, sigma * (1.0 + pre * (1.0 - sigma))


def forward_kernel(pos, video_at, cot_at, w1_at, w2_at, both, slopes, keep, send, *rest):
    video, first, w1, w2, wide, sems = rest
    rows = PIX // COLS
    loads = [
        pltpu.make_async_copy(source, target, sems.at[at])
        for at, (source, target) in enumerate(
            [(video_at, video), (w1_at, w1), (w2_at, w2), (cot_at, both.at[:, COLS : 2 * COLS, :])]
        )
    ]
    for load in loads:
        load.start()
    loads[0].wait()
    fill_windows(wide, video[...])
    loads[1].wait()
    act, slope = silu_pair(conv_from(wide, w1))
    first[...] = act.astype(BF)
    stores = [(first, video, keep), (video, first, send)]
    start_by_core(pos, sems, 4, stores)
    slopes[0:PIX, :] = slope
    fill_windows(wide, first[...])
    loads[2].wait()
    act, slope = silu_pair(conv_from(wide, w2))
    slopes[PIX : 2 * PIX, :] = slope
    both[:, 0:COLS, :] = act.astype(BF).reshape(rows, COLS, CH)
    loads[3].wait()
    wait_by_core(sems, 4, stores)


def ahead_sum(padded, weight):
    total = None
    for step in range(3):
        term = dot_nt(padded[step * COLS : step * COLS + PIX, :], weight[step * CH : (step + 1) * CH, :])
        total = term if total is None else total + term
    return total


def time_kernel(pos, both_at, wt1_at, wt2_at, act_back, keep, send, *rest):
    act, cot, wt1, wt2, time_act, time_grad, behind, ahead, sems = rest
    loads = [
        pltpu.make_async_copy(source, target, sems.at[at])
        for at, (source, target) in enumerate(
            [
                (both_at.at[:, COLS : 2 * COLS, :], cot),
                (wt2_at, wt2),
                (both_at.at[:, 0:COLS, :], act),
                (wt1_at, wt1),
            ]
        )
    ]
    for load in loads:
        load.start()
    edge = jnp.zeros((2 * COLS, CH), BF)
    loads[0].wait()
    ahead[0:PIX, :] = cot[...].reshape(PIX, CH)
    ahead[PIX:PAD, :] = edge
    loads[1].wait()
    back = ahead_sum(ahead, wt2)
    loads[2].wait()
    behind[0 : 2 * COLS, :] = edge
    behind[2 * COLS : PAD, :] = act[...].reshape(PIX, CH)
    loads[3].wait()
    pre = None
    for step in range(3):
        at = (2 - step) * COLS
        term = dot_nn(behind[at : at + PIX, :], wt1[step * CH : (step + 1) * CH, :])
        pre = term if pre is None else pre + term
    value, slope = silu_pair(pre)
    grad = (back * slope).astype(BF)
    time_act[...] = value.astype(BF).reshape(PIX // COLS, COLS, CH)
    time_grad[...] = grad.reshape(PIX // COLS, COLS, CH)
    stores = [
        (act, time_act, keep.at[0]),
        (time_grad, cot, keep.at[1]),
        (time_act, act, send.at[0]),
        (cot, time_grad, send.at[1]),
    ]
    start_by_core(pos, sems, 4, stores)
    ahead[0:PIX, :] = grad
    act_back[...] = ahead_sum(ahead, wt1).astype(BF)
    wait_by_core(sems, 4, stores)


def time_weights_kernel(keep, recv, out):
    for step in range(3):
        rows = PIX - step * COLS
        total = dot_tn(keep[0, 0:rows, :], keep[1, step * COLS : PIX, :])
        total = total + dot_tn(recv[0, 0:rows, :], recv[1, step * COLS : PIX, :])
        out[step * CH : (step + 1) * CH, :] = (total * SCALE).astype(BF)


def backward_kernel(pos, act_back, slopes, w2, first_grad, keep, send, wide):
    second = (act_back[...].astype(F32) * slopes[PIX : 2 * PIX, :]).astype(BF)
    fill_windows(wide, second)
    first = (back_from(wide, w2) * slopes[0:PIX, :]).astype(BF)
    first_grad[...] = first

    @pl.when(pos[0] == 0)
    def _():
        keep[...] = second
        send[...] = first

    @pl.when(pos[0] != 0)
    def _():
        keep[...] = first
        send[...] = second


def space_weights_kernel(keep_x, recv_x, keep_g, recv_g, time_part, out, wide, other):
    fill_windows(wide, keep_x[...])
    fill_windows(other, recv_x[...])
    for tap in range(3):
        for side in range(3):
            rows = slice(tap * COLS, tap * COLS + PIX)
            lanes = slice(side * CH, (side + 1) * CH)
            total = dot_tn(wide[rows, lanes], keep_g[...])
            total = total + dot_tn(other[rows, lanes], recv_g[...])
            at = (tap * 3 + side) * CH
            out[at : at + CH, :] = (total * SCALE).astype(BF)
    out[9 * CH : 12 * CH, :] = time_part[...]


def spread_kernel(owner, pos, half, *refs):
    spat1, spat2, time1, time2, stage, sems = refs[-6:]
    targets = [(spat2, time1), (spat1, time2)]

    def copies(at):
        space, time = targets[at]
        rows = 3 * CH
        for piece in range(3):
            part = pl.ds(piece * rows, rows)
            yield pltpu.make_async_copy(stage.at[part], space.at[part], sems.at[piece])
        yield pltpu.make_async_copy(stage.at[pl.ds(3 * rows, rows)], time, sems.at[3])

    for at in range(2):

        @pl.when((pos[0] ^ owner) == at)
        def _():
            for piece, copy in enumerate(copies(at)):
                rows = slice(piece * 3 * CH, (piece + 1) * 3 * CH)
                stage[rows, :] = half[rows, :].astype(F32)
                copy.start()
            for copy in copies(at):
                copy.wait()


def input_kernel(first_grad, w1, out, wide):
    fill_windows(wide, first_grad[...])
    out[...] = back_from(wide, w1).astype(BF)


def swap_cores(values):
    return lax.ppermute(values, "core", [(0, 1), (1, 0)])


def swap_frames(values):
    blocks = values.reshape(PIX // COLS, COLS, CH)
    return lax.all_to_all(blocks, FRAME_AXES, 0, 0, tiled=True).reshape(PIX, CH)


def scatter_sum(values, axes, count):
    parts = values.reshape(count, -1, CH)
    arrived = lax.all_to_all(parts, axes, 0, 0, tiled=True)
    return jnp.sum(arrived.astype(F32), axis=0).astype(BF)


def gather_all(values, axes, count):
    copies = jnp.broadcast_to(values[None], (count,) + values.shape)
    return lax.all_to_all(copies, axes, 0, 0, tiled=True).reshape(-1, CH)


def body(video, cotangent, w_spat1, w_spat2, w_time1, w_time2):
    pos = lax.axis_index("core").astype(jnp.int32).reshape(1)
    w1, w2, wt1, wt2 = (w.reshape(-1, CH) for w in (w_spat1, w_spat2, w_time1, w_time2))
    rows = PIX // COLS
    slab = ((PIX, CH), BF)
    pair = ((2, rows, COLS, CH), BF)
    wide, tall = pltpu.VMEM((PAD, 3 * CH), BF), pltpu.VMEM((PAD, CH), BF)
    frame, lines = pltpu.VMEM((PIX, CH), BF), pltpu.VMEM((rows, COLS, CH), BF)
    space, time = pltpu.VMEM((9 * CH, CH), BF), pltpu.VMEM((3 * CH, CH), BF)
    conv_flops, time_flops = 2 * PIX * 9 * CH * CH, 2 * PIX * 3 * CH * CH

    both, slopes, keep_x, send_x = call(
        forward_kernel,
        [((rows, 2 * COLS, CH), BF), ((2 * PIX, CH), F32), slab, slab],
        (pos, video.reshape(PIX, CH), cotangent.reshape(rows, COLS, CH), w1, w2),
        [frame, frame, space, space, wide, pltpu.SemaphoreType.DMA((6,))],
        2 * conv_flops,
        (1, 2, 3, 4),
        (2, 3),
        vmem=60,
    )
    both = lax.all_to_all(both, FRAME_AXES, 0, 0, tiled=True)
    recv_x = swap_cores(send_x)
    act_back, keep_t, send_t = call(
        time_kernel,
        [slab, pair, pair],
        (pos, both, wt1, wt2),
        [lines, lines, time, time, lines, lines, tall, tall, pltpu.SemaphoreType.DMA((8,))],
        3 * time_flops,
        (1, 2, 3),
        (1, 2),
        vmem=60,
    )
    act_back = swap_frames(act_back)
    recv_t = swap_cores(send_t)
    keep_t, recv_t = keep_t.reshape(2, PIX, CH), recv_t.reshape(2, PIX, CH)
    (time_part,) = call(
        time_weights_kernel, [((3 * CH, CH), BF)], (keep_t, recv_t), (), 2 * time_flops
    )
    first_grad, keep_g, send_g = call(
        backward_kernel, [slab, slab, slab], (pos, act_back, slopes, w2), [wide], conv_flops
    )
    recv_g = swap_cores(send_g)
    (part,) = call(
        space_weights_kernel,
        [((12 * CH, CH), BF)],
        (keep_x, recv_x, keep_g, recv_g, time_part),
        [wide, wide],
        2 * conv_flops,
    )

    part = scatter_sum(part, ("zl", "x", "y"), 32)
    part = jnp.sum(gather_all(part, "zh", 4).reshape(4, -1, CH).astype(F32), axis=0).astype(BF)
    part = gather_all(part, ("zl", "x", "y"), 32)
    peer = swap_cores(part)
    part, first_grad = lax.optimization_barrier((part, first_grad))
    (grad_input,) = call(input_kernel, [slab], (first_grad, w1), [wide], conv_flops)
    grads = [((9 * CH, CH), F32)] * 2 + [((3 * CH, CH), F32)] * 2
    scratch = [pltpu.VMEM((12 * CH, CH), F32), pltpu.SemaphoreType.DMA((4,))]
    outs = call(
        functools.partial(spread_kernel, 0), grads, (pos, part), scratch, 0, (), (0, 1, 2, 3)
    )
    outs = call(
        functools.partial(spread_kernel, 1),
        grads,
        (pos, peer, *outs),
        scratch,
        0,
        (2, 3, 4, 5),
        (0, 1, 2, 3),
        {2: 0, 3: 1, 4: 2, 5: 3},
    )
    return (
        grad_input.reshape(video.shape),
        outs[0].reshape(w_spat1.shape),
        outs[1].reshape(w_spat2.shape),
        outs[2].reshape(w_time1.shape),
        outs[3].reshape(w_time2.shape),
    )


def solution(mesh):
    fine = Mesh(mesh.devices.reshape(4, 2, 4, 4, 2), ("zh", "zl", "x", "y", "core"))
    frames = P(("y", "core"), FRAME_AXES, None, None, None)
    return jax.shard_map(
        body,
        mesh=fine,
        in_specs=(frames, frames, P(), P(), P(), P()),
        out_specs=(frames, P(), P(), P(), P()),
        check_vma=False,
    )
```

```python
import functools
import math

import jax
import jax.numpy as jnp
from jax import lax
from jax.experimental import pallas as pl
from jax.experimental.pallas import tpu as pltpu
from jax.sharding import Mesh
from jax.sharding import PartitionSpec as P

CH = 256
COLS = 16
PIX = 512
PAD = PIX + 2 * COLS
FRAME_AXES = ("zh", "zl", "x")
SCALE = 1.0 / math.sqrt(131072)
BF = jnp.bfloat16
F32 = jnp.float32
VMEM = pl.BlockSpec(memory_space=pltpu.VMEM)
SMEM = pl.BlockSpec(memory_space=pltpu.SMEM)
HBM = pl.BlockSpec(memory_space=pltpu.HBM)


def dot_nn(left, right):
    return lax.dot_general(left, right, (((1,), (0,)), ((), ())), preferred_element_type=F32)


def dot_nt(left, right):
    return lax.dot_general(left, right, (((1,), (1,)), ((), ())), preferred_element_type=F32)


def dot_tn(left, right):
    return lax.dot_general(left, right, (((0,), (0,)), ((), ())), preferred_element_type=F32)


def call(kernel, outs, ins, scratch=(), flops=0, hbm_in=(), hbm_out=(), aliases=None, vmem=40):
    specs = [SMEM if value.dtype == jnp.int32 else VMEM for value in ins]
    for at in hbm_in:
        specs[at] = HBM
    moved = sum(value.size * value.dtype.itemsize for value in ins)
    return pl.pallas_call(
        kernel,
        out_shape=[jax.ShapeDtypeStruct(shape, kind) for shape, kind in outs],
        in_specs=specs,
        out_specs=[HBM if at in hbm_out else VMEM for at in range(len(outs))],
        scratch_shapes=list(scratch),
        input_output_aliases=aliases or {},
        cost_estimate=pl.CostEstimate(flops=flops, bytes_accessed=moved, transcendentals=0),
        compiler_params=pltpu.CompilerParams(vmem_limit_bytes=vmem * 1024 * 1024),
    )(*ins)


def start_by_core(pos, sems, first, pairs):
    for at, (even, odd, target) in enumerate(pairs):

        @pl.when(pos[0] == 0)
        def _():
            pltpu.make_async_copy(even, target, sems.at[first + at]).start()

        @pl.when(pos[0] != 0)
        def _():
            pltpu.make_async_copy(odd, target, sems.at[first + at]).start()


def wait_by_core(sems, first, pairs):
    for at, (even, _, target) in enumerate(pairs):
        pltpu.make_async_copy(even, target, sems.at[first + at]).wait()


def fill_windows(wide, values):
    edge = jnp.zeros((COLS, 3 * CH), BF)
    wide[0:COLS, :] = edge
    wide[COLS + PIX : PAD, :] = edge
    column = lax.broadcasted_iota(jnp.int32, (PIX, CH), 0) & (COLS - 1)
    full = values.astype(F32)
    before = jnp.where(column == 0, 0.0, pltpu.roll(full, 1, 0))
    after = jnp.where(column == COLS - 1, 0.0, pltpu.roll(full, PIX - 1, 0))
    wide[COLS : COLS + PIX, 0:CH] = before.astype(BF)
    wide[COLS : COLS + PIX, CH : 2 * CH] = values.astype(BF)
    wide[COLS : COLS + PIX, 2 * CH : 3 * CH] = after.astype(BF)


def conv_from(wide, weight, loads=(None, None, None)):
    total = None
    for tap, load in enumerate(loads):
        if load is not None:
            load.wait()
        term = dot_nn(
            wide[tap * COLS : tap * COLS + PIX, :], weight[tap * 3 * CH : (tap + 1) * 3 * CH, :]
        )
        total = term if total is None else total + term
    return total


def back_from(wide, weight):
    total = None
    for tap in range(3):
        for side in range(3):
            at = (tap * 3 + side) * CH
            term = dot_nt(
                wide[(2 - tap) * COLS : (2 - tap) * COLS + PIX, (2 - side) * CH : (3 - side) * CH],
                weight[at : at + CH, :],
            )
            total = term if total is None else total + term
    return total


def silu_pair(pre):
    sigma = 0.5 + 0.5 * jnp.tanh(0.5 * pre)
    act = pre * sigma
    return act, sigma * (1.0 + pre * (1.0 - sigma))


def forward_kernel(pos, video_at, cot_at, w1_at, w2_at, both_at, slopes_at, keep, send, *rest):
    video, first, act2, slopes, w1, w2, wide, sems = rest
    pieces = [(video_at, video)]
    for source, target in ((w1_at, w1), (w2_at, w2)):
        for tap in range(3):
            part = pl.ds(tap * 3 * CH, 3 * CH)
            pieces.append((source.at[part], target.at[part]))
    pieces.append((cot_at, both_at.at[:, COLS : 2 * COLS, :]))
    pieces.append((slopes.at[0], slopes_at.at[0]))
    pieces.append((slopes.at[1], slopes_at.at[1]))
    pieces.append((act2, both_at.at[:, 0:COLS, :]))
    moves = [
        pltpu.make_async_copy(source, target, sems.at[at])
        for at, (source, target) in enumerate(pieces)
    ]
    for move in moves[0:8]:
        move.start()
    moves[0].wait()
    fill_windows(wide, video[...])
    act, slope = silu_pair(conv_from(wide, w1, moves[1:4]))
    first[...] = act.astype(BF)
    stores = [(first, video, keep), (video, first, send)]
    start_by_core(pos, sems, 11, stores)
    slopes[0] = slope.astype(BF)
    moves[8].start()
    fill_windows(wide, first[...])
    act, slope = silu_pair(conv_from(wide, w2, moves[4:7]))
    act2[...] = act.astype(BF).reshape(PIX // COLS, COLS, CH)
    moves[10].start()
    slopes[1] = slope.astype(BF)
    moves[9].start()
    for move in moves[7:11]:
        move.wait()
    wait_by_core(sems, 11, stores)


def ahead_sum(padded, weight):
    total = None
    for step in range(3):
        term = dot_nt(padded[step * COLS : step * COLS + PIX, :], weight[step * CH : (step + 1) * CH, :])
        total = term if total is None else total + term
    return total


def time_kernel(pos, both_at, wt1_at, wt2_at, back_at, keep, send, *rest):
    act, cot, wt1, wt2, time_act, time_grad, act_back, behind, ahead, sems = rest
    loads = [
        pltpu.make_async_copy(source, target, sems.at[at])
        for at, (source, target) in enumerate(
            [
                (both_at.at[:, COLS : 2 * COLS, :], cot),
                (wt2_at, wt2),
                (both_at.at[:, 0:COLS, :], act),
                (wt1_at, wt1),
            ]
        )
    ]
    for load in loads:
        load.start()
    edge = jnp.zeros((2 * COLS, CH), BF)
    loads[0].wait()
    ahead[0:PIX, :] = cot[...].reshape(PIX, CH)
    ahead[PIX:PAD, :] = edge
    loads[1].wait()
    back = ahead_sum(ahead, wt2)
    loads[2].wait()
    behind[0 : 2 * COLS, :] = edge
    behind[2 * COLS : PAD, :] = act[...].reshape(PIX, CH)
    loads[3].wait()
    pre = None
    for step in range(3):
        at = (2 - step) * COLS
        term = dot_nn(behind[at : at + PIX, :], wt1[step * CH : (step + 1) * CH, :])
        pre = term if pre is None else pre + term
    value, slope = silu_pair(pre)
    grad = (back * slope).astype(BF)
    time_act[...] = value.astype(BF).reshape(PIX // COLS, COLS, CH)
    time_grad[...] = grad.reshape(PIX // COLS, COLS, CH)
    stores = [
        (act, time_act, keep.at[0]),
        (time_grad, cot, keep.at[1]),
        (time_act, act, send.at[0]),
        (cot, time_grad, send.at[1]),
    ]
    start_by_core(pos, sems, 4, stores)
    ahead[0:PIX, :] = grad
    act_back[...] = ahead_sum(ahead, wt1).astype(BF)
    last = pltpu.make_async_copy(act_back, back_at, sems.at[8])
    last.start()
    wait_by_core(sems, 4, stores)
    last.wait()


def time_weights_kernel(keep, recv, out):
    for step in range(3):
        rows = PIX - step * COLS
        total = dot_tn(keep[0, 0:rows, :], keep[1, step * COLS : PIX, :])
        total = total + dot_tn(recv[0, 0:rows, :], recv[1, step * COLS : PIX, :])
        out[step * CH : (step + 1) * CH, :] = (total * SCALE).astype(BF)


def backward_kernel(pos, act_back, slopes, w2, first_grad, keep, send, wide):
    second = (act_back[...].astype(F32) * slopes[1].astype(F32)).astype(BF)
    fill_windows(wide, second)
    first = (back_from(wide, w2) * slopes[0].astype(F32)).astype(BF)
    first_grad[...] = first

    @pl.when(pos[0] == 0)
    def _():
        keep[...] = second
        send[...] = first

    @pl.when(pos[0] != 0)
    def _():
        keep[...] = first
        send[...] = second


def space_weights_kernel(keep_x, recv_x, keep_g, recv_g, time_part, out, wide, other):
    fill_windows(wide, keep_x[...])
    fill_windows(other, recv_x[...])
    for tap in range(3):
        for side in range(3):
            rows = slice(tap * COLS, tap * COLS + PIX)
            lanes = slice(side * CH, (side + 1) * CH)
            total = dot_tn(wide[rows, lanes], keep_g[...])
            total = total + dot_tn(other[rows, lanes], recv_g[...])
            at = (tap * 3 + side) * CH
            out[at : at + CH, :] = (total * SCALE).astype(BF)
    out[9 * CH : 12 * CH, :] = time_part[...]


def spread_kernel(owner, pos, half, *refs):
    spat1, spat2, time1, time2, stage, sems = refs[-6:]
    targets = [(spat2, time1), (spat1, time2)]

    def copies(at):
        space, time = targets[at]
        rows = 3 * CH
        for piece in range(3):
            part = pl.ds(piece * rows, rows)
            yield pltpu.make_async_copy(stage.at[part], space.at[part], sems.at[piece])
        yield pltpu.make_async_copy(stage.at[pl.ds(3 * rows, rows)], time, sems.at[3])

    for at in range(2):

        @pl.when((pos[0] ^ owner) == at)
        def _():
            for piece, copy in enumerate(copies(at)):
                rows = slice(piece * 3 * CH, (piece + 1) * 3 * CH)
                stage[rows, :] = half[rows, :].astype(F32)
                copy.start()
            for copy in copies(at):
                copy.wait()


def input_kernel(first_grad, w1, out, wide):
    fill_windows(wide, first_grad[...])
    out[...] = back_from(wide, w1).astype(BF)


def swap_cores(values):
    return lax.ppermute(values, "core", [(0, 1), (1, 0)])


def swap_frames(values):
    blocks = values.reshape(PIX // COLS, COLS, CH)
    return lax.all_to_all(blocks, FRAME_AXES, 0, 0, tiled=True).reshape(PIX, CH)


def gather_all(values, axes, count):
    copies = jnp.broadcast_to(values[None], (count,) + values.shape)
    return lax.all_to_all(copies, axes, 0, 0, tiled=True).reshape(-1, CH)


def body(video, cotangent, w_spat1, w_spat2, w_time1, w_time2):
    pos = lax.axis_index("core").astype(jnp.int32).reshape(1)
    w1, w2, wt1, wt2 = (w.reshape(-1, CH) for w in (w_spat1, w_spat2, w_time1, w_time2))
    rows = PIX // COLS
    slab = ((PIX, CH), BF)
    pair = ((2, rows, COLS, CH), BF)
    wide, tall = pltpu.VMEM((PAD, 3 * CH), BF), pltpu.VMEM((PAD, CH), BF)
    frame, lines = pltpu.VMEM((PIX, CH), BF), pltpu.VMEM((rows, COLS, CH), BF)
    both_slopes = pltpu.VMEM((2, PIX, CH), BF)
    space, time = pltpu.VMEM((9 * CH, CH), BF), pltpu.VMEM((3 * CH, CH), BF)
    conv_flops, time_flops = 2 * PIX * 9 * CH * CH, 2 * PIX * 3 * CH * CH

    both, slopes, keep_x, send_x = call(
        forward_kernel,
        [((rows, 2 * COLS, CH), BF), ((2, PIX, CH), BF), slab, slab],
        (pos, video.reshape(PIX, CH), cotangent.reshape(rows, COLS, CH), w1, w2),
        [frame, frame, lines, both_slopes, space, space, wide, pltpu.SemaphoreType.DMA((13,))],
        2 * conv_flops,
        (1, 2, 3, 4),
        (0, 1, 2, 3),
        vmem=60,
    )
    both = lax.all_to_all(both, FRAME_AXES, 0, 0, tiled=True)
    recv_x = swap_cores(send_x)
    act_back, keep_t, send_t = call(
        time_kernel,
        [slab, pair, pair],
        (pos, both, wt1, wt2),
        [lines, lines, time, time, lines, lines, frame, tall, tall, pltpu.SemaphoreType.DMA((9,))],
        3 * time_flops,
        (1, 2, 3),
        (0, 1, 2),
        vmem=60,
    )
    act_back = swap_frames(act_back)
    recv_t = swap_cores(send_t)
    keep_t, recv_t = keep_t.reshape(2, PIX, CH), recv_t.reshape(2, PIX, CH)
    (time_part,) = call(
        time_weights_kernel, [((3 * CH, CH), BF)], (keep_t, recv_t), (), 2 * time_flops
    )
    first_grad, keep_g, send_g = call(
        backward_kernel, [slab, slab, slab], (pos, act_back, slopes, w2), [wide], conv_flops
    )
    recv_g = swap_cores(send_g)
    (part,) = call(
        space_weights_kernel,
        [((12 * CH, CH), BF)],
        (keep_x, recv_x, keep_g, recv_g, time_part),
        [wide, wide],
        2 * conv_flops,
    )

    (grad_input,) = call(input_kernel, [slab], (first_grad, w1), [wide], conv_flops)
    part = lax.all_to_all(part.reshape(32, -1, CH), ("zl", "x", "y"), 0, 0, tiled=True)
    part, grad_input = lax.optimization_barrier((part, grad_input))
    part = jnp.sum(part.astype(F32), axis=0).astype(BF)
    near, far, other = (
        lax.ppermute(part, "zh", [(at, (at + step) % 4) for at in range(4)]).astype(F32)
        for step in (1, 3, 2)
    )
    part = ((part.astype(F32) + other) + (near + far)).astype(BF)
    part = gather_all(part, ("zl", "x", "y"), 32)
    peer = swap_cores(part)
    grads = [((9 * CH, CH), F32)] * 2 + [((3 * CH, CH), F32)] * 2
    scratch = [pltpu.VMEM((12 * CH, CH), F32), pltpu.SemaphoreType.DMA((4,))]
    outs = call(
        functools.partial(spread_kernel, 0), grads, (pos, part), scratch, 0, (), (0, 1, 2, 3)
    )
    outs = call(
        functools.partial(spread_kernel, 1),
        grads,
        (pos, peer, *outs),
        scratch,
        0,
        (2, 3, 4, 5),
        (0, 1, 2, 3),
        {2: 0, 3: 1, 4: 2, 5: 3},
    )
    return (
        grad_input.reshape(video.shape),
        outs[0].reshape(w_spat1.shape),
        outs[1].reshape(w_spat2.shape),
        outs[2].reshape(w_time1.shape),
        outs[3].reshape(w_time2.shape),
    )


def solution(mesh):
    fine = Mesh(mesh.devices.reshape(4, 2, 4, 4, 2), ("zh", "zl", "x", "y", "core"))
    frames = P(("y", "core"), FRAME_AXES, None, None, None)
    return jax.shard_map(
        body,
        mesh=fine,
        in_specs=(frames, frames, P(), P(), P(), P()),
        out_specs=(frames, P(), P(), P(), P()),
        check_vma=False,
    )
```

```python
import functools
import math

import jax
import jax.numpy as jnp
from jax import lax
from jax.experimental import pallas as pl
from jax.experimental.pallas import tpu as pltpu
from jax.sharding import Mesh
from jax.sharding import PartitionSpec as P

CH = 256
COLS = 16
PIX = 512
PAD = PIX + 2 * COLS
FRAME_AXES = ("zh", "zl", "x")
SCALE = 1.0 / math.sqrt(131072)
BF = jnp.bfloat16
F32 = jnp.float32
VMEM = pl.BlockSpec(memory_space=pltpu.VMEM)
SMEM = pl.BlockSpec(memory_space=pltpu.SMEM)
HBM = pl.BlockSpec(memory_space=pltpu.HBM)


def dot_nn(left, right):
    return lax.dot_general(left, right, (((1,), (0,)), ((), ())), preferred_element_type=F32)


def dot_nt(left, right):
    return lax.dot_general(left, right, (((1,), (1,)), ((), ())), preferred_element_type=F32)


def dot_tn(left, right):
    return lax.dot_general(left, right, (((0,), (0,)), ((), ())), preferred_element_type=F32)


def call(kernel, outs, ins, scratch=(), flops=0, hbm_in=(), hbm_out=(), aliases=None, vmem=40):
    specs = [SMEM if value.dtype == jnp.int32 else VMEM for value in ins]
    for at in hbm_in:
        specs[at] = HBM
    moved = sum(value.size * value.dtype.itemsize for value in ins)
    return pl.pallas_call(
        kernel,
        out_shape=[jax.ShapeDtypeStruct(shape, kind) for shape, kind in outs],
        in_specs=specs,
        out_specs=[HBM if at in hbm_out else VMEM for at in range(len(outs))],
        scratch_shapes=list(scratch),
        input_output_aliases=aliases or {},
        cost_estimate=pl.CostEstimate(flops=flops, bytes_accessed=moved, transcendentals=0),
        compiler_params=pltpu.CompilerParams(vmem_limit_bytes=vmem * 1024 * 1024),
    )(*ins)


def start_by_core(pos, sems, first, pairs):
    for at, (even, odd, target) in enumerate(pairs):

        @pl.when(pos[0] == 0)
        def _():
            pltpu.make_async_copy(even, target, sems.at[first + at]).start()

        @pl.when(pos[0] != 0)
        def _():
            pltpu.make_async_copy(odd, target, sems.at[first + at]).start()


def wait_by_core(sems, first, pairs):
    for at, (even, _, target) in enumerate(pairs):
        pltpu.make_async_copy(even, target, sems.at[first + at]).wait()


def fill_windows(wide, values):
    edge = jnp.zeros((COLS, 3 * CH), BF)
    wide[0:COLS, :] = edge
    wide[COLS + PIX : PAD, :] = edge
    column = lax.broadcasted_iota(jnp.int32, (PIX, CH), 0) & (COLS - 1)
    full = values.astype(F32)
    before = jnp.where(column == 0, 0.0, pltpu.roll(full, 1, 0))
    after = jnp.where(column == COLS - 1, 0.0, pltpu.roll(full, PIX - 1, 0))
    wide[COLS : COLS + PIX, 0:CH] = before.astype(BF)
    wide[COLS : COLS + PIX, CH : 2 * CH] = values.astype(BF)
    wide[COLS : COLS + PIX, 2 * CH : 3 * CH] = after.astype(BF)


def conv_from(wide, weight, loads=(None, None, None)):
    total = None
    for tap, load in enumerate(loads):
        if load is not None:
            load.wait()
        term = dot_nn(
            wide[tap * COLS : tap * COLS + PIX, :], weight[tap * 3 * CH : (tap + 1) * 3 * CH, :]
        )
        total = term if total is None else total + term
    return total


def back_from(wide, weight):
    total = None
    for tap in range(3):
        for side in range(3):
            at = (tap * 3 + side) * CH
            term = dot_nt(
                wide[(2 - tap) * COLS : (2 - tap) * COLS + PIX, (2 - side) * CH : (3 - side) * CH],
                weight[at : at + CH, :],
            )
            total = term if total is None else total + term
    return total


def silu_pair(pre):
    sigma = 0.5 + 0.5 * jnp.tanh(0.5 * pre)
    act = pre * sigma
    return act, sigma * (1.0 + pre * (1.0 - sigma))


def forward_kernel(pos, video_at, cot_at, w1_at, w2_at, both_at, slopes_at, keep, send, *rest):
    video, first, both, slopes, w1, w2, wide, sems = rest
    pieces = [(video_at, video)]
    for source, target in ((w1_at, w1), (w2_at, w2)):
        for tap in range(3):
            part = pl.ds(tap * 3 * CH, 3 * CH)
            pieces.append((source.at[part], target.at[part]))
    pieces.append((cot_at, both.at[:, COLS : 2 * COLS, :]))
    pieces.append((slopes.at[0], slopes_at.at[0]))
    pieces.append((slopes.at[1], slopes_at.at[1]))
    pieces.append((both, both_at))
    moves = [
        pltpu.make_async_copy(source, target, sems.at[at])
        for at, (source, target) in enumerate(pieces)
    ]
    for move in moves[0:8]:
        move.start()
    moves[0].wait()
    fill_windows(wide, video[...])
    act, slope = silu_pair(conv_from(wide, w1, moves[1:4]))
    first[...] = act.astype(BF)
    stores = [(first, video, keep), (video, first, send)]
    start_by_core(pos, sems, 11, stores)
    slopes[0] = slope.astype(BF)
    moves[8].start()
    fill_windows(wide, first[...])
    act, slope = silu_pair(conv_from(wide, w2, moves[4:7]))
    both[:, 0:COLS, :] = act.astype(BF).reshape(PIX // COLS, COLS, CH)
    moves[7].wait()
    moves[10].start()
    slopes[1] = slope.astype(BF)
    moves[9].start()
    for move in moves[8:11]:
        move.wait()
    wait_by_core(sems, 11, stores)


def ahead_sum(padded, weight):
    total = None
    for step in range(3):
        term = dot_nt(padded[step * COLS : step * COLS + PIX, :], weight[step * CH : (step + 1) * CH, :])
        total = term if total is None else total + term
    return total


def time_kernel(pos, both_at, wt1_at, wt2_at, back_at, keep, send, *rest):
    act, cot, wt1, wt2, time_act, time_grad, act_back, behind, ahead, sems = rest
    loads = [
        pltpu.make_async_copy(source, target, sems.at[at])
        for at, (source, target) in enumerate(
            [
                (both_at.at[:, COLS : 2 * COLS, :], cot),
                (wt2_at, wt2),
                (both_at.at[:, 0:COLS, :], act),
                (wt1_at, wt1),
            ]
        )
    ]
    for load in loads:
        load.start()
    edge = jnp.zeros((2 * COLS, CH), BF)
    loads[0].wait()
    ahead[0:PIX, :] = cot[...].reshape(PIX, CH)
    ahead[PIX:PAD, :] = edge
    loads[1].wait()
    back = ahead_sum(ahead, wt2)
    loads[2].wait()
    behind[0 : 2 * COLS, :] = edge
    behind[2 * COLS : PAD, :] = act[...].reshape(PIX, CH)
    loads[3].wait()
    pre = None
    for step in range(3):
        at = (2 - step) * COLS
        term = dot_nn(behind[at : at + PIX, :], wt1[step * CH : (step + 1) * CH, :])
        pre = term if pre is None else pre + term
    value, slope = silu_pair(pre)
    grad = (back * slope).astype(BF)
    time_act[...] = value.astype(BF).reshape(PIX // COLS, COLS, CH)
    time_grad[...] = grad.reshape(PIX // COLS, COLS, CH)
    stores = [
        (act, time_act, keep.at[0]),
        (time_grad, cot, keep.at[1]),
        (time_act, act, send.at[0]),
        (cot, time_grad, send.at[1]),
    ]
    start_by_core(pos, sems, 4, stores)
    ahead[0:PIX, :] = grad
    act_back[...] = ahead_sum(ahead, wt1).astype(BF)
    last = pltpu.make_async_copy(act_back, back_at, sems.at[8])
    last.start()
    wait_by_core(sems, 4, stores)
    last.wait()


def time_weights_kernel(keep, recv, out):
    for step in range(3):
        rows = PIX - step * COLS
        total = dot_tn(keep[0, 0:rows, :], keep[1, step * COLS : PIX, :])
        total = total + dot_tn(recv[0, 0:rows, :], recv[1, step * COLS : PIX, :])
        out[step * CH : (step + 1) * CH, :] = (total * SCALE).astype(BF)


def backward_kernel(pos, act_back, slopes, w2, first_grad, keep, send, wide):
    second = (act_back[...].astype(F32) * slopes[1].astype(F32)).astype(BF)
    fill_windows(wide, second)
    first = (back_from(wide, w2) * slopes[0].astype(F32)).astype(BF)
    first_grad[...] = first

    @pl.when(pos[0] == 0)
    def _():
        keep[...] = second
        send[...] = first

    @pl.when(pos[0] != 0)
    def _():
        keep[...] = first
        send[...] = second


def space_weights_kernel(keep_x, recv_x, keep_g, recv_g, time_part, out, wide, other):
    fill_windows(wide, keep_x[...])
    fill_windows(other, recv_x[...])
    for tap in range(3):
        for side in range(3):
            rows = slice(tap * COLS, tap * COLS + PIX)
            lanes = slice(side * CH, (side + 1) * CH)
            total = dot_tn(wide[rows, lanes], keep_g[...])
            total = total + dot_tn(other[rows, lanes], recv_g[...])
            at = (tap * 3 + side) * CH
            out[at : at + CH, :] = (total * SCALE).astype(BF)
    out[9 * CH : 12 * CH, :] = time_part[...]


def spread_kernel(owner, pos, half, *refs):
    spat1, spat2, time1, time2, stage, sems = refs[-6:]
    targets = [(spat2, time1), (spat1, time2)]

    def copies(at):
        space, time = targets[at]
        rows = 3 * CH
        for piece in range(3):
            part = pl.ds(piece * rows, rows)
            yield pltpu.make_async_copy(stage.at[part], space.at[part], sems.at[piece])
        yield pltpu.make_async_copy(stage.at[pl.ds(3 * rows, rows)], time, sems.at[3])

    for at in range(2):

        @pl.when((pos[0] ^ owner) == at)
        def _():
            for piece, copy in enumerate(copies(at)):
                rows = slice(piece * 3 * CH, (piece + 1) * 3 * CH)
                stage[rows, :] = half[rows, :].astype(F32)
                copy.start()
            for copy in copies(at):
                copy.wait()


def input_kernel(first_grad, w1, out, wide):
    fill_windows(wide, first_grad[...])
    out[...] = back_from(wide, w1).astype(BF)


def swap_cores(values):
    return lax.ppermute(values, "core", [(0, 1), (1, 0)])


def swap_frames(values):
    blocks = values.reshape(PIX // COLS, COLS, CH)
    return lax.all_to_all(blocks, FRAME_AXES, 0, 0, tiled=True).reshape(PIX, CH)


def scatter_sum(values, axes, count):
    parts = values.reshape(count, -1, CH)
    arrived = lax.all_to_all(parts, axes, 0, 0, tiled=True)
    return jnp.sum(arrived.astype(F32), axis=0).astype(BF)


def gather_all(values, axes, count):
    copies = jnp.broadcast_to(values[None], (count,) + values.shape)
    return lax.all_to_all(copies, axes, 0, 0, tiled=True).reshape(-1, CH)


def body(video, cotangent, w_spat1, w_spat2, w_time1, w_time2):
    pos = lax.axis_index("core").astype(jnp.int32).reshape(1)
    w1, w2, wt1, wt2 = (w.reshape(-1, CH) for w in (w_spat1, w_spat2, w_time1, w_time2))
    rows = PIX // COLS
    slab = ((PIX, CH), BF)
    pair = ((2, rows, COLS, CH), BF)
    wide, tall = pltpu.VMEM((PAD, 3 * CH), BF), pltpu.VMEM((PAD, CH), BF)
    frame, lines = pltpu.VMEM((PIX, CH), BF), pltpu.VMEM((rows, COLS, CH), BF)
    both_slopes = pltpu.VMEM((2, PIX, CH), BF)
    space, time = pltpu.VMEM((9 * CH, CH), BF), pltpu.VMEM((3 * CH, CH), BF)
    conv_flops, time_flops = 2 * PIX * 9 * CH * CH, 2 * PIX * 3 * CH * CH

    both, slopes, keep_x, send_x = call(
        forward_kernel,
        [((rows, 2 * COLS, CH), BF), ((2, PIX, CH), BF), slab, slab],
        (pos, video.reshape(PIX, CH), cotangent.reshape(rows, COLS, CH), w1, w2),
        [frame, frame, pltpu.VMEM((rows, 2 * COLS, CH), BF), both_slopes, space, space, wide, pltpu.SemaphoreType.DMA((13,))],
        2 * conv_flops,
        (1, 2, 3, 4),
        (0, 1, 2, 3),
        vmem=60,
    )
    both = lax.all_to_all(both, FRAME_AXES, 0, 0, tiled=True)
    recv_x = swap_cores(send_x)
    act_back, keep_t, send_t = call(
        time_kernel,
        [slab, pair, pair],
        (pos, both, wt1, wt2),
        [lines, lines, time, time, lines, lines, frame, tall, tall, pltpu.SemaphoreType.DMA((9,))],
        3 * time_flops,
        (1, 2, 3),
        (0, 1, 2),
        vmem=60,
    )
    act_back = swap_frames(act_back)
    recv_t = swap_cores(send_t)
    keep_t, recv_t = keep_t.reshape(2, PIX, CH), recv_t.reshape(2, PIX, CH)
    (time_part,) = call(
        time_weights_kernel, [((3 * CH, CH), BF)], (keep_t, recv_t), (), 2 * time_flops
    )
    first_grad, keep_g, send_g = call(
        backward_kernel, [slab, slab, slab], (pos, act_back, slopes, w2), [wide], conv_flops
    )
    recv_g = swap_cores(send_g)
    (part,) = call(
        space_weights_kernel,
        [((12 * CH, CH), BF)],
        (keep_x, recv_x, keep_g, recv_g, time_part),
        [wide, wide],
        2 * conv_flops,
    )

    part = scatter_sum(part, ("zl", "x", "y"), 32)
    part = jnp.sum(gather_all(part, "zh", 4).reshape(4, -1, CH).astype(F32), axis=0).astype(BF)
    part = gather_all(part, ("zl", "x", "y"), 32)
    peer = swap_cores(part)
    part, first_grad = lax.optimization_barrier((part, first_grad))
    (grad_input,) = call(input_kernel, [slab], (first_grad, w1), [wide], conv_flops)
    grads = [((9 * CH, CH), F32)] * 2 + [((3 * CH, CH), F32)] * 2
    scratch = [pltpu.VMEM((12 * CH, CH), F32), pltpu.SemaphoreType.DMA((4,))]
    outs = call(
        functools.partial(spread_kernel, 0), grads, (pos, part), scratch, 0, (), (0, 1, 2, 3)
    )
    outs = call(
        functools.partial(spread_kernel, 1),
        grads,
        (pos, peer, *outs),
        scratch,
        0,
        (2, 3, 4, 5),
        (0, 1, 2, 3),
        {2: 0, 3: 1, 4: 2, 5: 3},
    )
    return (
        grad_input.reshape(video.shape),
        outs[0].reshape(w_spat1.shape),
        outs[1].reshape(w_spat2.shape),
        outs[2].reshape(w_time1.shape),
        outs[3].reshape(w_time2.shape),
    )


def solution(mesh):
    fine = Mesh(mesh.devices.reshape(4, 2, 4, 4, 2), ("zh", "zl", "x", "y", "core"))
    frames = P(("y", "core"), FRAME_AXES, None, None, None)
    return jax.shard_map(
        body,
        mesh=fine,
        in_specs=(frames, frames, P(), P(), P(), P()),
        out_specs=(frames, P(), P(), P(), P()),
        check_vma=False,
    )
```

```python
import functools
import math

import jax
import jax.numpy as jnp
from jax import lax
from jax.experimental import pallas as pl
from jax.experimental.pallas import tpu as pltpu
from jax.sharding import Mesh
from jax.sharding import PartitionSpec as P

CH = 256
COLS = 16
PIX = 512
HALF = PIX // 2
PAD = PIX + 2 * COLS
FRAME_AXES = ("zh", "zl", "x")
SCALE = 1.0 / math.sqrt(131072)
BF = jnp.bfloat16
F32 = jnp.float32
VMEM = pl.BlockSpec(memory_space=pltpu.VMEM)
SMEM = pl.BlockSpec(memory_space=pltpu.SMEM)
HBM = pl.BlockSpec(memory_space=pltpu.HBM)


def dot_nn(left, right):
    return lax.dot_general(left, right, (((1,), (0,)), ((), ())), preferred_element_type=F32)


def dot_nt(left, right):
    return lax.dot_general(left, right, (((1,), (1,)), ((), ())), preferred_element_type=F32)


def dot_tn(left, right):
    return lax.dot_general(left, right, (((0,), (0,)), ((), ())), preferred_element_type=F32)


def call(kernel, outs, ins, scratch=(), flops=0, hbm_in=(), hbm_out=(), aliases=None, vmem=40):
    specs = [SMEM if value.dtype == jnp.int32 else VMEM for value in ins]
    for at in hbm_in:
        specs[at] = HBM
    moved = sum(value.size * value.dtype.itemsize for value in ins)
    return pl.pallas_call(
        kernel,
        out_shape=[jax.ShapeDtypeStruct(shape, kind) for shape, kind in outs],
        in_specs=specs,
        out_specs=[HBM if at in hbm_out else VMEM for at in range(len(outs))],
        scratch_shapes=list(scratch),
        input_output_aliases=aliases or {},
        cost_estimate=pl.CostEstimate(flops=flops, bytes_accessed=moved, transcendentals=0),
        compiler_params=pltpu.CompilerParams(vmem_limit_bytes=vmem * 1024 * 1024),
    )(*ins)


def start_by_core(pos, sems, first, pairs):
    for at, (even, odd, target) in enumerate(pairs):

        @pl.when(pos[0] == 0)
        def _():
            pltpu.make_async_copy(even, target, sems.at[first + at]).start()

        @pl.when(pos[0] != 0)
        def _():
            pltpu.make_async_copy(odd, target, sems.at[first + at]).start()


def wait_by_core(sems, first, pairs):
    for at, (even, _, target) in enumerate(pairs):
        pltpu.make_async_copy(even, target, sems.at[first + at]).wait()


def fill_windows(wide, values):
    edge = jnp.zeros((COLS, 3 * CH), BF)
    wide[0:COLS, :] = edge
    wide[COLS + PIX : PAD, :] = edge
    column = lax.broadcasted_iota(jnp.int32, (PIX, CH), 0) & (COLS - 1)
    full = values.astype(F32)
    before = jnp.where(column == 0, 0.0, pltpu.roll(full, 1, 0))
    after = jnp.where(column == COLS - 1, 0.0, pltpu.roll(full, PIX - 1, 0))
    wide[COLS : COLS + PIX, 0:CH] = before.astype(BF)
    wide[COLS : COLS + PIX, CH : 2 * CH] = values.astype(BF)
    wide[COLS : COLS + PIX, 2 * CH : 3 * CH] = after.astype(BF)


def conv_half(wide, weight, half):
    total = None
    for tap in range(3):
        at = tap * COLS + half * HALF
        term = dot_nn(wide[at : at + HALF, :], weight[tap * 3 * CH : (tap + 1) * 3 * CH, :])
        total = term if total is None else total + term
    return total


def back_from(wide, weight):
    total = None
    for tap in range(3):
        for side in range(3):
            at = (tap * 3 + side) * CH
            term = dot_nt(
                wide[(2 - tap) * COLS : (2 - tap) * COLS + PIX, (2 - side) * CH : (3 - side) * CH],
                weight[at : at + CH, :],
            )
            total = term if total is None else total + term
    return total


def silu_pair(pre):
    sigma = 0.5 + 0.5 * jnp.tanh(0.5 * pre)
    act = pre * sigma
    return act, sigma * (1.0 + pre * (1.0 - sigma))


def forward_kernel(pos, video_at, cot_at, w1_at, w2_at, both_at, slopes_at, keep, send, *rest):
    video, first, both, slopes, w1, w2, wide, sems = rest
    pieces = [(video_at, video)]
    for source, target in ((w1_at, w1), (w2_at, w2)):
        for tap in range(3):
            part = pl.ds(tap * 3 * CH, 3 * CH)
            pieces.append((source.at[part], target.at[part]))
    pieces.append((cot_at, both.at[:, COLS : 2 * COLS, :]))
    pieces.append((slopes.at[0], slopes_at.at[0]))
    for half in range(2):
        part = pl.ds(half * HALF, HALF)
        pieces.append((slopes.at[1, part], slopes_at.at[1, part]))
        part = pl.ds(half * (HALF // COLS), HALF // COLS)
        pieces.append((both.at[part], both_at.at[part]))
    moves = [
        pltpu.make_async_copy(source, target, sems.at[at])
        for at, (source, target) in enumerate(pieces)
    ]
    for move in moves[0:8]:
        move.start()
    moves[0].wait()
    fill_windows(wide, video[...])
    for move in moves[1:4]:
        move.wait()
    for half in range(2):
        rows = slice(half * HALF, (half + 1) * HALF)
        act, slope = silu_pair(conv_half(wide, w1, half))
        first[rows, :] = act.astype(BF)
        slopes[0, rows, :] = slope.astype(BF)
    stores = [(first, video, keep), (video, first, send)]
    start_by_core(pos, sems, 13, stores)
    moves[8].start()
    fill_windows(wide, first[...])
    for move in moves[4:8]:
        move.wait()
    for half in range(2):
        rows = slice(half * HALF, (half + 1) * HALF)
        act, slope = silu_pair(conv_half(wide, w2, half))
        lines = HALF // COLS
        both[half * lines : (half + 1) * lines, 0:COLS, :] = act.astype(BF).reshape(lines, COLS, CH)
        slopes[1, rows, :] = slope.astype(BF)
    for move in moves[9:13]:
        move.start()
    for move in moves[8:13]:
        move.wait()
    wait_by_core(sems, 13, stores)


def ahead_sum(padded, weight, half):
    total = None
    for step in range(3):
        at = step * COLS + half * HALF
        term = dot_nt(padded[at : at + HALF, :], weight[step * CH : (step + 1) * CH, :])
        total = term if total is None else total + term
    return total


def time_kernel(pos, both_at, wt1_at, wt2_at, back_at, keep, send, *rest):
    act, cot, wt1, wt2, time_act, time_grad, act_back, behind, ahead, later, sems = rest
    loads = [
        pltpu.make_async_copy(source, target, sems.at[at])
        for at, (source, target) in enumerate(
            [
                (both_at.at[:, COLS : 2 * COLS, :], cot),
                (wt2_at, wt2),
                (both_at.at[:, 0:COLS, :], act),
                (wt1_at, wt1),
            ]
        )
    ]
    for load in loads:
        load.start()
    edge = jnp.zeros((2 * COLS, CH), BF)
    loads[0].wait()
    ahead[0:PIX, :] = cot[...].reshape(PIX, CH)
    ahead[PIX:PAD, :] = edge
    loads[2].wait()
    behind[0 : 2 * COLS, :] = edge
    behind[2 * COLS : PAD, :] = act[...].reshape(PIX, CH)
    loads[1].wait()
    loads[3].wait()
    for half in range(2):
        pre = None
        for step in range(3):
            at = (2 - step) * COLS + half * HALF
            term = dot_nn(behind[at : at + HALF, :], wt1[step * CH : (step + 1) * CH, :])
            pre = term if pre is None else pre + term
        value, slope = silu_pair(pre)
        grad = (ahead_sum(ahead, wt2, half) * slope).astype(BF)
        lines = slice(half * (HALF // COLS), (half + 1) * (HALF // COLS))
        time_act[lines] = value.astype(BF).reshape(HALF // COLS, COLS, CH)
        time_grad[lines] = grad.reshape(HALF // COLS, COLS, CH)
        later[half * HALF : (half + 1) * HALF, :] = grad
    later[PIX:PAD, :] = edge
    stores = [
        (act, time_act, keep.at[0]),
        (time_grad, cot, keep.at[1]),
        (time_act, act, send.at[0]),
        (cot, time_grad, send.at[1]),
    ]
    start_by_core(pos, sems, 4, stores)
    tails = []
    for half in range(2):
        rows = pl.ds(half * HALF, HALF)
        act_back[rows, :] = ahead_sum(later, wt1, half).astype(BF)
        tails.append(pltpu.make_async_copy(act_back.at[rows], back_at.at[rows], sems.at[8 + half]))
        tails[half].start()
    wait_by_core(sems, 4, stores)
    for tail in tails:
        tail.wait()


def time_weights_kernel(keep, recv, out):
    for step in range(3):
        rows = PIX - step * COLS
        total = dot_tn(keep[0, 0:rows, :], keep[1, step * COLS : PIX, :])
        total = total + dot_tn(recv[0, 0:rows, :], recv[1, step * COLS : PIX, :])
        out[step * CH : (step + 1) * CH, :] = (total * SCALE).astype(BF)


def backward_kernel(pos, act_back, slopes, w2, first_grad, keep, send, wide):
    second = (act_back[...].astype(F32) * slopes[1].astype(F32)).astype(BF)
    fill_windows(wide, second)
    first = (back_from(wide, w2) * slopes[0].astype(F32)).astype(BF)
    first_grad[...] = first

    @pl.when(pos[0] == 0)
    def _():
        keep[...] = second
        send[...] = first

    @pl.when(pos[0] != 0)
    def _():
        keep[...] = first
        send[...] = second


def own_weights_kernel(keep_x, keep_g, out, wide):
    fill_windows(wide, keep_x[...])
    for tap in range(3):
        for side in range(3):
            rows = slice(tap * COLS, tap * COLS + PIX)
            lanes = slice(side * CH, (side + 1) * CH)
            at = (tap * 3 + side) * CH
            out[at : at + CH, :] = dot_tn(wide[rows, lanes], keep_g[...])


def space_weights_kernel(partial, recv_x, recv_g, time_part, out, wide):
    fill_windows(wide, recv_x[...])
    for tap in range(3):
        for side in range(3):
            rows = slice(tap * COLS, tap * COLS + PIX)
            lanes = slice(side * CH, (side + 1) * CH)
            at = (tap * 3 + side) * CH
            total = partial[at : at + CH, :] + dot_tn(wide[rows, lanes], recv_g[...])
            out[at : at + CH, :] = (total * SCALE).astype(BF)
    out[9 * CH : 12 * CH, :] = time_part[...]


def spread_kernel(owner, pos, half, *refs):
    spat1, spat2, time1, time2, stage, sems = refs[-6:]
    targets = [(spat2, time1), (spat1, time2)]

    def copies(at):
        space, time = targets[at]
        rows = 3 * CH
        for piece in range(3):
            part = pl.ds(piece * rows, rows)
            yield pltpu.make_async_copy(stage.at[part], space.at[part], sems.at[piece])
        yield pltpu.make_async_copy(stage.at[pl.ds(3 * rows, rows)], time, sems.at[3])

    for at in range(2):

        @pl.when((pos[0] ^ owner) == at)
        def _():
            for piece, copy in enumerate(copies(at)):
                rows = slice(piece * 3 * CH, (piece + 1) * 3 * CH)
                stage[rows, :] = half[rows, :].astype(F32)
                copy.start()
            for copy in copies(at):
                copy.wait()


def input_kernel(first_grad, w1, out, wide):
    fill_windows(wide, first_grad[...])
    out[...] = back_from(wide, w1).astype(BF)


def swap_cores(values):
    return lax.ppermute(values, "core", [(0, 1), (1, 0)])


def swap_frames(values):
    blocks = values.reshape(PIX // COLS, COLS, CH)
    return lax.all_to_all(blocks, FRAME_AXES, 0, 0, tiled=True).reshape(PIX, CH)


def scatter_sum(values, axes, count):
    parts = values.reshape(count, -1, CH)
    arrived = lax.all_to_all(parts, axes, 0, 0, tiled=True)
    return jnp.sum(arrived.astype(F32), axis=0).astype(BF)


def gather_all(values, axes, count):
    copies = jnp.broadcast_to(values[None], (count,) + values.shape)
    return lax.all_to_all(copies, axes, 0, 0, tiled=True).reshape(-1, CH)


def body(video, cotangent, w_spat1, w_spat2, w_time1, w_time2):
    pos = lax.axis_index("core").astype(jnp.int32).reshape(1)
    w1, w2, wt1, wt2 = (w.reshape(-1, CH) for w in (w_spat1, w_spat2, w_time1, w_time2))
    rows = PIX // COLS
    slab = ((PIX, CH), BF)
    pair = ((2, rows, COLS, CH), BF)
    wide, tall = pltpu.VMEM((PAD, 3 * CH), BF), pltpu.VMEM((PAD, CH), BF)
    frame, lines = pltpu.VMEM((PIX, CH), BF), pltpu.VMEM((rows, COLS, CH), BF)
    both_slopes = pltpu.VMEM((2, PIX, CH), BF)
    space, time = pltpu.VMEM((9 * CH, CH), BF), pltpu.VMEM((3 * CH, CH), BF)
    conv_flops, time_flops = 2 * PIX * 9 * CH * CH, 2 * PIX * 3 * CH * CH

    both, slopes, keep_x, send_x = call(
        forward_kernel,
        [((rows, 2 * COLS, CH), BF), ((2, PIX, CH), BF), slab, slab],
        (pos, video.reshape(PIX, CH), cotangent.reshape(rows, COLS, CH), w1, w2),
        [frame, frame, pltpu.VMEM((rows, 2 * COLS, CH), BF), both_slopes, space, space, wide, pltpu.SemaphoreType.DMA((15,))],
        2 * conv_flops,
        (1, 2, 3, 4),
        (0, 1, 2, 3),
        vmem=60,
    )
    both = lax.all_to_all(both, FRAME_AXES, 0, 0, tiled=True)
    recv_x = swap_cores(send_x)
    act_back, keep_t, send_t = call(
        time_kernel,
        [slab, pair, pair],
        (pos, both, wt1, wt2),
        [lines, lines, time, time, lines, lines, frame, tall, tall, tall, pltpu.SemaphoreType.DMA((10,))],
        3 * time_flops,
        (1, 2, 3),
        (0, 1, 2),
        vmem=60,
    )
    act_back = swap_frames(act_back)
    recv_t = swap_cores(send_t)
    keep_t, recv_t = keep_t.reshape(2, PIX, CH), recv_t.reshape(2, PIX, CH)
    (time_part,) = call(
        time_weights_kernel, [((3 * CH, CH), BF)], (keep_t, recv_t), (), 2 * time_flops
    )
    act_back, time_part = lax.optimization_barrier((act_back, time_part))
    first_grad, keep_g, send_g = call(
        backward_kernel, [slab, slab, slab], (pos, act_back, slopes, w2), [wide], conv_flops
    )
    recv_g = swap_cores(send_g)
    (partial,) = call(
        own_weights_kernel, [((9 * CH, CH), F32)], (keep_x, keep_g), [wide], conv_flops
    )
    (part,) = call(
        space_weights_kernel,
        [((12 * CH, CH), BF)],
        (partial, recv_x, recv_g, time_part),
        [wide],
        conv_flops,
    )

    part = scatter_sum(part, ("zl", "x", "y"), 32)
    part = jnp.sum(gather_all(part, "zh", 4).reshape(4, -1, CH).astype(F32), axis=0).astype(BF)
    part = gather_all(part, ("zl", "x", "y"), 32)
    peer = swap_cores(part)
    part, first_grad = lax.optimization_barrier((part, first_grad))
    (grad_input,) = call(input_kernel, [slab], (first_grad, w1), [wide], conv_flops)
    grads = [((9 * CH, CH), F32)] * 2 + [((3 * CH, CH), F32)] * 2
    scratch = [pltpu.VMEM((12 * CH, CH), F32), pltpu.SemaphoreType.DMA((4,))]
    outs = call(
        functools.partial(spread_kernel, 0), grads, (pos, part), scratch, 0, (), (0, 1, 2, 3)
    )
    outs = call(
        functools.partial(spread_kernel, 1),
        grads,
        (pos, peer, *outs),
        scratch,
        0,
        (2, 3, 4, 5),
        (0, 1, 2, 3),
        {2: 0, 3: 1, 4: 2, 5: 3},
    )
    return (
        grad_input.reshape(video.shape),
        outs[0].reshape(w_spat1.shape),
        outs[1].reshape(w_spat2.shape),
        outs[2].reshape(w_time1.shape),
        outs[3].reshape(w_time2.shape),
    )


def solution(mesh):
    fine = Mesh(mesh.devices.reshape(4, 2, 4, 4, 2), ("zh", "zl", "x", "y", "core"))
    frames = P(("y", "core"), FRAME_AXES, None, None, None)
    return jax.shard_map(
        body,
        mesh=fine,
        in_specs=(frames, frames, P(), P(), P(), P()),
        out_specs=(frames, P(), P(), P(), P()),
        check_vma=False,
    )
```

```python
import functools
import math

import jax
import jax.numpy as jnp
from jax import lax
from jax.experimental import pallas as pl
from jax.experimental.pallas import tpu as pltpu
from jax.sharding import Mesh
from jax.sharding import PartitionSpec as P

CH = 256
COLS = 16
PIX = 512
HALF = PIX // 2
PAD = PIX + 2 * COLS
FRAME_AXES = ("zh", "zl", "x")
SCALE = 1.0 / math.sqrt(131072)
BF = jnp.bfloat16
F32 = jnp.float32
VMEM = pl.BlockSpec(memory_space=pltpu.VMEM)
SMEM = pl.BlockSpec(memory_space=pltpu.SMEM)
HBM = pl.BlockSpec(memory_space=pltpu.HBM)


def dot_nn(left, right):
    return lax.dot_general(left, right, (((1,), (0,)), ((), ())), preferred_element_type=F32)


def dot_nt(left, right):
    return lax.dot_general(left, right, (((1,), (1,)), ((), ())), preferred_element_type=F32)


def dot_tn(left, right):
    return lax.dot_general(left, right, (((0,), (0,)), ((), ())), preferred_element_type=F32)


def call(kernel, outs, ins, scratch=(), flops=0, hbm_in=(), hbm_out=(), aliases=None, vmem=40):
    specs = [SMEM if value.dtype == jnp.int32 else VMEM for value in ins]
    for at in hbm_in:
        specs[at] = HBM
    moved = sum(value.size * value.dtype.itemsize for value in ins)
    return pl.pallas_call(
        kernel,
        out_shape=[jax.ShapeDtypeStruct(shape, kind) for shape, kind in outs],
        in_specs=specs,
        out_specs=[HBM if at in hbm_out else VMEM for at in range(len(outs))],
        scratch_shapes=list(scratch),
        input_output_aliases=aliases or {},
        cost_estimate=pl.CostEstimate(flops=flops, bytes_accessed=moved, transcendentals=0),
        compiler_params=pltpu.CompilerParams(vmem_limit_bytes=vmem * 1024 * 1024),
    )(*ins)


def start_by_core(pos, sems, first, pairs):
    for at, (even, odd, target) in enumerate(pairs):

        @pl.when(pos[0] == 0)
        def _():
            pltpu.make_async_copy(even, target, sems.at[first + at]).start()

        @pl.when(pos[0] != 0)
        def _():
            pltpu.make_async_copy(odd, target, sems.at[first + at]).start()


def wait_by_core(sems, first, pairs):
    for at, (even, _, target) in enumerate(pairs):
        pltpu.make_async_copy(even, target, sems.at[first + at]).wait()


def fill_windows(wide, values):
    edge = jnp.zeros((COLS, 3 * CH), BF)
    wide[0:COLS, :] = edge
    wide[COLS + PIX : PAD, :] = edge
    column = lax.broadcasted_iota(jnp.int32, (PIX, CH), 0) & (COLS - 1)
    full = values.astype(F32)
    before = jnp.where(column == 0, 0.0, pltpu.roll(full, 1, 0))
    after = jnp.where(column == COLS - 1, 0.0, pltpu.roll(full, PIX - 1, 0))
    wide[COLS : COLS + PIX, 0:CH] = before.astype(BF)
    wide[COLS : COLS + PIX, CH : 2 * CH] = values.astype(BF)
    wide[COLS : COLS + PIX, 2 * CH : 3 * CH] = after.astype(BF)


def conv_half(wide, weight, half):
    total = None
    for tap in range(3):
        at = tap * COLS + half * HALF
        term = dot_nn(wide[at : at + HALF, :], weight[tap * 3 * CH : (tap + 1) * 3 * CH, :])
        total = term if total is None else total + term
    return total


def back_from(wide, weight):
    total = None
    for tap in range(3):
        for side in range(3):
            at = (tap * 3 + side) * CH
            term = dot_nt(
                wide[(2 - tap) * COLS : (2 - tap) * COLS + PIX, (2 - side) * CH : (3 - side) * CH],
                weight[at : at + CH, :],
            )
            total = term if total is None else total + term
    return total


def silu_pair(pre):
    sigma = 0.5 + 0.5 * jnp.tanh(0.5 * pre)
    act = pre * sigma
    return act, sigma * (1.0 + pre * (1.0 - sigma))


def forward_kernel(pos, video_at, cot_at, w1_at, w2_at, both_at, slopes_at, keep, send, *rest):
    video, first, both, slopes, w1, w2, wide, sems = rest
    pieces = [(video_at, video)]
    for source, target in ((w1_at, w1), (w2_at, w2)):
        for tap in range(3):
            part = pl.ds(tap * 3 * CH, 3 * CH)
            pieces.append((source.at[part], target.at[part]))
    pieces.append((cot_at, both.at[:, COLS : 2 * COLS, :]))
    pieces.append((slopes.at[0], slopes_at.at[0]))
    for half in range(2):
        part = pl.ds(half * HALF, HALF)
        pieces.append((slopes.at[1, part], slopes_at.at[1, part]))
        part = pl.ds(half * (HALF // COLS), HALF // COLS)
        pieces.append((both.at[part], both_at.at[part]))
    moves = [
        pltpu.make_async_copy(source, target, sems.at[at])
        for at, (source, target) in enumerate(pieces)
    ]
    for move in moves[0:8]:
        move.start()
    moves[0].wait()
    fill_windows(wide, video[...])
    for move in moves[1:4]:
        move.wait()
    for half in range(2):
        rows = slice(half * HALF, (half + 1) * HALF)
        act, slope = silu_pair(conv_half(wide, w1, half))
        first[rows, :] = act.astype(BF)
        slopes[0, rows, :] = slope.astype(BF)
    stores = [(first, video, keep), (video, first, send)]
    start_by_core(pos, sems, 13, stores)
    moves[8].start()
    fill_windows(wide, first[...])
    for move in moves[4:8]:
        move.wait()
    for half in range(2):
        rows = slice(half * HALF, (half + 1) * HALF)
        act, slope = silu_pair(conv_half(wide, w2, half))
        lines = HALF // COLS
        both[half * lines : (half + 1) * lines, 0:COLS, :] = act.astype(BF).reshape(lines, COLS, CH)
        slopes[1, rows, :] = slope.astype(BF)
    for move in moves[9:13]:
        move.start()
    for move in moves[8:13]:
        move.wait()
    wait_by_core(sems, 13, stores)


def ahead_sum(padded, weight, half):
    total = None
    for step in range(3):
        at = step * COLS + half * HALF
        term = dot_nt(padded[at : at + HALF, :], weight[step * CH : (step + 1) * CH, :])
        total = term if total is None else total + term
    return total


def time_kernel(pos, both_at, wt1_at, wt2_at, back_at, keep, send, *rest):
    act, cot, wt1, wt2, time_act, time_grad, act_back, behind, ahead, later, sems = rest
    loads = [
        pltpu.make_async_copy(source, target, sems.at[at])
        for at, (source, target) in enumerate(
            [
                (both_at.at[:, COLS : 2 * COLS, :], cot),
                (wt2_at, wt2),
                (both_at.at[:, 0:COLS, :], act),
                (wt1_at, wt1),
            ]
        )
    ]
    for load in loads:
        load.start()
    edge = jnp.zeros((2 * COLS, CH), BF)
    loads[0].wait()
    ahead[0:PIX, :] = cot[...].reshape(PIX, CH)
    ahead[PIX:PAD, :] = edge
    loads[2].wait()
    behind[0 : 2 * COLS, :] = edge
    behind[2 * COLS : PAD, :] = act[...].reshape(PIX, CH)
    loads[1].wait()
    loads[3].wait()
    for half in range(2):
        pre = None
        for step in range(3):
            at = (2 - step) * COLS + half * HALF
            term = dot_nn(behind[at : at + HALF, :], wt1[step * CH : (step + 1) * CH, :])
            pre = term if pre is None else pre + term
        value, slope = silu_pair(pre)
        grad = (ahead_sum(ahead, wt2, half) * slope).astype(BF)
        lines = slice(half * (HALF // COLS), (half + 1) * (HALF // COLS))
        time_act[lines] = value.astype(BF).reshape(HALF // COLS, COLS, CH)
        time_grad[lines] = grad.reshape(HALF // COLS, COLS, CH)
        later[half * HALF : (half + 1) * HALF, :] = grad
    later[PIX:PAD, :] = edge
    stores = [
        (act, time_act, keep.at[0]),
        (time_grad, cot, keep.at[1]),
        (time_act, act, send.at[0]),
        (cot, time_grad, send.at[1]),
    ]
    start_by_core(pos, sems, 4, stores)
    tails = []
    for half in range(2):
        rows = pl.ds(half * HALF, HALF)
        act_back[rows, :] = ahead_sum(later, wt1, half).astype(BF)
        tails.append(pltpu.make_async_copy(act_back.at[rows], back_at.at[rows], sems.at[8 + half]))
        tails[half].start()
    wait_by_core(sems, 4, stores)
    for tail in tails:
        tail.wait()


def time_weights_kernel(keep, recv, out):
    for step in range(3):
        rows = PIX - step * COLS
        total = dot_tn(keep[0, 0:rows, :], keep[1, step * COLS : PIX, :])
        total = total + dot_tn(recv[0, 0:rows, :], recv[1, step * COLS : PIX, :])
        out[step * CH : (step + 1) * CH, :] = (total * SCALE).astype(BF)


def backward_kernel(pos, act_back, slopes, w2, first_grad, keep, send, wide):
    second = (act_back[...].astype(F32) * slopes[1].astype(F32)).astype(BF)
    fill_windows(wide, second)
    first = (back_from(wide, w2) * slopes[0].astype(F32)).astype(BF)
    first_grad[...] = first

    @pl.when(pos[0] == 0)
    def _():
        keep[...] = second
        send[...] = first

    @pl.when(pos[0] != 0)
    def _():
        keep[...] = first
        send[...] = second


def own_weights_kernel(keep_x, keep_g, out, wide):
    fill_windows(wide, keep_x[...])
    for tap in range(3):
        for side in range(3):
            rows = slice(tap * COLS, tap * COLS + PIX)
            lanes = slice(side * CH, (side + 1) * CH)
            at = (tap * 3 + side) * CH
            out[at : at + CH, :] = dot_tn(wide[rows, lanes], keep_g[...])


def space_weights_kernel(partial, recv_x, recv_g, time_part, out, wide):
    fill_windows(wide, recv_x[...])
    for tap in range(3):
        for side in range(3):
            rows = slice(tap * COLS, tap * COLS + PIX)
            lanes = slice(side * CH, (side + 1) * CH)
            at = (tap * 3 + side) * CH
            total = partial[at : at + CH, :] + dot_tn(wide[rows, lanes], recv_g[...])
            out[at : at + CH, :] = (total * SCALE).astype(BF)
    out[9 * CH : 12 * CH, :] = time_part[...]


def spread_kernel(owner, pos, half, *refs):
    spat1, spat2, time1, time2, stage, sems = refs[-6:]
    targets = [(spat2, time1), (spat1, time2)]

    def copies(at):
        space, time = targets[at]
        rows = 3 * CH
        for piece in range(3):
            part = pl.ds(piece * rows, rows)
            yield pltpu.make_async_copy(stage.at[part], space.at[part], sems.at[piece])
        yield pltpu.make_async_copy(stage.at[pl.ds(3 * rows, rows)], time, sems.at[3])

    for at in range(2):

        @pl.when((pos[0] ^ owner) == at)
        def _():
            for piece, copy in enumerate(copies(at)):
                rows = slice(piece * 3 * CH, (piece + 1) * 3 * CH)
                stage[rows, :] = half[rows, :].astype(F32)
                copy.start()
            for copy in copies(at):
                copy.wait()


def input_kernel(first_grad, w1, out, wide):
    fill_windows(wide, first_grad[...])
    out[...] = back_from(wide, w1).astype(BF)


def swap_cores(values):
    return lax.ppermute(values, "core", [(0, 1), (1, 0)])


def swap_frames(values):
    blocks = values.reshape(PIX // COLS, COLS, CH)
    return lax.all_to_all(blocks, FRAME_AXES, 0, 0, tiled=True).reshape(PIX, CH)


def scatter_sum(values, axes, count):
    parts = values.reshape(count, -1, CH)
    arrived = lax.all_to_all(parts, axes, 0, 0, tiled=True)
    return jnp.sum(arrived.astype(F32), axis=0).astype(BF)


def gather_all(values, axes, count):
    copies = jnp.broadcast_to(values[None], (count,) + values.shape)
    return lax.all_to_all(copies, axes, 0, 0, tiled=True).reshape(-1, CH)


def body(video, cotangent, w_spat1, w_spat2, w_time1, w_time2):
    pos = lax.axis_index("core").astype(jnp.int32).reshape(1)
    w1, w2, wt1, wt2 = (w.reshape(-1, CH) for w in (w_spat1, w_spat2, w_time1, w_time2))
    rows = PIX // COLS
    slab = ((PIX, CH), BF)
    pair = ((2, rows, COLS, CH), BF)
    wide, tall = pltpu.VMEM((PAD, 3 * CH), BF), pltpu.VMEM((PAD, CH), BF)
    frame, lines = pltpu.VMEM((PIX, CH), BF), pltpu.VMEM((rows, COLS, CH), BF)
    both_slopes = pltpu.VMEM((2, PIX, CH), BF)
    space, time = pltpu.VMEM((9 * CH, CH), BF), pltpu.VMEM((3 * CH, CH), BF)
    conv_flops, time_flops = 2 * PIX * 9 * CH * CH, 2 * PIX * 3 * CH * CH

    both, slopes, keep_x, send_x = call(
        forward_kernel,
        [((rows, 2 * COLS, CH), BF), ((2, PIX, CH), BF), slab, slab],
        (pos, video.reshape(PIX, CH), cotangent.reshape(rows, COLS, CH), w1, w2),
        [frame, frame, pltpu.VMEM((rows, 2 * COLS, CH), BF), both_slopes, space, space, wide, pltpu.SemaphoreType.DMA((15,))],
        2 * conv_flops,
        (1, 2, 3, 4),
        (0, 1, 2, 3),
        vmem=60,
    )
    both = lax.all_to_all(both, FRAME_AXES, 0, 0, tiled=True)
    recv_x = swap_cores(send_x)
    act_back, keep_t, send_t = call(
        time_kernel,
        [slab, pair, pair],
        (pos, both, wt1, wt2),
        [lines, lines, time, time, lines, lines, frame, tall, tall, tall, pltpu.SemaphoreType.DMA((10,))],
        3 * time_flops,
        (1, 2, 3),
        (0, 1, 2),
        vmem=60,
    )
    act_back = swap_frames(act_back)
    recv_t = swap_cores(send_t)
    keep_t, recv_t = keep_t.reshape(2, PIX, CH), recv_t.reshape(2, PIX, CH)
    (time_part,) = call(
        time_weights_kernel, [((3 * CH, CH), BF)], (keep_t, recv_t), (), 2 * time_flops
    )
    first_grad, keep_g, send_g = call(
        backward_kernel, [slab, slab, slab], (pos, act_back, slopes, w2), [wide], conv_flops
    )
    recv_g = swap_cores(send_g)
    (partial,) = call(
        own_weights_kernel, [((9 * CH, CH), F32)], (keep_x, keep_g), [wide], conv_flops
    )
    (part,) = call(
        space_weights_kernel,
        [((12 * CH, CH), BF)],
        (partial, recv_x, recv_g, time_part),
        [wide],
        conv_flops,
    )

    part = scatter_sum(part, ("zl", "x", "y"), 32)
    part = jnp.sum(gather_all(part, "zh", 4).reshape(4, -1, CH).astype(F32), axis=0).astype(BF)
    part = gather_all(part, ("zl", "x", "y"), 32)
    peer = swap_cores(part)
    part, first_grad = lax.optimization_barrier((part, first_grad))
    (grad_input,) = call(input_kernel, [slab], (first_grad, w1), [wide], conv_flops)
    grads = [((9 * CH, CH), F32)] * 2 + [((3 * CH, CH), F32)] * 2
    scratch = [pltpu.VMEM((12 * CH, CH), F32), pltpu.SemaphoreType.DMA((4,))]
    outs = call(
        functools.partial(spread_kernel, 0), grads, (pos, part), scratch, 0, (), (0, 1, 2, 3)
    )
    outs = call(
        functools.partial(spread_kernel, 1),
        grads,
        (pos, peer, *outs),
        scratch,
        0,
        (2, 3, 4, 5),
        (0, 1, 2, 3),
        {2: 0, 3: 1, 4: 2, 5: 3},
    )
    return (
        grad_input.reshape(video.shape),
        outs[0].reshape(w_spat1.shape),
        outs[1].reshape(w_spat2.shape),
        outs[2].reshape(w_time1.shape),
        outs[3].reshape(w_time2.shape),
    )


def solution(mesh):
    fine = Mesh(mesh.devices.reshape(4, 2, 4, 4, 2), ("zh", "zl", "x", "y", "core"))
    frames = P(("y", "core"), FRAME_AXES, None, None, None)
    return jax.shard_map(
        body,
        mesh=fine,
        in_specs=(frames, frames, P(), P(), P(), P()),
        out_specs=(frames, P(), P(), P(), P()),
        check_vma=False,
    )
```

```python
import functools
import math

import jax
import jax.numpy as jnp
from jax import lax
from jax.experimental import pallas as pl
from jax.experimental.pallas import tpu as pltpu
from jax.sharding import Mesh
from jax.sharding import PartitionSpec as P

CH = 256
COLS = 16
PIX = 512
HALF = PIX // 2
PAD = PIX + 2 * COLS
FRAME_AXES = ("zh", "zl", "x")
SCALE = 1.0 / math.sqrt(131072)
BF = jnp.bfloat16
F32 = jnp.float32
VMEM = pl.BlockSpec(memory_space=pltpu.VMEM)
SMEM = pl.BlockSpec(memory_space=pltpu.SMEM)
HBM = pl.BlockSpec(memory_space=pltpu.HBM)


def dot_nn(left, right):
    return lax.dot_general(left, right, (((1,), (0,)), ((), ())), preferred_element_type=F32)


def dot_nt(left, right):
    return lax.dot_general(left, right, (((1,), (1,)), ((), ())), preferred_element_type=F32)


def dot_tn(left, right):
    return lax.dot_general(left, right, (((0,), (0,)), ((), ())), preferred_element_type=F32)


def call(kernel, outs, ins, scratch=(), flops=0, hbm_in=(), hbm_out=(), aliases=None, vmem=40):
    specs = [SMEM if value.dtype == jnp.int32 else VMEM for value in ins]
    for at in hbm_in:
        specs[at] = HBM
    moved = sum(value.size * value.dtype.itemsize for value in ins)
    return pl.pallas_call(
        kernel,
        out_shape=[jax.ShapeDtypeStruct(shape, kind) for shape, kind in outs],
        in_specs=specs,
        out_specs=[HBM if at in hbm_out else VMEM for at in range(len(outs))],
        scratch_shapes=list(scratch),
        input_output_aliases=aliases or {},
        cost_estimate=pl.CostEstimate(flops=flops, bytes_accessed=moved, transcendentals=0),
        compiler_params=pltpu.CompilerParams(vmem_limit_bytes=vmem * 1024 * 1024),
    )(*ins)


def start_by_core(pos, sems, first, pairs):
    for at, (even, odd, target) in enumerate(pairs):

        @pl.when(pos[0] == 0)
        def _():
            pltpu.make_async_copy(even, target, sems.at[first + at]).start()

        @pl.when(pos[0] != 0)
        def _():
            pltpu.make_async_copy(odd, target, sems.at[first + at]).start()


def wait_by_core(sems, first, pairs):
    for at, (even, _, target) in enumerate(pairs):
        pltpu.make_async_copy(even, target, sems.at[first + at]).wait()


def fill_windows(wide, values):
    edge = jnp.zeros((COLS, 3 * CH), BF)
    wide[0:COLS, :] = edge
    wide[COLS + PIX : PAD, :] = edge
    column = lax.broadcasted_iota(jnp.int32, (PIX, CH), 0) & (COLS - 1)
    full = values.astype(F32)
    before = jnp.where(column == 0, 0.0, pltpu.roll(full, 1, 0))
    after = jnp.where(column == COLS - 1, 0.0, pltpu.roll(full, PIX - 1, 0))
    wide[COLS : COLS + PIX, 0:CH] = before.astype(BF)
    wide[COLS : COLS + PIX, CH : 2 * CH] = values.astype(BF)
    wide[COLS : COLS + PIX, 2 * CH : 3 * CH] = after.astype(BF)


def conv_half(wide, weight, half):
    total = None
    for tap in range(3):
        at = tap * COLS + half * HALF
        term = dot_nn(wide[at : at + HALF, :], weight[tap * 3 * CH : (tap + 1) * 3 * CH, :])
        total = term if total is None else total + term
    return total


def back_from(wide, weight):
    total = None
    for tap in range(3):
        for side in range(3):
            at = (tap * 3 + side) * CH
            term = dot_nt(
                wide[(2 - tap) * COLS : (2 - tap) * COLS + PIX, (2 - side) * CH : (3 - side) * CH],
                weight[at : at + CH, :],
            )
            total = term if total is None else total + term
    return total


def silu_pair(pre):
    sigma = 0.5 + 0.5 * jnp.tanh(0.5 * pre)
    act = pre * sigma
    return act, sigma * (1.0 + pre * (1.0 - sigma))


def forward_kernel(pos, video_at, cot_at, w1_at, w2_at, both_at, slopes_at, keep, send, *rest):
    video, first, both, slopes, w1, w2, wide, sems = rest
    pieces = [(video_at, video)]
    for source, target in ((w1_at, w1), (w2_at, w2)):
        for tap in range(3):
            part = pl.ds(tap * 3 * CH, 3 * CH)
            pieces.append((source.at[part], target.at[part]))
    pieces.append((cot_at, both.at[:, COLS : 2 * COLS, :]))
    pieces.append((slopes.at[0], slopes_at.at[0]))
    for half in range(2):
        part = pl.ds(half * HALF, HALF)
        pieces.append((slopes.at[1, part], slopes_at.at[1, part]))
        part = pl.ds(half * (HALF // COLS), HALF // COLS)
        pieces.append((both.at[part], both_at.at[part]))
    moves = [
        pltpu.make_async_copy(source, target, sems.at[at])
        for at, (source, target) in enumerate(pieces)
    ]
    for move in moves[0:8]:
        move.start()
    moves[0].wait()
    fill_windows(wide, video[...])
    for move in moves[1:4]:
        move.wait()
    for half in range(2):
        rows = slice(half * HALF, (half + 1) * HALF)
        act, slope = silu_pair(conv_half(wide, w1, half))
        first[rows, :] = act.astype(BF)
        slopes[0, rows, :] = slope.astype(BF)
    stores = [(first, video, keep), (video, first, send)]
    start_by_core(pos, sems, 13, stores)
    moves[8].start()
    fill_windows(wide, first[...])
    for move in moves[4:8]:
        move.wait()
    for half in range(2):
        rows = slice(half * HALF, (half + 1) * HALF)
        act, slope = silu_pair(conv_half(wide, w2, half))
        lines = HALF // COLS
        both[half * lines : (half + 1) * lines, 0:COLS, :] = act.astype(BF).reshape(lines, COLS, CH)
        slopes[1, rows, :] = slope.astype(BF)
    for move in moves[9:13]:
        move.start()
    for move in moves[8:13]:
        move.wait()
    wait_by_core(sems, 13, stores)


def ahead_sum(padded, weight, half):
    total = None
    for step in range(3):
        at = step * COLS + half * HALF
        term = dot_nt(padded[at : at + HALF, :], weight[step * CH : (step + 1) * CH, :])
        total = term if total is None else total + term
    return total


def time_kernel(pos, both_at, wt1_at, wt2_at, back_at, keep, send, *rest):
    act, cot, wt1, wt2, time_act, time_grad, act_back, behind, ahead, later, sems = rest
    loads = [
        pltpu.make_async_copy(source, target, sems.at[at])
        for at, (source, target) in enumerate(
            [
                (both_at.at[:, COLS : 2 * COLS, :], cot),
                (wt2_at, wt2),
                (both_at.at[:, 0:COLS, :], act),
                (wt1_at, wt1),
            ]
        )
    ]
    for load in loads:
        load.start()
    edge = jnp.zeros((2 * COLS, CH), BF)
    loads[0].wait()
    ahead[0:PIX, :] = cot[...].reshape(PIX, CH)
    ahead[PIX:PAD, :] = edge
    loads[2].wait()
    behind[0 : 2 * COLS, :] = edge
    behind[2 * COLS : PAD, :] = act[...].reshape(PIX, CH)
    loads[1].wait()
    loads[3].wait()
    for half in range(2):
        pre = None
        for step in range(3):
            at = (2 - step) * COLS + half * HALF
            term = dot_nn(behind[at : at + HALF, :], wt1[step * CH : (step + 1) * CH, :])
            pre = term if pre is None else pre + term
        value, slope = silu_pair(pre)
        grad = (ahead_sum(ahead, wt2, half) * slope).astype(BF)
        lines = slice(half * (HALF // COLS), (half + 1) * (HALF // COLS))
        time_act[lines] = value.astype(BF).reshape(HALF // COLS, COLS, CH)
        time_grad[lines] = grad.reshape(HALF // COLS, COLS, CH)
        later[half * HALF : (half + 1) * HALF, :] = grad
    later[PIX:PAD, :] = edge
    stores = [
        (act, time_act, keep.at[0]),
        (time_grad, cot, keep.at[1]),
        (time_act, act, send.at[0]),
        (cot, time_grad, send.at[1]),
    ]
    start_by_core(pos, sems, 4, stores)
    tails = []
    for half in range(2):
        rows = pl.ds(half * HALF, HALF)
        act_back[rows, :] = ahead_sum(later, wt1, half).astype(BF)
        tails.append(pltpu.make_async_copy(act_back.at[rows], back_at.at[rows], sems.at[8 + half]))
        tails[half].start()
    wait_by_core(sems, 4, stores)
    for tail in tails:
        tail.wait()


def time_weights_kernel(keep, recv, out):
    for step in range(3):
        rows = PIX - step * COLS
        total = dot_tn(keep[0, 0:rows, :], keep[1, step * COLS : PIX, :])
        total = total + dot_tn(recv[0, 0:rows, :], recv[1, step * COLS : PIX, :])
        out[step * CH : (step + 1) * CH, :] = (total * SCALE).astype(BF)


def backward_kernel(pos, act_back, slopes, w2, first_grad, keep, send, wide):
    second = (act_back[...].astype(F32) * slopes[1].astype(F32)).astype(BF)
    fill_windows(wide, second)
    first = (back_from(wide, w2) * slopes[0].astype(F32)).astype(BF)
    first_grad[...] = first

    @pl.when(pos[0] == 0)
    def _():
        keep[...] = second
        send[...] = first

    @pl.when(pos[0] != 0)
    def _():
        keep[...] = first
        send[...] = second


def own_weights_kernel(keep_x, keep_g, out, wide):
    fill_windows(wide, keep_x[...])
    for tap in range(3):
        for side in range(3):
            rows = slice(tap * COLS, tap * COLS + PIX)
            lanes = slice(side * CH, (side + 1) * CH)
            at = (tap * 3 + side) * CH
            out[at : at + CH, :] = dot_tn(wide[rows, lanes], keep_g[...])


def space_weights_kernel(partial, recv_x, recv_g, time_part, out, wide):
    fill_windows(wide, recv_x[...])
    for tap in range(3):
        for side in range(3):
            rows = slice(tap * COLS, tap * COLS + PIX)
            lanes = slice(side * CH, (side + 1) * CH)
            at = (tap * 3 + side) * CH
            total = partial[at : at + CH, :] + dot_tn(wide[rows, lanes], recv_g[...])
            out[at : at + CH, :] = (total * SCALE).astype(BF)
    out[9 * CH : 12 * CH, :] = time_part[...]


def spread_kernel(owner, pos, half, *refs):
    spat1, spat2, time1, time2, stage, sems = refs[-6:]
    targets = [(spat2, time1), (spat1, time2)]

    def copies(at):
        space, time = targets[at]
        for piece in range(12):
            source = stage.at[pl.ds(piece * CH, CH)]
            target = space if piece < 9 else time
            part = pl.ds((piece if piece < 9 else piece - 9) * CH, CH)
            yield pltpu.make_async_copy(source, target.at[part], sems.at[piece])

    for at in range(2):

        @pl.when((pos[0] ^ owner) == at)
        def _():
            for piece, copy in enumerate(copies(at)):
                rows = slice(piece * CH, (piece + 1) * CH)
                stage[rows, :] = half[rows, :].astype(F32)
                copy.start()
            for copy in copies(at):
                copy.wait()


def input_kernel(first_grad, w1, out, wide):
    fill_windows(wide, first_grad[...])
    out[...] = back_from(wide, w1).astype(BF)


def swap_cores(values):
    return lax.ppermute(values, "core", [(0, 1), (1, 0)])


def swap_frames(values):
    blocks = values.reshape(PIX // COLS, COLS, CH)
    return lax.all_to_all(blocks, FRAME_AXES, 0, 0, tiled=True).reshape(PIX, CH)


def scatter_sum(values, axes, count):
    parts = values.reshape(count, -1, CH)
    arrived = lax.all_to_all(parts, axes, 0, 0, tiled=True)
    return jnp.sum(arrived.astype(F32), axis=0).astype(BF)


def gather_all(values, axes, count):
    copies = jnp.broadcast_to(values[None], (count,) + values.shape)
    return lax.all_to_all(copies, axes, 0, 0, tiled=True).reshape(-1, CH)


def body(video, cotangent, w_spat1, w_spat2, w_time1, w_time2):
    pos = lax.axis_index("core").astype(jnp.int32).reshape(1)
    w1, w2, wt1, wt2 = (w.reshape(-1, CH) for w in (w_spat1, w_spat2, w_time1, w_time2))
    rows = PIX // COLS
    slab = ((PIX, CH), BF)
    pair = ((2, rows, COLS, CH), BF)
    wide, tall = pltpu.VMEM((PAD, 3 * CH), BF), pltpu.VMEM((PAD, CH), BF)
    frame, lines = pltpu.VMEM((PIX, CH), BF), pltpu.VMEM((rows, COLS, CH), BF)
    both_slopes = pltpu.VMEM((2, PIX, CH), BF)
    space, time = pltpu.VMEM((9 * CH, CH), BF), pltpu.VMEM((3 * CH, CH), BF)
    conv_flops, time_flops = 2 * PIX * 9 * CH * CH, 2 * PIX * 3 * CH * CH

    both, slopes, keep_x, send_x = call(
        forward_kernel,
        [((rows, 2 * COLS, CH), BF), ((2, PIX, CH), BF), slab, slab],
        (pos, video.reshape(PIX, CH), cotangent.reshape(rows, COLS, CH), w1, w2),
        [frame, frame, pltpu.VMEM((rows, 2 * COLS, CH), BF), both_slopes, space, space, wide, pltpu.SemaphoreType.DMA((15,))],
        2 * conv_flops,
        (1, 2, 3, 4),
        (0, 1, 2, 3),
        vmem=60,
    )
    both = lax.all_to_all(both, FRAME_AXES, 0, 0, tiled=True)
    recv_x = swap_cores(send_x)
    act_back, keep_t, send_t = call(
        time_kernel,
        [slab, pair, pair],
        (pos, both, wt1, wt2),
        [lines, lines, time, time, lines, lines, frame, tall, tall, tall, pltpu.SemaphoreType.DMA((10,))],
        3 * time_flops,
        (1, 2, 3),
        (0, 1, 2),
        vmem=60,
    )
    act_back = swap_frames(act_back)
    recv_t = swap_cores(send_t)
    keep_t, recv_t = keep_t.reshape(2, PIX, CH), recv_t.reshape(2, PIX, CH)
    (time_part,) = call(
        time_weights_kernel, [((3 * CH, CH), BF)], (keep_t, recv_t), (), 2 * time_flops
    )
    first_grad, keep_g, send_g = call(
        backward_kernel, [slab, slab, slab], (pos, act_back, slopes, w2), [wide], conv_flops
    )
    recv_g = swap_cores(send_g)
    (partial,) = call(
        own_weights_kernel, [((9 * CH, CH), F32)], (keep_x, keep_g), [wide], conv_flops
    )
    (part,) = call(
        space_weights_kernel,
        [((12 * CH, CH), BF)],
        (partial, recv_x, recv_g, time_part),
        [wide],
        conv_flops,
    )

    part = scatter_sum(part, ("y", "zl", "x"), 32)
    part = jnp.sum(gather_all(part, "zh", 4).reshape(4, -1, CH).astype(F32), axis=0).astype(BF)
    part = gather_all(part, ("y", "zl", "x"), 32)
    peer = swap_cores(part)
    part, first_grad = lax.optimization_barrier((part, first_grad))
    (grad_input,) = call(input_kernel, [slab], (first_grad, w1), [wide], conv_flops)
    grads = [((9 * CH, CH), F32)] * 2 + [((3 * CH, CH), F32)] * 2
    scratch = [pltpu.VMEM((12 * CH, CH), F32), pltpu.SemaphoreType.DMA((12,))]
    outs = call(
        functools.partial(spread_kernel, 0), grads, (pos, part), scratch, 0, (), (0, 1, 2, 3)
    )
    outs = call(
        functools.partial(spread_kernel, 1),
        grads,
        (pos, peer, *outs),
        scratch,
        0,
        (2, 3, 4, 5),
        (0, 1, 2, 3),
        {2: 0, 3: 1, 4: 2, 5: 3},
    )
    return (
        grad_input.reshape(video.shape),
        outs[0].reshape(w_spat1.shape),
        outs[1].reshape(w_spat2.shape),
        outs[2].reshape(w_time1.shape),
        outs[3].reshape(w_time2.shape),
    )


def solution(mesh):
    fine = Mesh(mesh.devices.reshape(4, 2, 4, 4, 2), ("zh", "zl", "x", "y", "core"))
    frames = P(("y", "core"), FRAME_AXES, None, None, None)
    return jax.shard_map(
        body,
        mesh=fine,
        in_specs=(frames, frames, P(), P(), P(), P()),
        out_specs=(frames, P(), P(), P(), P()),
        check_vma=False,
    )
```

```python
import functools
import math

import jax
import jax.numpy as jnp
from jax import lax
from jax.experimental import pallas as pl
from jax.experimental.pallas import tpu as pltpu
from jax.sharding import Mesh
from jax.sharding import PartitionSpec as P

CH = 256
COLS = 16
PIX = 512
HALF = PIX // 2
PAD = PIX + 2 * COLS
FRAME_AXES = ("zh", "zl", "x")
SCALE = 1.0 / math.sqrt(131072)
BF = jnp.bfloat16
F32 = jnp.float32
VMEM = pl.BlockSpec(memory_space=pltpu.VMEM)
SMEM = pl.BlockSpec(memory_space=pltpu.SMEM)
HBM = pl.BlockSpec(memory_space=pltpu.HBM)


def dot_nn(left, right):
    return lax.dot_general(left, right, (((1,), (0,)), ((), ())), preferred_element_type=F32)


def dot_nt(left, right):
    return lax.dot_general(left, right, (((1,), (1,)), ((), ())), preferred_element_type=F32)


def dot_tn(left, right):
    return lax.dot_general(left, right, (((0,), (0,)), ((), ())), preferred_element_type=F32)


def call(kernel, outs, ins, scratch=(), flops=0, hbm_in=(), hbm_out=(), aliases=None, vmem=40):
    specs = [SMEM if value.dtype == jnp.int32 else VMEM for value in ins]
    for at in hbm_in:
        specs[at] = HBM
    moved = sum(value.size * value.dtype.itemsize for value in ins)
    return pl.pallas_call(
        kernel,
        out_shape=[jax.ShapeDtypeStruct(shape, kind) for shape, kind in outs],
        in_specs=specs,
        out_specs=[HBM if at in hbm_out else VMEM for at in range(len(outs))],
        scratch_shapes=list(scratch),
        input_output_aliases=aliases or {},
        cost_estimate=pl.CostEstimate(flops=flops, bytes_accessed=moved, transcendentals=0),
        compiler_params=pltpu.CompilerParams(vmem_limit_bytes=vmem * 1024 * 1024),
    )(*ins)


def start_by_core(pos, sems, first, pairs):
    for at, (even, odd, target) in enumerate(pairs):

        @pl.when(pos[0] == 0)
        def _():
            pltpu.make_async_copy(even, target, sems.at[first + at]).start()

        @pl.when(pos[0] != 0)
        def _():
            pltpu.make_async_copy(odd, target, sems.at[first + at]).start()


def wait_by_core(sems, first, pairs):
    for at, (even, _, target) in enumerate(pairs):
        pltpu.make_async_copy(even, target, sems.at[first + at]).wait()


def fill_windows(wide, values):
    edge = jnp.zeros((COLS, 3 * CH), BF)
    wide[0:COLS, :] = edge
    wide[COLS + PIX : PAD, :] = edge
    column = lax.broadcasted_iota(jnp.int32, (PIX, CH), 0) & (COLS - 1)
    full = values.astype(F32)
    before = jnp.where(column == 0, 0.0, pltpu.roll(full, 1, 0))
    after = jnp.where(column == COLS - 1, 0.0, pltpu.roll(full, PIX - 1, 0))
    wide[COLS : COLS + PIX, 0:CH] = before.astype(BF)
    wide[COLS : COLS + PIX, CH : 2 * CH] = values.astype(BF)
    wide[COLS : COLS + PIX, 2 * CH : 3 * CH] = after.astype(BF)


def conv_half(wide, weight, half):
    total = None
    for tap in range(3):
        at = tap * COLS + half * HALF
        term = dot_nn(wide[at : at + HALF, :], weight[tap * 3 * CH : (tap + 1) * 3 * CH, :])
        total = term if total is None else total + term
    return total


def back_from(wide, weight):
    total = None
    for tap in range(3):
        for side in range(3):
            at = (tap * 3 + side) * CH
            term = dot_nt(
                wide[(2 - tap) * COLS : (2 - tap) * COLS + PIX, (2 - side) * CH : (3 - side) * CH],
                weight[at : at + CH, :],
            )
            total = term if total is None else total + term
    return total


def silu_pair(pre):
    sigma = 0.5 + 0.5 * jnp.tanh(0.5 * pre)
    act = pre * sigma
    return act, sigma * (1.0 + pre * (1.0 - sigma))


def forward_kernel(pos, video_at, cot_at, w1_at, w2_at, both_at, slopes_at, keep, send, *rest):
    video, first, both, slopes, w1, w2, wide, sems = rest
    pieces = [(video_at, video)]
    for source, target in ((w1_at, w1), (w2_at, w2)):
        for tap in range(3):
            part = pl.ds(tap * 3 * CH, 3 * CH)
            pieces.append((source.at[part], target.at[part]))
    pieces.append((cot_at, both.at[:, COLS : 2 * COLS, :]))
    pieces.append((slopes.at[0], slopes_at.at[0]))
    for half in range(2):
        part = pl.ds(half * HALF, HALF)
        pieces.append((slopes.at[1, part], slopes_at.at[1, part]))
        part = pl.ds(half * (HALF // COLS), HALF // COLS)
        pieces.append((both.at[part], both_at.at[part]))
    moves = [
        pltpu.make_async_copy(source, target, sems.at[at])
        for at, (source, target) in enumerate(pieces)
    ]
    for move in moves[0:8]:
        move.start()
    moves[0].wait()
    fill_windows(wide, video[...])
    for move in moves[1:4]:
        move.wait()
    for half in range(2):
        rows = slice(half * HALF, (half + 1) * HALF)
        act, slope = silu_pair(conv_half(wide, w1, half))
        first[rows, :] = act.astype(BF)
        slopes[0, rows, :] = slope.astype(BF)
    stores = [(first, video, keep), (video, first, send)]
    start_by_core(pos, sems, 13, stores)
    moves[8].start()
    fill_windows(wide, first[...])
    for move in moves[4:8]:
        move.wait()
    for half in range(2):
        rows = slice(half * HALF, (half + 1) * HALF)
        act, slope = silu_pair(conv_half(wide, w2, half))
        lines = HALF // COLS
        both[half * lines : (half + 1) * lines, 0:COLS, :] = act.astype(BF).reshape(lines, COLS, CH)
        slopes[1, rows, :] = slope.astype(BF)
    for move in moves[9:13]:
        move.start()
    for move in moves[8:13]:
        move.wait()
    wait_by_core(sems, 13, stores)


def ahead_sum(padded, weight, half):
    total = None
    for step in range(3):
        at = step * COLS + half * HALF
        term = dot_nt(padded[at : at + HALF, :], weight[step * CH : (step + 1) * CH, :])
        total = term if total is None else total + term
    return total


def time_kernel(pos, both_at, wt1_at, wt2_at, back_at, keep, send, *rest):
    act, cot, wt1, wt2, time_act, time_grad, act_back, behind, ahead, later, sems = rest
    loads = [
        pltpu.make_async_copy(source, target, sems.at[at])
        for at, (source, target) in enumerate(
            [
                (both_at.at[:, COLS : 2 * COLS, :], cot),
                (wt2_at, wt2),
                (both_at.at[:, 0:COLS, :], act),
                (wt1_at, wt1),
            ]
        )
    ]
    for load in loads:
        load.start()
    edge = jnp.zeros((2 * COLS, CH), BF)
    loads[0].wait()
    ahead[0:PIX, :] = cot[...].reshape(PIX, CH)
    ahead[PIX:PAD, :] = edge
    loads[2].wait()
    behind[0 : 2 * COLS, :] = edge
    behind[2 * COLS : PAD, :] = act[...].reshape(PIX, CH)
    loads[1].wait()
    loads[3].wait()
    for half in range(2):
        pre = None
        for step in range(3):
            at = (2 - step) * COLS + half * HALF
            term = dot_nn(behind[at : at + HALF, :], wt1[step * CH : (step + 1) * CH, :])
            pre = term if pre is None else pre + term
        value, slope = silu_pair(pre)
        grad = (ahead_sum(ahead, wt2, half) * slope).astype(BF)
        lines = slice(half * (HALF // COLS), (half + 1) * (HALF // COLS))
        time_act[lines] = value.astype(BF).reshape(HALF // COLS, COLS, CH)
        time_grad[lines] = grad.reshape(HALF // COLS, COLS, CH)
        later[half * HALF : (half + 1) * HALF, :] = grad
    later[PIX:PAD, :] = edge
    stores = [
        (act, time_act, keep.at[0]),
        (time_grad, cot, keep.at[1]),
        (time_act, act, send.at[0]),
        (cot, time_grad, send.at[1]),
    ]
    start_by_core(pos, sems, 4, stores)
    tails = []
    for half in range(2):
        rows = pl.ds(half * HALF, HALF)
        act_back[rows, :] = ahead_sum(later, wt1, half).astype(BF)
        tails.append(pltpu.make_async_copy(act_back.at[rows], back_at.at[rows], sems.at[8 + half]))
        tails[half].start()
    wait_by_core(sems, 4, stores)
    for tail in tails:
        tail.wait()


def time_weights_kernel(keep, recv, out):
    for step in range(3):
        rows = PIX - step * COLS
        total = dot_tn(keep[0, 0:rows, :], keep[1, step * COLS : PIX, :])
        total = total + dot_tn(recv[0, 0:rows, :], recv[1, step * COLS : PIX, :])
        out[step * CH : (step + 1) * CH, :] = (total * SCALE).astype(BF)


def backward_kernel(pos, act_back, slopes, w2, first_grad, keep, send, wide):
    second = (act_back[...].astype(F32) * slopes[1].astype(F32)).astype(BF)
    fill_windows(wide, second)
    first = (back_from(wide, w2) * slopes[0].astype(F32)).astype(BF)
    first_grad[...] = first

    @pl.when(pos[0] == 0)
    def _():
        keep[...] = second
        send[...] = first

    @pl.when(pos[0] != 0)
    def _():
        keep[...] = first
        send[...] = second


def own_weights_kernel(keep_x, keep_g, out, wide):
    fill_windows(wide, keep_x[...])
    for tap in range(3):
        for side in range(3):
            rows = slice(tap * COLS, tap * COLS + PIX)
            lanes = slice(side * CH, (side + 1) * CH)
            at = (tap * 3 + side) * CH
            out[at : at + CH, :] = dot_tn(wide[rows, lanes], keep_g[...])


def space_weights_kernel(partial, recv_x, recv_g, time_part, out, wide):
    fill_windows(wide, recv_x[...])
    for tap in range(3):
        for side in range(3):
            rows = slice(tap * COLS, tap * COLS + PIX)
            lanes = slice(side * CH, (side + 1) * CH)
            at = (tap * 3 + side) * CH
            total = partial[at : at + CH, :] + dot_tn(wide[rows, lanes], recv_g[...])
            out[at : at + CH, :] = (total * SCALE).astype(BF)
    out[9 * CH : 12 * CH, :] = time_part[...]


def spread_kernel(owner, pos, half, *refs):
    spat1, spat2, time1, time2, stage, sems = refs[-6:]
    targets = [(spat2, time1), (spat1, time2)]

    def copies(at):
        space, time = targets[at]
        rows = 3 * CH
        for piece in range(3):
            part = pl.ds(piece * rows, rows)
            yield pltpu.make_async_copy(stage.at[part], space.at[part], sems.at[piece])
        yield pltpu.make_async_copy(stage.at[pl.ds(3 * rows, rows)], time, sems.at[3])

    for at in range(2):

        @pl.when((pos[0] ^ owner) == at)
        def _():
            for piece, copy in enumerate(copies(at)):
                rows = slice(piece * 3 * CH, (piece + 1) * 3 * CH)
                stage[rows, :] = half[rows, :].astype(F32)
                copy.start()
            for copy in copies(at):
                copy.wait()


def input_kernel(first_grad, w1, out, wide):
    fill_windows(wide, first_grad[...])
    out[...] = back_from(wide, w1).astype(BF)


def swap_cores(values):
    return lax.ppermute(values, "core", [(0, 1), (1, 0)])


def swap_frames(values):
    blocks = values.reshape(PIX // COLS, COLS, CH)
    return lax.all_to_all(blocks, FRAME_AXES, 0, 0, tiled=True).reshape(PIX, CH)


def scatter_sum(values, axes, count):
    parts = values.reshape(count, -1, CH)
    arrived = lax.all_to_all(parts, axes, 0, 0, tiled=True)
    return jnp.sum(arrived.astype(F32), axis=0).astype(BF)


def gather_all(values, axes, count):
    copies = jnp.broadcast_to(values[None], (count,) + values.shape)
    return lax.all_to_all(copies, axes, 0, 0, tiled=True).reshape(-1, CH)


def body(video, cotangent, w_spat1, w_spat2, w_time1, w_time2):
    pos = lax.axis_index("core").astype(jnp.int32).reshape(1)
    w1, w2, wt1, wt2 = (w.reshape(-1, CH) for w in (w_spat1, w_spat2, w_time1, w_time2))
    rows = PIX // COLS
    slab = ((PIX, CH), BF)
    pair = ((2, rows, COLS, CH), BF)
    wide, tall = pltpu.VMEM((PAD, 3 * CH), BF), pltpu.VMEM((PAD, CH), BF)
    frame, lines = pltpu.VMEM((PIX, CH), BF), pltpu.VMEM((rows, COLS, CH), BF)
    both_slopes = pltpu.VMEM((2, PIX, CH), BF)
    space, time = pltpu.VMEM((9 * CH, CH), BF), pltpu.VMEM((3 * CH, CH), BF)
    conv_flops, time_flops = 2 * PIX * 9 * CH * CH, 2 * PIX * 3 * CH * CH

    both, slopes, keep_x, send_x = call(
        forward_kernel,
        [((rows, 2 * COLS, CH), BF), ((2, PIX, CH), BF), slab, slab],
        (pos, video.reshape(PIX, CH), cotangent.reshape(rows, COLS, CH), w1, w2),
        [frame, frame, pltpu.VMEM((rows, 2 * COLS, CH), BF), both_slopes, space, space, wide, pltpu.SemaphoreType.DMA((15,))],
        2 * conv_flops,
        (1, 2, 3, 4),
        (0, 1, 2, 3),
        vmem=60,
    )
    both = lax.all_to_all(both, FRAME_AXES, 0, 0, tiled=True)
    recv_x = swap_cores(send_x)
    act_back, keep_t, send_t = call(
        time_kernel,
        [slab, pair, pair],
        (pos, both, wt1, wt2),
        [lines, lines, time, time, lines, lines, frame, tall, tall, tall, pltpu.SemaphoreType.DMA((10,))],
        3 * time_flops,
        (1, 2, 3),
        (0, 1, 2),
        vmem=60,
    )
    act_back = swap_frames(act_back)
    recv_t = swap_cores(send_t)
    keep_t, recv_t = keep_t.reshape(2, PIX, CH), recv_t.reshape(2, PIX, CH)
    (time_part,) = call(
        time_weights_kernel, [((3 * CH, CH), BF)], (keep_t, recv_t), (), 2 * time_flops
    )
    first_grad, keep_g, send_g = call(
        backward_kernel, [slab, slab, slab], (pos, act_back, slopes, w2), [wide], conv_flops
    )
    recv_g = swap_cores(send_g)
    (partial,) = call(
        own_weights_kernel, [((9 * CH, CH), F32)], (keep_x, keep_g), [wide], conv_flops
    )
    (part,) = call(
        space_weights_kernel,
        [((12 * CH, CH), BF)],
        (partial, recv_x, recv_g, time_part),
        [wide],
        conv_flops,
    )

    part = scatter_sum(part, ("zl", "x", "y"), 32)
    for pairs in (((0, 1), (1, 0), (2, 3), (3, 2)), ((0, 3), (3, 0), (1, 2), (2, 1))):
        arrived = lax.ppermute(part, "zh", pairs)
        part = (part.astype(F32) + arrived.astype(F32)).astype(BF)
    part = gather_all(part, ("zl", "x", "y"), 32)
    peer = swap_cores(part)
    part, first_grad = lax.optimization_barrier((part, first_grad))
    (grad_input,) = call(input_kernel, [slab], (first_grad, w1), [wide], conv_flops)
    grads = [((9 * CH, CH), F32)] * 2 + [((3 * CH, CH), F32)] * 2
    scratch = [pltpu.VMEM((12 * CH, CH), F32), pltpu.SemaphoreType.DMA((4,))]
    outs = call(
        functools.partial(spread_kernel, 0), grads, (pos, part), scratch, 0, (), (0, 1, 2, 3)
    )
    outs = call(
        functools.partial(spread_kernel, 1),
        grads,
        (pos, peer, *outs),
        scratch,
        0,
        (2, 3, 4, 5),
        (0, 1, 2, 3),
        {2: 0, 3: 1, 4: 2, 5: 3},
    )
    return (
        grad_input.reshape(video.shape),
        outs[0].reshape(w_spat1.shape),
        outs[1].reshape(w_spat2.shape),
        outs[2].reshape(w_time1.shape),
        outs[3].reshape(w_time2.shape),
    )


def solution(mesh):
    fine = Mesh(mesh.devices.reshape(4, 2, 4, 4, 2), ("zh", "zl", "x", "y", "core"))
    frames = P(("y", "core"), FRAME_AXES, None, None, None)
    return jax.shard_map(
        body,
        mesh=fine,
        in_specs=(frames, frames, P(), P(), P(), P()),
        out_specs=(frames, P(), P(), P(), P()),
        check_vma=False,
    )
```

```python
import functools
import math

import jax
import jax.numpy as jnp
from jax import lax
from jax.experimental import pallas as pl
from jax.experimental.pallas import tpu as pltpu
from jax.sharding import Mesh
from jax.sharding import PartitionSpec as P

CH = 256
COLS = 16
PIX = 512
HALF = PIX // 2
PAD = PIX + 2 * COLS
FRAME_AXES = ("zh", "zl", "x")
SCALE = 1.0 / math.sqrt(131072)
BF = jnp.bfloat16
F32 = jnp.float32
VMEM = pl.BlockSpec(memory_space=pltpu.VMEM)
SMEM = pl.BlockSpec(memory_space=pltpu.SMEM)
HBM = pl.BlockSpec(memory_space=pltpu.HBM)


def dot_nn(left, right):
    return lax.dot_general(left, right, (((1,), (0,)), ((), ())), preferred_element_type=F32)


def dot_nt(left, right):
    return lax.dot_general(left, right, (((1,), (1,)), ((), ())), preferred_element_type=F32)


def dot_tn(left, right):
    return lax.dot_general(left, right, (((0,), (0,)), ((), ())), preferred_element_type=F32)


def call(kernel, outs, ins, scratch=(), flops=0, hbm_in=(), hbm_out=(), aliases=None, vmem=40):
    specs = [SMEM if value.dtype == jnp.int32 else VMEM for value in ins]
    for at in hbm_in:
        specs[at] = HBM
    moved = sum(value.size * value.dtype.itemsize for value in ins)
    return pl.pallas_call(
        kernel,
        out_shape=[jax.ShapeDtypeStruct(shape, kind) for shape, kind in outs],
        in_specs=specs,
        out_specs=[HBM if at in hbm_out else VMEM for at in range(len(outs))],
        scratch_shapes=list(scratch),
        input_output_aliases=aliases or {},
        cost_estimate=pl.CostEstimate(flops=flops, bytes_accessed=moved, transcendentals=0),
        compiler_params=pltpu.CompilerParams(vmem_limit_bytes=vmem * 1024 * 1024),
    )(*ins)


def start_by_core(pos, sems, first, pairs):
    for at, (even, odd, target) in enumerate(pairs):

        @pl.when(pos[0] == 0)
        def _():
            pltpu.make_async_copy(even, target, sems.at[first + at]).start()

        @pl.when(pos[0] != 0)
        def _():
            pltpu.make_async_copy(odd, target, sems.at[first + at]).start()


def wait_by_core(sems, first, pairs):
    for at, (even, _, target) in enumerate(pairs):
        pltpu.make_async_copy(even, target, sems.at[first + at]).wait()


def fill_windows(wide, values):
    edge = jnp.zeros((COLS, 3 * CH), BF)
    wide[0:COLS, :] = edge
    wide[COLS + PIX : PAD, :] = edge
    column = lax.broadcasted_iota(jnp.int32, (PIX, CH), 0) & (COLS - 1)
    full = values.astype(F32)
    before = jnp.where(column == 0, 0.0, pltpu.roll(full, 1, 0))
    after = jnp.where(column == COLS - 1, 0.0, pltpu.roll(full, PIX - 1, 0))
    wide[COLS : COLS + PIX, 0:CH] = before.astype(BF)
    wide[COLS : COLS + PIX, CH : 2 * CH] = values.astype(BF)
    wide[COLS : COLS + PIX, 2 * CH : 3 * CH] = after.astype(BF)


def conv_half(wide, weight, half):
    total = None
    for tap in range(3):
        at = tap * COLS + half * HALF
        term = dot_nn(wide[at : at + HALF, :], weight[tap * 3 * CH : (tap + 1) * 3 * CH, :])
        total = term if total is None else total + term
    return total


def back_from(wide, weight):
    total = None
    for tap in range(3):
        for side in range(3):
            at = (tap * 3 + side) * CH
            term = dot_nt(
                wide[(2 - tap) * COLS : (2 - tap) * COLS + PIX, (2 - side) * CH : (3 - side) * CH],
                weight[at : at + CH, :],
            )
            total = term if total is None else total + term
    return total


def silu_pair(pre):
    sigma = 0.5 + 0.5 * jnp.tanh(0.5 * pre)
    act = pre * sigma
    return act, sigma * (1.0 + pre * (1.0 - sigma))


def forward_kernel(pos, video_at, cot_at, w1_at, w2_at, both_at, slopes_at, keep, send, *rest):
    video, first, both, slopes, w1, w2, wide, sems = rest
    pieces = [(video_at, video)]
    for source, target in ((w1_at, w1), (w2_at, w2)):
        for tap in range(3):
            part = pl.ds(tap * 3 * CH, 3 * CH)
            pieces.append((source.at[part], target.at[part]))
    pieces.append((cot_at, both.at[:, COLS : 2 * COLS, :]))
    pieces.append((slopes.at[0], slopes_at.at[0]))
    for half in range(2):
        part = pl.ds(half * HALF, HALF)
        pieces.append((slopes.at[1, part], slopes_at.at[1, part]))
        part = pl.ds(half * (HALF // COLS), HALF // COLS)
        pieces.append((both.at[part], both_at.at[part]))
    moves = [
        pltpu.make_async_copy(source, target, sems.at[at])
        for at, (source, target) in enumerate(pieces)
    ]
    for move in moves[0:8]:
        move.start()
    moves[0].wait()
    fill_windows(wide, video[...])
    for move in moves[1:4]:
        move.wait()
    for half in range(2):
        rows = slice(half * HALF, (half + 1) * HALF)
        act, slope = silu_pair(conv_half(wide, w1, half))
        first[rows, :] = act.astype(BF)
        slopes[0, rows, :] = slope.astype(BF)
    stores = [(first, video, keep), (video, first, send)]
    start_by_core(pos, sems, 13, stores)
    moves[8].start()
    fill_windows(wide, first[...])
    for move in moves[4:8]:
        move.wait()
    for half in range(2):
        rows = slice(half * HALF, (half + 1) * HALF)
        act, slope = silu_pair(conv_half(wide, w2, half))
        lines = HALF // COLS
        both[half * lines : (half + 1) * lines, 0:COLS, :] = act.astype(BF).reshape(lines, COLS, CH)
        slopes[1, rows, :] = slope.astype(BF)
    for move in moves[9:13]:
        move.start()
    for move in moves[8:13]:
        move.wait()
    wait_by_core(sems, 13, stores)


def ahead_sum(padded, weight, half):
    total = None
    for step in range(3):
        at = step * COLS + half * HALF
        term = dot_nt(padded[at : at + HALF, :], weight[step * CH : (step + 1) * CH, :])
        total = term if total is None else total + term
    return total


def time_kernel(pos, both_at, wt1_at, wt2_at, back_at, keep, send, *rest):
    act, cot, wt1, wt2, time_act, time_grad, act_back, behind, ahead, later, sems = rest
    loads = [
        pltpu.make_async_copy(source, target, sems.at[at])
        for at, (source, target) in enumerate(
            [
                (both_at.at[:, COLS : 2 * COLS, :], cot),
                (wt2_at, wt2),
                (both_at.at[:, 0:COLS, :], act),
                (wt1_at, wt1),
            ]
        )
    ]
    for load in loads:
        load.start()
    edge = jnp.zeros((2 * COLS, CH), BF)
    loads[0].wait()
    ahead[0:PIX, :] = cot[...].reshape(PIX, CH)
    ahead[PIX:PAD, :] = edge
    loads[2].wait()
    behind[0 : 2 * COLS, :] = edge
    behind[2 * COLS : PAD, :] = act[...].reshape(PIX, CH)
    loads[1].wait()
    loads[3].wait()
    for half in range(2):
        pre = None
        for step in range(3):
            at = (2 - step) * COLS + half * HALF
            term = dot_nn(behind[at : at + HALF, :], wt1[step * CH : (step + 1) * CH, :])
            pre = term if pre is None else pre + term
        value, slope = silu_pair(pre)
        grad = (ahead_sum(ahead, wt2, half) * slope).astype(BF)
        lines = slice(half * (HALF // COLS), (half + 1) * (HALF // COLS))
        time_act[lines] = value.astype(BF).reshape(HALF // COLS, COLS, CH)
        time_grad[lines] = grad.reshape(HALF // COLS, COLS, CH)
        later[half * HALF : (half + 1) * HALF, :] = grad
    later[PIX:PAD, :] = edge
    stores = [
        (act, time_act, keep.at[0]),
        (time_grad, cot, keep.at[1]),
        (time_act, act, send.at[0]),
        (cot, time_grad, send.at[1]),
    ]
    start_by_core(pos, sems, 4, stores)
    tails = []
    for half in range(2):
        rows = pl.ds(half * HALF, HALF)
        act_back[rows, :] = ahead_sum(later, wt1, half).astype(BF)
        tails.append(pltpu.make_async_copy(act_back.at[rows], back_at.at[rows], sems.at[8 + half]))
        tails[half].start()
    wait_by_core(sems, 4, stores)
    for tail in tails:
        tail.wait()


def time_weights_kernel(keep, recv, out):
    for step in range(3):
        rows = PIX - step * COLS
        total = dot_tn(keep[0, 0:rows, :], keep[1, step * COLS : PIX, :])
        total = total + dot_tn(recv[0, 0:rows, :], recv[1, step * COLS : PIX, :])
        out[step * CH : (step + 1) * CH, :] = (total * SCALE).astype(BF)


def backward_kernel(pos, act_back, slopes, w2, first_grad, keep, send, wide):
    second = (act_back[...].astype(F32) * slopes[1].astype(F32)).astype(BF)
    fill_windows(wide, second)
    first = (back_from(wide, w2) * slopes[0].astype(F32)).astype(BF)
    first_grad[...] = first

    @pl.when(pos[0] == 0)
    def _():
        keep[...] = second
        send[...] = first

    @pl.when(pos[0] != 0)
    def _():
        keep[...] = first
        send[...] = second


def own_weights_kernel(keep_x, keep_g, out, wide):
    fill_windows(wide, keep_x[...])
    for tap in range(3):
        for side in range(3):
            rows = slice(tap * COLS, tap * COLS + PIX)
            lanes = slice(side * CH, (side + 1) * CH)
            at = (tap * 3 + side) * CH
            out[at : at + CH, :] = dot_tn(wide[rows, lanes], keep_g[...])


def space_weights_kernel(partial, recv_x, recv_g, time_part, out, wide):
    fill_windows(wide, recv_x[...])
    for tap in range(3):
        for side in range(3):
            rows = slice(tap * COLS, tap * COLS + PIX)
            lanes = slice(side * CH, (side + 1) * CH)
            at = (tap * 3 + side) * CH
            total = partial[at : at + CH, :] + dot_tn(wide[rows, lanes], recv_g[...])
            out[at : at + CH, :] = (total * SCALE).astype(BF)
    out[9 * CH : 12 * CH, :] = time_part[...]


def spread_kernel(owner, pieces, pos, half, *refs):
    spat1, spat2, time1, time2, stage, sems = refs[-6:]
    targets = [(spat2, time1), (spat1, time2)]
    rows = 3 * CH

    def copies(at):
        space, time = targets[at]
        for slot, piece in enumerate(pieces):
            target = space.at[pl.ds(piece * rows, rows)] if piece < 3 else time
            source = stage.at[pl.ds(slot * rows, rows)]
            yield pltpu.make_async_copy(source, target, sems.at[slot])

    for at in range(2):

        @pl.when((pos[0] ^ owner) == at)
        def _():
            for slot, copy in enumerate(copies(at)):
                part = slice(slot * rows, (slot + 1) * rows)
                stage[part, :] = half[part, :].astype(F32)
                copy.start()
            for copy in copies(at):
                copy.wait()


def input_kernel(first_grad, w1, out, wide):
    fill_windows(wide, first_grad[...])
    out[...] = back_from(wide, w1).astype(BF)


def swap_cores(values):
    return lax.ppermute(values, "core", [(0, 1), (1, 0)])


def swap_frames(values):
    blocks = values.reshape(PIX // COLS, COLS, CH)
    return lax.all_to_all(blocks, FRAME_AXES, 0, 0, tiled=True).reshape(PIX, CH)


def scatter_sum(values, axes, count):
    parts = values.reshape(count, -1, CH)
    arrived = lax.all_to_all(parts, axes, 0, 0, tiled=True)
    return jnp.sum(arrived.astype(F32), axis=0).astype(BF)


def gather_all(values, axes, count):
    copies = jnp.broadcast_to(values[None], (count,) + values.shape)
    return lax.all_to_all(copies, axes, 0, 0, tiled=True).reshape(-1, CH)


def body(video, cotangent, w_spat1, w_spat2, w_time1, w_time2):
    pos = lax.axis_index("core").astype(jnp.int32).reshape(1)
    w1, w2, wt1, wt2 = (w.reshape(-1, CH) for w in (w_spat1, w_spat2, w_time1, w_time2))
    rows = PIX // COLS
    slab = ((PIX, CH), BF)
    pair = ((2, rows, COLS, CH), BF)
    wide, tall = pltpu.VMEM((PAD, 3 * CH), BF), pltpu.VMEM((PAD, CH), BF)
    frame, lines = pltpu.VMEM((PIX, CH), BF), pltpu.VMEM((rows, COLS, CH), BF)
    both_slopes = pltpu.VMEM((2, PIX, CH), BF)
    space, time = pltpu.VMEM((9 * CH, CH), BF), pltpu.VMEM((3 * CH, CH), BF)
    conv_flops, time_flops = 2 * PIX * 9 * CH * CH, 2 * PIX * 3 * CH * CH

    both, slopes, keep_x, send_x = call(
        forward_kernel,
        [((rows, 2 * COLS, CH), BF), ((2, PIX, CH), BF), slab, slab],
        (pos, video.reshape(PIX, CH), cotangent.reshape(rows, COLS, CH), w1, w2),
        [frame, frame, pltpu.VMEM((rows, 2 * COLS, CH), BF), both_slopes, space, space, wide, pltpu.SemaphoreType.DMA((15,))],
        2 * conv_flops,
        (1, 2, 3, 4),
        (0, 1, 2, 3),
        vmem=60,
    )
    both = lax.all_to_all(both, FRAME_AXES, 0, 0, tiled=True)
    recv_x = swap_cores(send_x)
    act_back, keep_t, send_t = call(
        time_kernel,
        [slab, pair, pair],
        (pos, both, wt1, wt2),
        [lines, lines, time, time, lines, lines, frame, tall, tall, tall, pltpu.SemaphoreType.DMA((10,))],
        3 * time_flops,
        (1, 2, 3),
        (0, 1, 2),
        vmem=60,
    )
    act_back = swap_frames(act_back)
    recv_t = swap_cores(send_t)
    keep_t, recv_t = keep_t.reshape(2, PIX, CH), recv_t.reshape(2, PIX, CH)
    (time_part,) = call(
        time_weights_kernel, [((3 * CH, CH), BF)], (keep_t, recv_t), (), 2 * time_flops
    )
    first_grad, keep_g, send_g = call(
        backward_kernel, [slab, slab, slab], (pos, act_back, slopes, w2), [wide], conv_flops
    )
    recv_g = swap_cores(send_g)
    (partial,) = call(
        own_weights_kernel, [((9 * CH, CH), F32)], (keep_x, keep_g), [wide], conv_flops
    )
    (part,) = call(
        space_weights_kernel,
        [((12 * CH, CH), BF)],
        (partial, recv_x, recv_g, time_part),
        [wide],
        conv_flops,
    )

    part = scatter_sum(part, ("zl", "x", "y"), 32)
    part, first_grad = lax.optimization_barrier((part, first_grad))
    (grad_input,) = call(input_kernel, [slab], (first_grad, w1), [wide], conv_flops)
    for pairs in (((0, 1), (1, 0), (2, 3), (3, 2)), ((0, 3), (3, 0), (1, 2), (2, 1))):
        arrived = lax.ppermute(part, "zh", pairs)
        arrived, grad_input = lax.optimization_barrier((arrived, grad_input))
        part = (part.astype(F32) + arrived.astype(F32)).astype(BF)
    part = gather_all(part, ("zl", "x", "y"), 32)
    grads = [((9 * CH, CH), F32)] * 2 + [((3 * CH, CH), F32)] * 2
    outs = []
    for owner, pieces in ((0, (0, 1, 2, 3)), (1, (0, 1)), (1, (2, 3))):
        piece = part[pieces[0] * 3 * CH : (pieces[-1] + 1) * 3 * CH]
        piece = swap_cores(piece) if owner else piece
        outs = call(
            functools.partial(spread_kernel, owner, pieces),
            grads,
            (pos, piece, *outs),
            [
                pltpu.VMEM((len(pieces) * 3 * CH, CH), F32),
                pltpu.SemaphoreType.DMA((len(pieces),)),
            ],
            0,
            (2, 3, 4, 5) if owner else (),
            (0, 1, 2, 3),
            {2: 0, 3: 1, 4: 2, 5: 3} if owner else None,
        )
    return (
        grad_input.reshape(video.shape),
        outs[0].reshape(w_spat1.shape),
        outs[1].reshape(w_spat2.shape),
        outs[2].reshape(w_time1.shape),
        outs[3].reshape(w_time2.shape),
    )


def solution(mesh):
    fine = Mesh(mesh.devices.reshape(4, 2, 4, 4, 2), ("zh", "zl", "x", "y", "core"))
    frames = P(("y", "core"), FRAME_AXES, None, None, None)
    return jax.shard_map(
        body,
        mesh=fine,
        in_specs=(frames, frames, P(), P(), P(), P()),
        out_specs=(frames, P(), P(), P(), P()),
        check_vma=False,
    )
```

```python
import functools
import math

import jax
import jax.numpy as jnp
from jax import lax
from jax.experimental import pallas as pl
from jax.experimental.pallas import tpu as pltpu
from jax.sharding import Mesh
from jax.sharding import PartitionSpec as P

CH = 256
COLS = 16
PIX = 512
HALF = PIX // 2
PAD = PIX + 2 * COLS
FRAME_AXES = ("zh", "zl", "x")
SCALE = 1.0 / math.sqrt(131072)
BF = jnp.bfloat16
F32 = jnp.float32
VMEM = pl.BlockSpec(memory_space=pltpu.VMEM)
SMEM = pl.BlockSpec(memory_space=pltpu.SMEM)
HBM = pl.BlockSpec(memory_space=pltpu.HBM)


def dot_nn(left, right):
    return lax.dot_general(left, right, (((1,), (0,)), ((), ())), preferred_element_type=F32)


def dot_nt(left, right):
    return lax.dot_general(left, right, (((1,), (1,)), ((), ())), preferred_element_type=F32)


def dot_tn(left, right):
    return lax.dot_general(left, right, (((0,), (0,)), ((), ())), preferred_element_type=F32)


def call(kernel, outs, ins, scratch=(), flops=0, hbm_in=(), hbm_out=(), aliases=None, vmem=40):
    specs = [SMEM if value.dtype == jnp.int32 else VMEM for value in ins]
    for at in hbm_in:
        specs[at] = HBM
    moved = sum(value.size * value.dtype.itemsize for value in ins)
    return pl.pallas_call(
        kernel,
        out_shape=[jax.ShapeDtypeStruct(shape, kind) for shape, kind in outs],
        in_specs=specs,
        out_specs=[HBM if at in hbm_out else VMEM for at in range(len(outs))],
        scratch_shapes=list(scratch),
        input_output_aliases=aliases or {},
        cost_estimate=pl.CostEstimate(flops=flops, bytes_accessed=moved, transcendentals=0),
        compiler_params=pltpu.CompilerParams(vmem_limit_bytes=vmem * 1024 * 1024),
    )(*ins)


def start_by_core(pos, sems, first, pairs):
    for at, (even, odd, target) in enumerate(pairs):

        @pl.when(pos[0] == 0)
        def _():
            pltpu.make_async_copy(even, target, sems.at[first + at]).start()

        @pl.when(pos[0] != 0)
        def _():
            pltpu.make_async_copy(odd, target, sems.at[first + at]).start()


def wait_by_core(sems, first, pairs):
    for at, (even, _, target) in enumerate(pairs):
        pltpu.make_async_copy(even, target, sems.at[first + at]).wait()


def fill_windows(wide, values):
    edge = jnp.zeros((COLS, 3 * CH), BF)
    wide[0:COLS, :] = edge
    wide[COLS + PIX : PAD, :] = edge
    column = lax.broadcasted_iota(jnp.int32, (PIX, CH), 0) & (COLS - 1)
    full = values.astype(F32)
    before = jnp.where(column == 0, 0.0, pltpu.roll(full, 1, 0))
    after = jnp.where(column == COLS - 1, 0.0, pltpu.roll(full, PIX - 1, 0))
    wide[COLS : COLS + PIX, 0:CH] = before.astype(BF)
    wide[COLS : COLS + PIX, CH : 2 * CH] = values.astype(BF)
    wide[COLS : COLS + PIX, 2 * CH : 3 * CH] = after.astype(BF)


def conv_half(wide, weight, half):
    total = None
    for tap in range(3):
        at = tap * COLS + half * HALF
        term = dot_nn(wide[at : at + HALF, :], weight[tap * 3 * CH : (tap + 1) * 3 * CH, :])
        total = term if total is None else total + term
    return total


def back_from(wide, weight):
    total = None
    for tap in range(3):
        for side in range(3):
            at = (tap * 3 + side) * CH
            term = dot_nt(
                wide[(2 - tap) * COLS : (2 - tap) * COLS + PIX, (2 - side) * CH : (3 - side) * CH],
                weight[at : at + CH, :],
            )
            total = term if total is None else total + term
    return total


def silu_pair(pre):
    sigma = 0.5 + 0.5 * jnp.tanh(0.5 * pre)
    act = pre * sigma
    return act, sigma * (1.0 + pre * (1.0 - sigma))


def forward_kernel(pos, video_at, cot_at, w1_at, w2_at, both_at, slopes_at, keep, send, *rest):
    video, first, both, slopes, w1, w2, wide, sems = rest
    pieces = [(video_at, video)]
    for source, target in ((w1_at, w1), (w2_at, w2)):
        for tap in range(3):
            part = pl.ds(tap * 3 * CH, 3 * CH)
            pieces.append((source.at[part], target.at[part]))
    pieces.append((cot_at, both.at[:, COLS : 2 * COLS, :]))
    pieces.append((slopes.at[0], slopes_at.at[0]))
    for half in range(2):
        part = pl.ds(half * HALF, HALF)
        pieces.append((slopes.at[1, part], slopes_at.at[1, part]))
        part = pl.ds(half * (HALF // COLS), HALF // COLS)
        pieces.append((both.at[part], both_at.at[part]))
    moves = [
        pltpu.make_async_copy(source, target, sems.at[at])
        for at, (source, target) in enumerate(pieces)
    ]
    for move in moves[0:8]:
        move.start()
    moves[0].wait()
    fill_windows(wide, video[...])
    for move in moves[1:4]:
        move.wait()
    for half in range(2):
        rows = slice(half * HALF, (half + 1) * HALF)
        act, slope = silu_pair(conv_half(wide, w1, half))
        first[rows, :] = act.astype(BF)
        slopes[0, rows, :] = slope.astype(BF)
    stores = [(first, video, keep), (video, first, send)]
    start_by_core(pos, sems, 13, stores)
    moves[8].start()
    fill_windows(wide, first[...])
    for move in moves[4:8]:
        move.wait()
    for half in range(2):
        rows = slice(half * HALF, (half + 1) * HALF)
        act, slope = silu_pair(conv_half(wide, w2, half))
        lines = HALF // COLS
        both[half * lines : (half + 1) * lines, 0:COLS, :] = act.astype(BF).reshape(lines, COLS, CH)
        slopes[1, rows, :] = slope.astype(BF)
    for move in moves[9:13]:
        move.start()
    for move in moves[8:13]:
        move.wait()
    wait_by_core(sems, 13, stores)


def ahead_sum(padded, weight, half):
    total = None
    for step in range(3):
        at = step * COLS + half * HALF
        term = dot_nt(padded[at : at + HALF, :], weight[step * CH : (step + 1) * CH, :])
        total = term if total is None else total + term
    return total


def time_kernel(pos, both_at, wt1_at, wt2_at, back_at, keep, send, *rest):
    act, cot, wt1, wt2, time_act, time_grad, act_back, behind, ahead, later, sems = rest
    loads = [
        pltpu.make_async_copy(source, target, sems.at[at])
        for at, (source, target) in enumerate(
            [
                (both_at.at[:, COLS : 2 * COLS, :], cot),
                (wt2_at, wt2),
                (both_at.at[:, 0:COLS, :], act),
                (wt1_at, wt1),
            ]
        )
    ]
    for load in loads:
        load.start()
    edge = jnp.zeros((2 * COLS, CH), BF)
    loads[0].wait()
    ahead[0:PIX, :] = cot[...].reshape(PIX, CH)
    ahead[PIX:PAD, :] = edge
    loads[2].wait()
    behind[0 : 2 * COLS, :] = edge
    behind[2 * COLS : PAD, :] = act[...].reshape(PIX, CH)
    loads[1].wait()
    loads[3].wait()
    for half in range(2):
        pre = None
        for step in range(3):
            at = (2 - step) * COLS + half * HALF
            term = dot_nn(behind[at : at + HALF, :], wt1[step * CH : (step + 1) * CH, :])
            pre = term if pre is None else pre + term
        value, slope = silu_pair(pre)
        grad = (ahead_sum(ahead, wt2, half) * slope).astype(BF)
        lines = slice(half * (HALF // COLS), (half + 1) * (HALF // COLS))
        time_act[lines] = value.astype(BF).reshape(HALF // COLS, COLS, CH)
        time_grad[lines] = grad.reshape(HALF // COLS, COLS, CH)
        later[half * HALF : (half + 1) * HALF, :] = grad
    later[PIX:PAD, :] = edge
    stores = [
        (act, time_act, keep.at[0]),
        (time_grad, cot, keep.at[1]),
        (time_act, act, send.at[0]),
        (cot, time_grad, send.at[1]),
    ]
    start_by_core(pos, sems, 4, stores)
    tails = []
    for half in range(2):
        rows = pl.ds(half * HALF, HALF)
        act_back[rows, :] = ahead_sum(later, wt1, half).astype(BF)
        tails.append(pltpu.make_async_copy(act_back.at[rows], back_at.at[rows], sems.at[8 + half]))
        tails[half].start()
    wait_by_core(sems, 4, stores)
    for tail in tails:
        tail.wait()


def time_weights_kernel(keep, recv, out):
    for step in range(3):
        rows = PIX - step * COLS
        total = dot_tn(keep[0, 0:rows, :], keep[1, step * COLS : PIX, :])
        total = total + dot_tn(recv[0, 0:rows, :], recv[1, step * COLS : PIX, :])
        out[step * CH : (step + 1) * CH, :] = (total * SCALE).astype(BF)


def backward_kernel(pos, act_back, slopes, w2, first_grad, keep, send, wide):
    second = (act_back[...].astype(F32) * slopes[1].astype(F32)).astype(BF)
    fill_windows(wide, second)
    first = (back_from(wide, w2) * slopes[0].astype(F32)).astype(BF)
    first_grad[...] = first

    @pl.when(pos[0] == 0)
    def _():
        keep[...] = second
        send[...] = first

    @pl.when(pos[0] != 0)
    def _():
        keep[...] = first
        send[...] = second


def own_weights_kernel(keep_x, keep_g, out, wide):
    fill_windows(wide, keep_x[...])
    for tap in range(3):
        for side in range(3):
            rows = slice(tap * COLS, tap * COLS + PIX)
            lanes = slice(side * CH, (side + 1) * CH)
            at = (tap * 3 + side) * CH
            out[at : at + CH, :] = dot_tn(wide[rows, lanes], keep_g[...])


def space_weights_kernel(partial, recv_x, recv_g, time_part, out, wide):
    fill_windows(wide, recv_x[...])
    for tap in range(3):
        for side in range(3):
            rows = slice(tap * COLS, tap * COLS + PIX)
            lanes = slice(side * CH, (side + 1) * CH)
            at = (tap * 3 + side) * CH
            total = partial[at : at + CH, :] + dot_tn(wide[rows, lanes], recv_g[...])
            out[at : at + CH, :] = (total * SCALE).astype(BF)
    out[9 * CH : 12 * CH, :] = time_part[...]


def spread_kernel(owner, pieces, pos, half, *refs):
    spat1, spat2, time1, time2, stage, sems = refs[-6:]
    targets = [(spat2, time1), (spat1, time2)]
    rows = 3 * CH

    def copies(at):
        space, time = targets[at]
        for slot, piece in enumerate(pieces):
            target = space.at[pl.ds(piece * rows, rows)] if piece < 3 else time
            source = stage.at[pl.ds(slot * rows, rows)]
            yield pltpu.make_async_copy(source, target, sems.at[slot])

    for at in range(2):

        @pl.when((pos[0] ^ owner) == at)
        def _():
            for slot, copy in enumerate(copies(at)):
                part = slice(slot * rows, (slot + 1) * rows)
                stage[part, :] = half[part, :].astype(F32)
                copy.start()
            for copy in copies(at):
                copy.wait()


def input_kernel(first_grad, w1, out, wide):
    fill_windows(wide, first_grad[...])
    out[...] = back_from(wide, w1).astype(BF)


def swap_cores(values):
    return lax.ppermute(values, "core", [(0, 1), (1, 0)])


def swap_frames(values):
    blocks = values.reshape(PIX // COLS, COLS, CH)
    return lax.all_to_all(blocks, FRAME_AXES, 0, 0, tiled=True).reshape(PIX, CH)


def scatter_sum(values, axes, count):
    parts = values.reshape(count, -1, CH)
    arrived = lax.all_to_all(parts, axes, 0, 0, tiled=True)
    return jnp.sum(arrived.astype(F32), axis=0).astype(BF)


def gather_all(values, axes, count):
    copies = jnp.broadcast_to(values[None], (count,) + values.shape)
    return lax.all_to_all(copies, axes, 0, 0, tiled=True).reshape(-1, CH)


def body(video, cotangent, w_spat1, w_spat2, w_time1, w_time2):
    pos = lax.axis_index("core").astype(jnp.int32).reshape(1)
    w1, w2, wt1, wt2 = (w.reshape(-1, CH) for w in (w_spat1, w_spat2, w_time1, w_time2))
    rows = PIX // COLS
    slab = ((PIX, CH), BF)
    pair = ((2, rows, COLS, CH), BF)
    wide, tall = pltpu.VMEM((PAD, 3 * CH), BF), pltpu.VMEM((PAD, CH), BF)
    frame, lines = pltpu.VMEM((PIX, CH), BF), pltpu.VMEM((rows, COLS, CH), BF)
    both_slopes = pltpu.VMEM((2, PIX, CH), BF)
    space, time = pltpu.VMEM((9 * CH, CH), BF), pltpu.VMEM((3 * CH, CH), BF)
    conv_flops, time_flops = 2 * PIX * 9 * CH * CH, 2 * PIX * 3 * CH * CH

    both, slopes, keep_x, send_x = call(
        forward_kernel,
        [((rows, 2 * COLS, CH), BF), ((2, PIX, CH), BF), slab, slab],
        (pos, video.reshape(PIX, CH), cotangent.reshape(rows, COLS, CH), w1, w2),
        [frame, frame, pltpu.VMEM((rows, 2 * COLS, CH), BF), both_slopes, space, space, wide, pltpu.SemaphoreType.DMA((15,))],
        2 * conv_flops,
        (1, 2, 3, 4),
        (0, 1, 2, 3),
        vmem=60,
    )
    both = lax.all_to_all(both, FRAME_AXES, 0, 0, tiled=True)
    act_back, keep_t, send_t = call(
        time_kernel,
        [slab, pair, pair],
        (pos, both, wt1, wt2),
        [lines, lines, time, time, lines, lines, frame, tall, tall, tall, pltpu.SemaphoreType.DMA((10,))],
        3 * time_flops,
        (1, 2, 3),
        (0, 1, 2),
        vmem=60,
    )
    act_back = swap_frames(act_back)
    act_back, send_t, send_x = lax.optimization_barrier((act_back, send_t, send_x))
    recv_t, recv_x = swap_cores(send_t), swap_cores(send_x)
    keep_t, recv_t = keep_t.reshape(2, PIX, CH), recv_t.reshape(2, PIX, CH)
    (time_part,) = call(
        time_weights_kernel, [((3 * CH, CH), BF)], (keep_t, recv_t), (), 2 * time_flops
    )
    first_grad, keep_g, send_g = call(
        backward_kernel, [slab, slab, slab], (pos, act_back, slopes, w2), [wide], conv_flops
    )
    recv_g = swap_cores(send_g)
    (partial,) = call(
        own_weights_kernel, [((9 * CH, CH), F32)], (keep_x, keep_g), [wide], conv_flops
    )
    (part,) = call(
        space_weights_kernel,
        [((12 * CH, CH), BF)],
        (partial, recv_x, recv_g, time_part),
        [wide],
        conv_flops,
    )

    part = scatter_sum(part, ("zl", "x", "y"), 32)
    part, first_grad = lax.optimization_barrier((part, first_grad))
    (grad_input,) = call(input_kernel, [slab], (first_grad, w1), [wide], conv_flops)
    for pairs in (((0, 1), (1, 0), (2, 3), (3, 2)), ((0, 3), (3, 0), (1, 2), (2, 1))):
        arrived = lax.ppermute(part, "zh", pairs)
        arrived, grad_input = lax.optimization_barrier((arrived, grad_input))
        part = (part.astype(F32) + arrived.astype(F32)).astype(BF)
    part = gather_all(part, ("zl", "x", "y"), 32)
    grads = [((9 * CH, CH), F32)] * 2 + [((3 * CH, CH), F32)] * 2
    outs = []
    for owner, pieces in ((0, (0, 1, 2, 3)), (1, (0, 1)), (1, (2, 3))):
        piece = part[pieces[0] * 3 * CH : (pieces[-1] + 1) * 3 * CH]
        piece = swap_cores(piece) if owner else piece
        outs = call(
            functools.partial(spread_kernel, owner, pieces),
            grads,
            (pos, piece, *outs),
            [
                pltpu.VMEM((len(pieces) * 3 * CH, CH), F32),
                pltpu.SemaphoreType.DMA((len(pieces),)),
            ],
            0,
            (2, 3, 4, 5) if owner else (),
            (0, 1, 2, 3),
            {2: 0, 3: 1, 4: 2, 5: 3} if owner else None,
        )
    return (
        grad_input.reshape(video.shape),
        outs[0].reshape(w_spat1.shape),
        outs[1].reshape(w_spat2.shape),
        outs[2].reshape(w_time1.shape),
        outs[3].reshape(w_time2.shape),
    )


def solution(mesh):
    fine = Mesh(mesh.devices.reshape(4, 2, 4, 4, 2), ("zh", "zl", "x", "y", "core"))
    frames = P(("y", "core"), FRAME_AXES, None, None, None)
    return jax.shard_map(
        body,
        mesh=fine,
        in_specs=(frames, frames, P(), P(), P(), P()),
        out_specs=(frames, P(), P(), P(), P()),
        check_vma=False,
    )
```

```python
import functools
import math

import jax
import jax.numpy as jnp
from jax import lax
from jax.experimental import pallas as pl
from jax.experimental.pallas import tpu as pltpu
from jax.sharding import Mesh
from jax.sharding import PartitionSpec as P

CH = 256
COLS = 16
PIX = 512
HALF = PIX // 2
PAD = PIX + 2 * COLS
FRAME_AXES = ("zh", "zl", "x")
SCALE = 1.0 / math.sqrt(131072)
BF = jnp.bfloat16
F32 = jnp.float32
VMEM = pl.BlockSpec(memory_space=pltpu.VMEM)
SMEM = pl.BlockSpec(memory_space=pltpu.SMEM)
HBM = pl.BlockSpec(memory_space=pltpu.HBM)


def dot_nn(left, right):
    return lax.dot_general(left, right, (((1,), (0,)), ((), ())), preferred_element_type=F32)


def dot_nt(left, right):
    return lax.dot_general(left, right, (((1,), (1,)), ((), ())), preferred_element_type=F32)


def dot_tn(left, right):
    return lax.dot_general(left, right, (((0,), (0,)), ((), ())), preferred_element_type=F32)


def call(kernel, outs, ins, scratch=(), flops=0, hbm_in=(), hbm_out=(), aliases=None, vmem=40):
    specs = [SMEM if value.dtype == jnp.int32 else VMEM for value in ins]
    for at in hbm_in:
        specs[at] = HBM
    moved = sum(value.size * value.dtype.itemsize for value in ins)
    return pl.pallas_call(
        kernel,
        out_shape=[jax.ShapeDtypeStruct(shape, kind) for shape, kind in outs],
        in_specs=specs,
        out_specs=[HBM if at in hbm_out else VMEM for at in range(len(outs))],
        scratch_shapes=list(scratch),
        input_output_aliases=aliases or {},
        cost_estimate=pl.CostEstimate(flops=flops, bytes_accessed=moved, transcendentals=0),
        compiler_params=pltpu.CompilerParams(vmem_limit_bytes=vmem * 1024 * 1024),
    )(*ins)


def start_by_core(pos, sems, first, pairs):
    for at, (even, odd, target) in enumerate(pairs):

        @pl.when(pos[0] == 0)
        def _():
            pltpu.make_async_copy(even, target, sems.at[first + at]).start()

        @pl.when(pos[0] != 0)
        def _():
            pltpu.make_async_copy(odd, target, sems.at[first + at]).start()


def wait_by_core(sems, first, pairs):
    for at, (even, _, target) in enumerate(pairs):
        pltpu.make_async_copy(even, target, sems.at[first + at]).wait()


def fill_windows(wide, values):
    edge = jnp.zeros((COLS, 3 * CH), BF)
    wide[0:COLS, :] = edge
    wide[COLS + PIX : PAD, :] = edge
    column = lax.broadcasted_iota(jnp.int32, (PIX, CH), 0) & (COLS - 1)
    full = values.astype(F32)
    before = jnp.where(column == 0, 0.0, pltpu.roll(full, 1, 0))
    after = jnp.where(column == COLS - 1, 0.0, pltpu.roll(full, PIX - 1, 0))
    wide[COLS : COLS + PIX, 0:CH] = before.astype(BF)
    wide[COLS : COLS + PIX, CH : 2 * CH] = values.astype(BF)
    wide[COLS : COLS + PIX, 2 * CH : 3 * CH] = after.astype(BF)


def conv_half(wide, weight, half):
    total = None
    for tap in range(3):
        at = tap * COLS + half * HALF
        term = dot_nn(wide[at : at + HALF, :], weight[tap * 3 * CH : (tap + 1) * 3 * CH, :])
        total = term if total is None else total + term
    return total


def back_from(wide, weight):
    total = None
    for tap in range(3):
        for side in range(3):
            at = (tap * 3 + side) * CH
            term = dot_nt(
                wide[(2 - tap) * COLS : (2 - tap) * COLS + PIX, (2 - side) * CH : (3 - side) * CH],
                weight[at : at + CH, :],
            )
            total = term if total is None else total + term
    return total


def silu_pair(pre):
    sigma = 0.5 + 0.5 * jnp.tanh(0.5 * pre)
    act = pre * sigma
    return act, sigma * (1.0 + pre * (1.0 - sigma))


def forward_kernel(pos, video_at, cot_at, w1_at, w2_at, both_at, slopes_at, keep, send, *rest):
    video, first, both, slopes, w1, w2, wide, sems = rest
    pieces = [(video_at, video)]
    for source, target in ((w1_at, w1), (w2_at, w2)):
        for tap in range(3):
            part = pl.ds(tap * 3 * CH, 3 * CH)
            pieces.append((source.at[part], target.at[part]))
    pieces.append((cot_at, both.at[:, COLS : 2 * COLS, :]))
    pieces.append((slopes.at[0], slopes_at.at[0]))
    for half in range(2):
        part = pl.ds(half * HALF, HALF)
        pieces.append((slopes.at[1, part], slopes_at.at[1, part]))
        part = pl.ds(half * (HALF // COLS), HALF // COLS)
        pieces.append((both.at[part], both_at.at[part]))
    moves = [
        pltpu.make_async_copy(source, target, sems.at[at])
        for at, (source, target) in enumerate(pieces)
    ]
    for move in moves[0:8]:
        move.start()
    moves[0].wait()
    fill_windows(wide, video[...])
    for move in moves[1:4]:
        move.wait()
    for half in range(2):
        rows = slice(half * HALF, (half + 1) * HALF)
        act, slope = silu_pair(conv_half(wide, w1, half))
        first[rows, :] = act.astype(BF)
        slopes[0, rows, :] = slope.astype(BF)
    stores = [(first, video, keep), (video, first, send)]
    start_by_core(pos, sems, 13, stores)
    moves[8].start()
    fill_windows(wide, first[...])
    for move in moves[4:8]:
        move.wait()
    for half in range(2):
        rows = slice(half * HALF, (half + 1) * HALF)
        act, slope = silu_pair(conv_half(wide, w2, half))
        lines = HALF // COLS
        both[half * lines : (half + 1) * lines, 0:COLS, :] = act.astype(BF).reshape(lines, COLS, CH)
        slopes[1, rows, :] = slope.astype(BF)
    for move in moves[9:13]:
        move.start()
    for move in moves[8:13]:
        move.wait()
    wait_by_core(sems, 13, stores)


def ahead_sum(padded, weight, half):
    total = None
    for step in range(3):
        at = step * COLS + half * HALF
        term = dot_nt(padded[at : at + HALF, :], weight[step * CH : (step + 1) * CH, :])
        total = term if total is None else total + term
    return total


def time_kernel(both_at, wt1_at, wt2_at, back_at, own_at, *rest):
    act, cot, wt1, wt2, time_act, time_grad, act_back, behind, ahead, later, sems = rest
    loads = [
        pltpu.make_async_copy(source, target, sems.at[at])
        for at, (source, target) in enumerate(
            [
                (both_at.at[:, COLS : 2 * COLS, :], cot),
                (wt2_at, wt2),
                (both_at.at[:, 0:COLS, :], act),
                (wt1_at, wt1),
            ]
        )
    ]
    for load in loads:
        load.start()
    edge = jnp.zeros((2 * COLS, CH), BF)
    loads[0].wait()
    ahead[0:PIX, :] = cot[...].reshape(PIX, CH)
    ahead[PIX:PAD, :] = edge
    loads[2].wait()
    behind[0 : 2 * COLS, :] = edge
    behind[2 * COLS : PAD, :] = act[...].reshape(PIX, CH)
    loads[1].wait()
    loads[3].wait()
    for half in range(2):
        pre = None
        for step in range(3):
            at = (2 - step) * COLS + half * HALF
            term = dot_nn(behind[at : at + HALF, :], wt1[step * CH : (step + 1) * CH, :])
            pre = term if pre is None else pre + term
        value, slope = silu_pair(pre)
        grad = (ahead_sum(ahead, wt2, half) * slope).astype(BF)
        lines = slice(half * (HALF // COLS), (half + 1) * (HALF // COLS))
        time_act[lines] = value.astype(BF).reshape(HALF // COLS, COLS, CH)
        time_grad[lines] = grad.reshape(HALF // COLS, COLS, CH)
        later[half * HALF : (half + 1) * HALF, :] = grad
    later[PIX:PAD, :] = edge
    stores = [
        pltpu.make_async_copy(source, own_at.at[at], sems.at[4 + at])
        for at, source in enumerate((act, time_grad, time_act, cot))
    ]
    for store in stores:
        store.start()
    tails = []
    for half in range(2):
        rows = pl.ds(half * HALF, HALF)
        act_back[rows, :] = ahead_sum(later, wt1, half).astype(BF)
        tails.append(pltpu.make_async_copy(act_back.at[rows], back_at.at[rows], sems.at[8 + half]))
        tails[half].start()
    for move in stores + tails:
        move.wait()


def time_weights_kernel(pos, own, keep, send):
    for step in range(3):
        rows = PIX - step * COLS
        first = dot_tn(own[0, 0:rows, :], own[1, step * COLS : PIX, :]) * SCALE
        second = dot_tn(own[2, 0:rows, :], own[3, step * COLS : PIX, :]) * SCALE
        part = slice(step * CH, (step + 1) * CH)
        keep[part, :] = jnp.where(pos[0] == 0, first, second).astype(BF)
        send[part, :] = jnp.where(pos[0] == 0, second, first).astype(BF)


def backward_kernel(pos, act_back, slopes, w2, first_grad, keep, send, wide):
    second = (act_back[...].astype(F32) * slopes[1].astype(F32)).astype(BF)
    fill_windows(wide, second)
    first = (back_from(wide, w2) * slopes[0].astype(F32)).astype(BF)
    first_grad[...] = first

    @pl.when(pos[0] == 0)
    def _():
        keep[...] = second
        send[...] = first

    @pl.when(pos[0] != 0)
    def _():
        keep[...] = first
        send[...] = second


def own_weights_kernel(keep_x, keep_g, out, wide):
    fill_windows(wide, keep_x[...])
    for tap in range(3):
        for side in range(3):
            rows = slice(tap * COLS, tap * COLS + PIX)
            lanes = slice(side * CH, (side + 1) * CH)
            at = (tap * 3 + side) * CH
            out[at : at + CH, :] = dot_tn(wide[rows, lanes], keep_g[...])


def space_weights_kernel(partial, recv_x, recv_g, keep_t, recv_t, out, wide):
    fill_windows(wide, recv_x[...])
    for tap in range(3):
        for side in range(3):
            rows = slice(tap * COLS, tap * COLS + PIX)
            lanes = slice(side * CH, (side + 1) * CH)
            at = (tap * 3 + side) * CH
            total = partial[at : at + CH, :] + dot_tn(wide[rows, lanes], recv_g[...])
            out[at : at + CH, :] = (total * SCALE).astype(BF)
    out[9 * CH : 12 * CH, :] = (keep_t[...].astype(F32) + recv_t[...].astype(F32)).astype(BF)


def spread_kernel(owner, pieces, pos, half, *refs):
    spat1, spat2, time1, time2, stage, sems = refs[-6:]
    targets = [(spat2, time1), (spat1, time2)]
    rows = 3 * CH

    def copies(at):
        space, time = targets[at]
        for slot, piece in enumerate(pieces):
            target = space.at[pl.ds(piece * rows, rows)] if piece < 3 else time
            source = stage.at[pl.ds(slot * rows, rows)]
            yield pltpu.make_async_copy(source, target, sems.at[slot])

    for at in range(2):

        @pl.when((pos[0] ^ owner) == at)
        def _():
            for slot, copy in enumerate(copies(at)):
                part = slice(slot * rows, (slot + 1) * rows)
                stage[part, :] = half[part, :].astype(F32)
                copy.start()
            for copy in copies(at):
                copy.wait()


def input_kernel(first_grad, w1, out, wide):
    fill_windows(wide, first_grad[...])
    out[...] = back_from(wide, w1).astype(BF)


def swap_cores(values):
    return lax.ppermute(values, "core", [(0, 1), (1, 0)])


def swap_frames(values):
    blocks = values.reshape(PIX // COLS, COLS, CH)
    return lax.all_to_all(blocks, FRAME_AXES, 0, 0, tiled=True).reshape(PIX, CH)


def scatter_sum(values, axes, count):
    parts = values.reshape(count, -1, CH)
    arrived = lax.all_to_all(parts, axes, 0, 0, tiled=True)
    return jnp.sum(arrived.astype(F32), axis=0).astype(BF)


def gather_all(values, axes, count):
    copies = jnp.broadcast_to(values[None], (count,) + values.shape)
    return lax.all_to_all(copies, axes, 0, 0, tiled=True).reshape(-1, CH)


def body(video, cotangent, w_spat1, w_spat2, w_time1, w_time2):
    pos = lax.axis_index("core").astype(jnp.int32).reshape(1)
    w1, w2, wt1, wt2 = (w.reshape(-1, CH) for w in (w_spat1, w_spat2, w_time1, w_time2))
    rows = PIX // COLS
    slab = ((PIX, CH), BF)
    wide, tall = pltpu.VMEM((PAD, 3 * CH), BF), pltpu.VMEM((PAD, CH), BF)
    frame, lines = pltpu.VMEM((PIX, CH), BF), pltpu.VMEM((rows, COLS, CH), BF)
    both_slopes = pltpu.VMEM((2, PIX, CH), BF)
    space, time = pltpu.VMEM((9 * CH, CH), BF), pltpu.VMEM((3 * CH, CH), BF)
    conv_flops, time_flops = 2 * PIX * 9 * CH * CH, 2 * PIX * 3 * CH * CH

    both, slopes, keep_x, send_x = call(
        forward_kernel,
        [((rows, 2 * COLS, CH), BF), ((2, PIX, CH), BF), slab, slab],
        (pos, video.reshape(PIX, CH), cotangent.reshape(rows, COLS, CH), w1, w2),
        [frame, frame, pltpu.VMEM((rows, 2 * COLS, CH), BF), both_slopes, space, space, wide, pltpu.SemaphoreType.DMA((15,))],
        2 * conv_flops,
        (1, 2, 3, 4),
        (0, 1, 2, 3),
        vmem=60,
    )
    both = lax.all_to_all(both, FRAME_AXES, 0, 0, tiled=True)
    recv_x = swap_cores(send_x)
    act_back, own = call(
        time_kernel,
        [slab, ((4, rows, COLS, CH), BF)],
        (both, wt1, wt2),
        [lines, lines, time, time, lines, lines, frame, tall, tall, tall, pltpu.SemaphoreType.DMA((10,))],
        3 * time_flops,
        (0, 1, 2),
        (0, 1),
        vmem=60,
    )
    act_back = swap_frames(act_back)
    taps = ((3 * CH, CH), BF)
    keep_t, send_t = call(
        time_weights_kernel, [taps, taps], (pos, own.reshape(4, PIX, CH)), (), 2 * time_flops
    )
    act_back, send_t = lax.optimization_barrier((act_back, send_t))
    recv_t = swap_cores(send_t)
    first_grad, keep_g, send_g = call(
        backward_kernel, [slab, slab, slab], (pos, act_back, slopes, w2), [wide], conv_flops
    )
    recv_g = swap_cores(send_g)
    (partial,) = call(
        own_weights_kernel, [((9 * CH, CH), F32)], (keep_x, keep_g), [wide], conv_flops
    )
    (part,) = call(
        space_weights_kernel,
        [((12 * CH, CH), BF)],
        (partial, recv_x, recv_g, keep_t, recv_t),
        [wide],
        conv_flops,
    )

    part = scatter_sum(part, ("zl", "x", "y"), 32)
    part, first_grad = lax.optimization_barrier((part, first_grad))
    (grad_input,) = call(input_kernel, [slab], (first_grad, w1), [wide], conv_flops)
    for pairs in (((0, 1), (1, 0), (2, 3), (3, 2)), ((0, 3), (3, 0), (1, 2), (2, 1))):
        arrived = lax.ppermute(part, "zh", pairs)
        arrived, grad_input = lax.optimization_barrier((arrived, grad_input))
        part = (part.astype(F32) + arrived.astype(F32)).astype(BF)
    part = gather_all(part, ("zl", "x", "y"), 32)
    grads = [((9 * CH, CH), F32)] * 2 + [((3 * CH, CH), F32)] * 2
    outs = []
    for owner, pieces in ((0, (0, 1, 2, 3)), (1, (0, 1)), (1, (2, 3))):
        piece = part[pieces[0] * 3 * CH : (pieces[-1] + 1) * 3 * CH]
        piece = swap_cores(piece) if owner else piece
        outs = call(
            functools.partial(spread_kernel, owner, pieces),
            grads,
            (pos, piece, *outs),
            [
                pltpu.VMEM((len(pieces) * 3 * CH, CH), F32),
                pltpu.SemaphoreType.DMA((len(pieces),)),
            ],
            0,
            (2, 3, 4, 5) if owner else (),
            (0, 1, 2, 3),
            {2: 0, 3: 1, 4: 2, 5: 3} if owner else None,
        )
    return (
        grad_input.reshape(video.shape),
        outs[0].reshape(w_spat1.shape),
        outs[1].reshape(w_spat2.shape),
        outs[2].reshape(w_time1.shape),
        outs[3].reshape(w_time2.shape),
    )


def solution(mesh):
    fine = Mesh(mesh.devices.reshape(4, 2, 4, 4, 2), ("zh", "zl", "x", "y", "core"))
    frames = P(("y", "core"), FRAME_AXES, None, None, None)
    return jax.shard_map(
        body,
        mesh=fine,
        in_specs=(frames, frames, P(), P(), P(), P()),
        out_specs=(frames, P(), P(), P(), P()),
        check_vma=False,
    )
```

```python
import functools
import math

import jax
import jax.numpy as jnp
from jax import lax
from jax.experimental import pallas as pl
from jax.experimental.pallas import tpu as pltpu
from jax.sharding import Mesh
from jax.sharding import PartitionSpec as P

CH = 256
COLS = 16
PIX = 512
HALF = PIX // 2
PAD = PIX + 2 * COLS
FRAME_AXES = ("zh", "zl", "x")
SCALE = 1.0 / math.sqrt(131072)
BF = jnp.bfloat16
F32 = jnp.float32
VMEM = pl.BlockSpec(memory_space=pltpu.VMEM)
SMEM = pl.BlockSpec(memory_space=pltpu.SMEM)
HBM = pl.BlockSpec(memory_space=pltpu.HBM)


def dot_nn(left, right):
    return lax.dot_general(left, right, (((1,), (0,)), ((), ())), preferred_element_type=F32)


def dot_nt(left, right):
    return lax.dot_general(left, right, (((1,), (1,)), ((), ())), preferred_element_type=F32)


def dot_tn(left, right):
    return lax.dot_general(left, right, (((0,), (0,)), ((), ())), preferred_element_type=F32)


def call(kernel, outs, ins, scratch=(), flops=0, hbm_in=(), hbm_out=(), aliases=None, vmem=40):
    specs = [SMEM if value.dtype == jnp.int32 else VMEM for value in ins]
    for at in hbm_in:
        specs[at] = HBM
    moved = sum(value.size * value.dtype.itemsize for value in ins)
    return pl.pallas_call(
        kernel,
        out_shape=[jax.ShapeDtypeStruct(shape, kind) for shape, kind in outs],
        in_specs=specs,
        out_specs=[HBM if at in hbm_out else VMEM for at in range(len(outs))],
        scratch_shapes=list(scratch),
        input_output_aliases=aliases or {},
        cost_estimate=pl.CostEstimate(flops=flops, bytes_accessed=moved, transcendentals=0),
        compiler_params=pltpu.CompilerParams(vmem_limit_bytes=vmem * 1024 * 1024),
    )(*ins)


def start_by_core(pos, sems, first, pairs):
    for at, (even, odd, target) in enumerate(pairs):

        @pl.when(pos[0] == 0)
        def _():
            pltpu.make_async_copy(even, target, sems.at[first + at]).start()

        @pl.when(pos[0] != 0)
        def _():
            pltpu.make_async_copy(odd, target, sems.at[first + at]).start()


def wait_by_core(sems, first, pairs):
    for at, (even, _, target) in enumerate(pairs):
        pltpu.make_async_copy(even, target, sems.at[first + at]).wait()


def fill_windows(wide, values):
    edge = jnp.zeros((COLS, 3 * CH), BF)
    wide[0:COLS, :] = edge
    wide[COLS + PIX : PAD, :] = edge
    column = lax.broadcasted_iota(jnp.int32, (PIX, CH), 0) & (COLS - 1)
    full = values.astype(F32)
    before = jnp.where(column == 0, 0.0, pltpu.roll(full, 1, 0))
    after = jnp.where(column == COLS - 1, 0.0, pltpu.roll(full, PIX - 1, 0))
    wide[COLS : COLS + PIX, 0:CH] = before.astype(BF)
    wide[COLS : COLS + PIX, CH : 2 * CH] = values.astype(BF)
    wide[COLS : COLS + PIX, 2 * CH : 3 * CH] = after.astype(BF)


def conv_half(wide, weight, half):
    total = None
    for tap in range(3):
        at = tap * COLS + half * HALF
        term = dot_nn(wide[at : at + HALF, :], weight[tap * 3 * CH : (tap + 1) * 3 * CH, :])
        total = term if total is None else total + term
    return total


def back_from(wide, weight):
    total = None
    for tap in range(3):
        for side in range(3):
            at = (tap * 3 + side) * CH
            term = dot_nt(
                wide[(2 - tap) * COLS : (2 - tap) * COLS + PIX, (2 - side) * CH : (3 - side) * CH],
                weight[at : at + CH, :],
            )
            total = term if total is None else total + term
    return total


def silu_pair(pre):
    sigma = 0.5 + 0.5 * jnp.tanh(0.5 * pre)
    act = pre * sigma
    return act, sigma * (1.0 + pre * (1.0 - sigma))


def forward_kernel(pos, video_at, cot_at, w1_at, w2_at, both_at, slopes_at, keep, send, *rest):
    video, first, both, slopes, w1, w2, wide, sems = rest
    pieces = [(video_at, video)]
    for source, target in ((w1_at, w1), (w2_at, w2)):
        for tap in range(3):
            part = pl.ds(tap * 3 * CH, 3 * CH)
            pieces.append((source.at[part], target.at[part]))
    pieces.append((cot_at, both.at[:, COLS : 2 * COLS, :]))
    pieces.append((slopes.at[0], slopes_at.at[0]))
    for half in range(2):
        part = pl.ds(half * HALF, HALF)
        pieces.append((slopes.at[1, part], slopes_at.at[1, part]))
        part = pl.ds(half * (HALF // COLS), HALF // COLS)
        pieces.append((both.at[part], both_at.at[part]))
    moves = [
        pltpu.make_async_copy(source, target, sems.at[at])
        for at, (source, target) in enumerate(pieces)
    ]
    for move in moves[0:8]:
        move.start()
    moves[0].wait()
    fill_windows(wide, video[...])
    for move in moves[1:4]:
        move.wait()
    for half in range(2):
        rows = slice(half * HALF, (half + 1) * HALF)
        act, slope = silu_pair(conv_half(wide, w1, half))
        first[rows, :] = act.astype(BF)
        slopes[0, rows, :] = slope.astype(BF)
    stores = [(first, video, keep), (video, first, send)]
    start_by_core(pos, sems, 13, stores)
    moves[8].start()
    fill_windows(wide, first[...])
    for move in moves[4:8]:
        move.wait()
    for half in range(2):
        rows = slice(half * HALF, (half + 1) * HALF)
        act, slope = silu_pair(conv_half(wide, w2, half))
        lines = HALF // COLS
        both[half * lines : (half + 1) * lines, 0:COLS, :] = act.astype(BF).reshape(lines, COLS, CH)
        slopes[1, rows, :] = slope.astype(BF)
    for move in moves[9:13]:
        move.start()
    for move in moves[8:13]:
        move.wait()
    wait_by_core(sems, 13, stores)


def ahead_sum(padded, weight, half):
    total = None
    for step in range(3):
        at = step * COLS + half * HALF
        term = dot_nt(padded[at : at + HALF, :], weight[step * CH : (step + 1) * CH, :])
        total = term if total is None else total + term
    return total


def time_kernel(both_at, wt1_at, wt2_at, back_at, own_at, *rest):
    act, cot, wt1, wt2, time_act, time_grad, act_back, behind, ahead, later, sems = rest
    loads = [
        pltpu.make_async_copy(source, target, sems.at[at])
        for at, (source, target) in enumerate(
            [
                (both_at.at[:, COLS : 2 * COLS, :], cot),
                (wt2_at, wt2),
                (both_at.at[:, 0:COLS, :], act),
                (wt1_at, wt1),
            ]
        )
    ]
    for load in loads:
        load.start()
    edge = jnp.zeros((2 * COLS, CH), BF)
    loads[0].wait()
    ahead[0:PIX, :] = cot[...].reshape(PIX, CH)
    ahead[PIX:PAD, :] = edge
    loads[2].wait()
    behind[0 : 2 * COLS, :] = edge
    behind[2 * COLS : PAD, :] = act[...].reshape(PIX, CH)
    loads[1].wait()
    loads[3].wait()
    for half in range(2):
        pre = None
        for step in range(3):
            at = (2 - step) * COLS + half * HALF
            term = dot_nn(behind[at : at + HALF, :], wt1[step * CH : (step + 1) * CH, :])
            pre = term if pre is None else pre + term
        value, slope = silu_pair(pre)
        grad = (ahead_sum(ahead, wt2, half) * slope).astype(BF)
        lines = slice(half * (HALF // COLS), (half + 1) * (HALF // COLS))
        time_act[lines] = value.astype(BF).reshape(HALF // COLS, COLS, CH)
        time_grad[lines] = grad.reshape(HALF // COLS, COLS, CH)
        later[half * HALF : (half + 1) * HALF, :] = grad
    later[PIX:PAD, :] = edge
    stores = [
        pltpu.make_async_copy(source, own_at.at[at], sems.at[4 + at])
        for at, source in enumerate((act, time_grad, time_act, cot))
    ]
    for store in stores:
        store.start()
    tails = []
    for half in range(2):
        rows = pl.ds(half * HALF, HALF)
        act_back[rows, :] = ahead_sum(later, wt1, half).astype(BF)
        tails.append(pltpu.make_async_copy(act_back.at[rows], back_at.at[rows], sems.at[8 + half]))
        tails[half].start()
    for move in stores + tails:
        move.wait()


def time_weights_kernel(pos, own, keep, send):
    for step in range(3):
        rows = PIX - step * COLS
        first = dot_tn(own[0, 0:rows, :], own[1, step * COLS : PIX, :]) * SCALE
        second = dot_tn(own[2, 0:rows, :], own[3, step * COLS : PIX, :]) * SCALE
        part = slice(step * CH, (step + 1) * CH)
        keep[part, :] = jnp.where(pos[0] == 0, first, second).astype(BF)
        send[part, :] = jnp.where(pos[0] == 0, second, first).astype(BF)


def backward_kernel(pos, act_back, slopes, w2, first_grad, keep, send, wide):
    second = (act_back[...].astype(F32) * slopes[1].astype(F32)).astype(BF)
    fill_windows(wide, second)
    first = (back_from(wide, w2) * slopes[0].astype(F32)).astype(BF)
    first_grad[...] = first

    @pl.when(pos[0] == 0)
    def _():
        keep[...] = second
        send[...] = first

    @pl.when(pos[0] != 0)
    def _():
        keep[...] = first
        send[...] = second


def own_weights_kernel(keep_x, keep_g, out, wide):
    fill_windows(wide, keep_x[...])
    for tap in range(3):
        for side in range(3):
            rows = slice(tap * COLS, tap * COLS + PIX)
            lanes = slice(side * CH, (side + 1) * CH)
            at = (tap * 3 + side) * CH
            out[at : at + CH, :] = dot_tn(wide[rows, lanes], keep_g[...])


def space_weights_kernel(partial, recv_x, recv_g, keep_t, recv_t, out, wide):
    fill_windows(wide, recv_x[...])
    for tap in range(3):
        for side in range(3):
            rows = slice(tap * COLS, tap * COLS + PIX)
            lanes = slice(side * CH, (side + 1) * CH)
            at = (tap * 3 + side) * CH
            total = partial[at : at + CH, :] + dot_tn(wide[rows, lanes], recv_g[...])
            out[at : at + CH, :] = (total * SCALE).astype(BF)
    out[9 * CH : 12 * CH, :] = (keep_t[...].astype(F32) + recv_t[...].astype(F32)).astype(BF)


def spread_kernel(owner, pieces, pos, half, *refs):
    spat1, spat2, time1, time2, stage, sems = refs[-6:]
    targets = [(spat2, time1), (spat1, time2)]
    rows = 3 * CH

    def copies(at):
        space, time = targets[at]
        for slot, piece in enumerate(pieces):
            target = space.at[pl.ds(piece * rows, rows)] if piece < 3 else time
            source = stage.at[pl.ds(slot * rows, rows)]
            yield pltpu.make_async_copy(source, target, sems.at[slot])

    for at in range(2):

        @pl.when((pos[0] ^ owner) == at)
        def _():
            for slot, copy in enumerate(copies(at)):
                part = slice(slot * rows, (slot + 1) * rows)
                stage[part, :] = half[part, :].astype(F32)
                copy.start()
            for copy in copies(at):
                copy.wait()


def input_kernel(first_grad, w1, out, wide):
    fill_windows(wide, first_grad[...])
    out[...] = back_from(wide, w1).astype(BF)


def swap_cores(values):
    return lax.ppermute(values, "core", [(0, 1), (1, 0)])


def swap_frames(values):
    blocks = values.reshape(PIX // COLS, COLS, CH)
    return lax.all_to_all(blocks, FRAME_AXES, 0, 0, tiled=True).reshape(PIX, CH)


def scatter_sum(values, axes, count):
    parts = values.reshape(count, -1, CH)
    arrived = lax.all_to_all(parts, axes, 0, 0, tiled=True)
    return jnp.sum(arrived.astype(F32), axis=0).astype(BF)


def gather_all(values, axes, count):
    copies = jnp.broadcast_to(values[None], (count,) + values.shape)
    return lax.all_to_all(copies, axes, 0, 0, tiled=True).reshape(-1, CH)


def body(video, cotangent, w_spat1, w_spat2, w_time1, w_time2):
    pos = lax.axis_index("core").astype(jnp.int32).reshape(1)
    w1, w2, wt1, wt2 = (w.reshape(-1, CH) for w in (w_spat1, w_spat2, w_time1, w_time2))
    rows = PIX // COLS
    slab = ((PIX, CH), BF)
    wide, tall = pltpu.VMEM((PAD, 3 * CH), BF), pltpu.VMEM((PAD, CH), BF)
    frame, lines = pltpu.VMEM((PIX, CH), BF), pltpu.VMEM((rows, COLS, CH), BF)
    both_slopes = pltpu.VMEM((2, PIX, CH), BF)
    space, time = pltpu.VMEM((9 * CH, CH), BF), pltpu.VMEM((3 * CH, CH), BF)
    conv_flops, time_flops = 2 * PIX * 9 * CH * CH, 2 * PIX * 3 * CH * CH

    both, slopes, keep_x, send_x = call(
        forward_kernel,
        [((rows, 2 * COLS, CH), BF), ((2, PIX, CH), BF), slab, slab],
        (pos, video.reshape(PIX, CH), cotangent.reshape(rows, COLS, CH), w1, w2),
        [frame, frame, pltpu.VMEM((rows, 2 * COLS, CH), BF), both_slopes, space, space, wide, pltpu.SemaphoreType.DMA((15,))],
        2 * conv_flops,
        (1, 2, 3, 4),
        (0, 1, 2, 3),
        vmem=60,
    )
    both = lax.all_to_all(both, FRAME_AXES, 0, 0, tiled=True)
    recv_x = swap_cores(send_x)
    act_back, own = call(
        time_kernel,
        [slab, ((4, rows, COLS, CH), BF)],
        (both, wt1, wt2),
        [lines, lines, time, time, lines, lines, frame, tall, tall, tall, pltpu.SemaphoreType.DMA((10,))],
        3 * time_flops,
        (0, 1, 2),
        (0, 1),
        vmem=60,
    )
    act_back = swap_frames(act_back)
    taps = ((3 * CH, CH), BF)
    keep_t, send_t = call(
        time_weights_kernel, [taps, taps], (pos, own.reshape(4, PIX, CH)), (), 2 * time_flops
    )
    act_back, keep_t = lax.optimization_barrier((act_back, keep_t))
    recv_t = swap_cores(send_t)
    first_grad, keep_g, send_g = call(
        backward_kernel, [slab, slab, slab], (pos, act_back, slopes, w2), [wide], conv_flops
    )
    recv_g = swap_cores(send_g)
    (partial,) = call(
        own_weights_kernel, [((9 * CH, CH), F32)], (keep_x, keep_g), [wide], conv_flops
    )
    (part,) = call(
        space_weights_kernel,
        [((12 * CH, CH), BF)],
        (partial, recv_x, recv_g, keep_t, recv_t),
        [wide],
        conv_flops,
    )

    part = scatter_sum(part, ("zl", "x", "y"), 32)
    part, first_grad = lax.optimization_barrier((part, first_grad))
    (grad_input,) = call(input_kernel, [slab], (first_grad, w1), [wide], conv_flops)
    for pairs in (((0, 1), (1, 0), (2, 3), (3, 2)), ((0, 3), (3, 0), (1, 2), (2, 1))):
        arrived = lax.ppermute(part, "zh", pairs)
        arrived, grad_input = lax.optimization_barrier((arrived, grad_input))
        part = (part.astype(F32) + arrived.astype(F32)).astype(BF)
    part = gather_all(part, ("zl", "x", "y"), 32)
    grads = [((9 * CH, CH), F32)] * 2 + [((3 * CH, CH), F32)] * 2
    outs = []
    for owner, pieces in ((0, (0, 1, 2, 3)), (1, (0, 1)), (1, (2, 3))):
        piece = part[pieces[0] * 3 * CH : (pieces[-1] + 1) * 3 * CH]
        piece = swap_cores(piece) if owner else piece
        outs = call(
            functools.partial(spread_kernel, owner, pieces),
            grads,
            (pos, piece, *outs),
            [
                pltpu.VMEM((len(pieces) * 3 * CH, CH), F32),
                pltpu.SemaphoreType.DMA((len(pieces),)),
            ],
            0,
            (2, 3, 4, 5) if owner else (),
            (0, 1, 2, 3),
            {2: 0, 3: 1, 4: 2, 5: 3} if owner else None,
        )
    return (
        grad_input.reshape(video.shape),
        outs[0].reshape(w_spat1.shape),
        outs[1].reshape(w_spat2.shape),
        outs[2].reshape(w_time1.shape),
        outs[3].reshape(w_time2.shape),
    )


def solution(mesh):
    fine = Mesh(mesh.devices.reshape(4, 2, 4, 4, 2), ("zh", "zl", "x", "y", "core"))
    frames = P(("y", "core"), FRAME_AXES, None, None, None)
    return jax.shard_map(
        body,
        mesh=fine,
        in_specs=(frames, frames, P(), P(), P(), P()),
        out_specs=(frames, P(), P(), P(), P()),
        check_vma=False,
    )
```

```python
import functools
import math

import jax
import jax.numpy as jnp
from jax import lax
from jax.experimental import pallas as pl
from jax.experimental.pallas import tpu as pltpu
from jax.sharding import Mesh
from jax.sharding import PartitionSpec as P

CH = 256
COLS = 16
PIX = 512
HALF = PIX // 2
PAD = PIX + 2 * COLS
FRAME_AXES = ("zh", "zl", "x")
SCALE = 1.0 / math.sqrt(131072)
BF = jnp.bfloat16
F32 = jnp.float32
VMEM = pl.BlockSpec(memory_space=pltpu.VMEM)
SMEM = pl.BlockSpec(memory_space=pltpu.SMEM)
HBM = pl.BlockSpec(memory_space=pltpu.HBM)


def dot_nn(left, right):
    return lax.dot_general(left, right, (((1,), (0,)), ((), ())), preferred_element_type=F32)


def dot_nt(left, right):
    return lax.dot_general(left, right, (((1,), (1,)), ((), ())), preferred_element_type=F32)


def dot_tn(left, right):
    return lax.dot_general(left, right, (((0,), (0,)), ((), ())), preferred_element_type=F32)


def call(kernel, outs, ins, scratch=(), flops=0, hbm_in=(), hbm_out=(), aliases=None, vmem=40):
    specs = [SMEM if value.dtype == jnp.int32 else VMEM for value in ins]
    for at in hbm_in:
        specs[at] = HBM
    moved = sum(value.size * value.dtype.itemsize for value in ins)
    return pl.pallas_call(
        kernel,
        out_shape=[jax.ShapeDtypeStruct(shape, kind) for shape, kind in outs],
        in_specs=specs,
        out_specs=[HBM if at in hbm_out else VMEM for at in range(len(outs))],
        scratch_shapes=list(scratch),
        input_output_aliases=aliases or {},
        cost_estimate=pl.CostEstimate(flops=flops, bytes_accessed=moved, transcendentals=0),
        compiler_params=pltpu.CompilerParams(vmem_limit_bytes=vmem * 1024 * 1024),
    )(*ins)


def start_by_core(pos, sems, first, pairs):
    for at, (even, odd, target) in enumerate(pairs):

        @pl.when(pos[0] == 0)
        def _():
            pltpu.make_async_copy(even, target, sems.at[first + at]).start()

        @pl.when(pos[0] != 0)
        def _():
            pltpu.make_async_copy(odd, target, sems.at[first + at]).start()


def wait_by_core(sems, first, pairs):
    for at, (even, _, target) in enumerate(pairs):
        pltpu.make_async_copy(even, target, sems.at[first + at]).wait()


def fill_windows(wide, values):
    edge = jnp.zeros((COLS, 3 * CH), BF)
    wide[0:COLS, :] = edge
    wide[COLS + PIX : PAD, :] = edge
    column = lax.broadcasted_iota(jnp.int32, (PIX, CH), 0) & (COLS - 1)
    full = values.astype(F32)
    before = jnp.where(column == 0, 0.0, pltpu.roll(full, 1, 0))
    after = jnp.where(column == COLS - 1, 0.0, pltpu.roll(full, PIX - 1, 0))
    wide[COLS : COLS + PIX, 0:CH] = before.astype(BF)
    wide[COLS : COLS + PIX, CH : 2 * CH] = values.astype(BF)
    wide[COLS : COLS + PIX, 2 * CH : 3 * CH] = after.astype(BF)


def conv_half(wide, weight, half):
    total = None
    for tap in range(3):
        at = tap * COLS + half * HALF
        term = dot_nn(wide[at : at + HALF, :], weight[tap * 3 * CH : (tap + 1) * 3 * CH, :])
        total = term if total is None else total + term
    return total


def back_from(wide, weight):
    total = None
    for tap in range(3):
        for side in range(3):
            at = (tap * 3 + side) * CH
            term = dot_nt(
                wide[(2 - tap) * COLS : (2 - tap) * COLS + PIX, (2 - side) * CH : (3 - side) * CH],
                weight[at : at + CH, :],
            )
            total = term if total is None else total + term
    return total


def silu_pair(pre):
    sigma = 0.5 + 0.5 * jnp.tanh(0.5 * pre)
    act = pre * sigma
    return act, sigma * (1.0 + pre * (1.0 - sigma))


def forward_kernel(pos, video_at, cot_at, w1_at, w2_at, both_at, slopes_at, keep, send, *rest):
    video, first, both, slopes, w1, w2, wide, sems = rest
    pieces = [(video_at, video)]
    for source, target in ((w1_at, w1), (w2_at, w2)):
        for tap in range(3):
            part = pl.ds(tap * 3 * CH, 3 * CH)
            pieces.append((source.at[part], target.at[part]))
    pieces.append((cot_at, both.at[:, COLS : 2 * COLS, :]))
    pieces.append((slopes.at[0], slopes_at.at[0]))
    for half in range(2):
        part = pl.ds(half * HALF, HALF)
        pieces.append((slopes.at[1, part], slopes_at.at[1, part]))
        part = pl.ds(half * (HALF // COLS), HALF // COLS)
        pieces.append((both.at[part], both_at.at[part]))
    moves = [
        pltpu.make_async_copy(source, target, sems.at[at])
        for at, (source, target) in enumerate(pieces)
    ]
    for move in moves[0:8]:
        move.start()
    moves[0].wait()
    fill_windows(wide, video[...])
    for move in moves[1:4]:
        move.wait()
    for half in range(2):
        rows = slice(half * HALF, (half + 1) * HALF)
        act, slope = silu_pair(conv_half(wide, w1, half))
        first[rows, :] = act.astype(BF)
        slopes[0, rows, :] = slope.astype(BF)
    stores = [(first, video, keep), (video, first, send)]
    start_by_core(pos, sems, 13, stores)
    moves[8].start()
    fill_windows(wide, first[...])
    for move in moves[4:8]:
        move.wait()
    for half in range(2):
        rows = slice(half * HALF, (half + 1) * HALF)
        act, slope = silu_pair(conv_half(wide, w2, half))
        lines = HALF // COLS
        both[half * lines : (half + 1) * lines, 0:COLS, :] = act.astype(BF).reshape(lines, COLS, CH)
        slopes[1, rows, :] = slope.astype(BF)
    for move in moves[9:13]:
        move.start()
    for move in moves[8:13]:
        move.wait()
    wait_by_core(sems, 13, stores)


def ahead_sum(padded, weight, half):
    total = None
    for step in range(3):
        at = step * COLS + half * HALF
        term = dot_nt(padded[at : at + HALF, :], weight[step * CH : (step + 1) * CH, :])
        total = term if total is None else total + term
    return total


def time_kernel(both_at, wt1_at, wt2_at, back_at, own_at, *rest):
    act, cot, wt1, wt2, time_act, time_grad, act_back, behind, ahead, later, sems = rest
    loads = [
        pltpu.make_async_copy(source, target, sems.at[at])
        for at, (source, target) in enumerate(
            [
                (both_at.at[:, COLS : 2 * COLS, :], cot),
                (wt2_at, wt2),
                (both_at.at[:, 0:COLS, :], act),
                (wt1_at, wt1),
            ]
        )
    ]
    for load in loads:
        load.start()
    edge = jnp.zeros((2 * COLS, CH), BF)
    loads[0].wait()
    ahead[0:PIX, :] = cot[...].reshape(PIX, CH)
    ahead[PIX:PAD, :] = edge
    loads[2].wait()
    behind[0 : 2 * COLS, :] = edge
    behind[2 * COLS : PAD, :] = act[...].reshape(PIX, CH)
    loads[1].wait()
    loads[3].wait()
    for half in range(2):
        pre = None
        for step in range(3):
            at = (2 - step) * COLS + half * HALF
            term = dot_nn(behind[at : at + HALF, :], wt1[step * CH : (step + 1) * CH, :])
            pre = term if pre is None else pre + term
        value, slope = silu_pair(pre)
        grad = (ahead_sum(ahead, wt2, half) * slope).astype(BF)
        lines = slice(half * (HALF // COLS), (half + 1) * (HALF // COLS))
        time_act[lines] = value.astype(BF).reshape(HALF // COLS, COLS, CH)
        time_grad[lines] = grad.reshape(HALF // COLS, COLS, CH)
        later[half * HALF : (half + 1) * HALF, :] = grad
    later[PIX:PAD, :] = edge
    stores = [
        pltpu.make_async_copy(source, own_at.at[at], sems.at[4 + at])
        for at, source in enumerate((act, time_grad, time_act, cot))
    ]
    for store in stores:
        store.start()
    tails = []
    for half in range(2):
        rows = pl.ds(half * HALF, HALF)
        act_back[rows, :] = ahead_sum(later, wt1, half).astype(BF)
        tails.append(pltpu.make_async_copy(act_back.at[rows], back_at.at[rows], sems.at[8 + half]))
        tails[half].start()
    for move in stores + tails:
        move.wait()


def time_weights_kernel(pos, own, keep, send):
    for step in range(3):
        rows = PIX - step * COLS
        first = dot_tn(own[0, 0:rows, :], own[1, step * COLS : PIX, :]) * SCALE
        second = dot_tn(own[2, 0:rows, :], own[3, step * COLS : PIX, :]) * SCALE
        part = slice(step * CH, (step + 1) * CH)
        keep[part, :] = jnp.where(pos[0] == 0, first, second).astype(BF)
        send[part, :] = jnp.where(pos[0] == 0, second, first).astype(BF)


def backward_kernel(pos, act_back, slopes, w2, first_grad, keep, send, wide):
    second = (act_back[...].astype(F32) * slopes[1].astype(F32)).astype(BF)
    fill_windows(wide, second)
    first = (back_from(wide, w2) * slopes[0].astype(F32)).astype(BF)
    first_grad[...] = first

    @pl.when(pos[0] == 0)
    def _():
        keep[...] = second
        send[...] = first

    @pl.when(pos[0] != 0)
    def _():
        keep[...] = first
        send[...] = second


def own_weights_kernel(keep_x, keep_g, out, wide):
    fill_windows(wide, keep_x[...])
    for tap in range(3):
        for side in range(3):
            rows = slice(tap * COLS, tap * COLS + PIX)
            lanes = slice(side * CH, (side + 1) * CH)
            at = (tap * 3 + side) * CH
            out[at : at + CH, :] = dot_tn(wide[rows, lanes], keep_g[...])


def space_weights_kernel(partial, recv_x, recv_g, keep_t, recv_t, out, wide):
    fill_windows(wide, recv_x[...])
    for tap in range(3):
        for side in range(3):
            rows = slice(tap * COLS, tap * COLS + PIX)
            lanes = slice(side * CH, (side + 1) * CH)
            at = (tap * 3 + side) * CH
            total = partial[at : at + CH, :] + dot_tn(wide[rows, lanes], recv_g[...])
            out[at : at + CH, :] = (total * SCALE).astype(BF)
    out[9 * CH : 12 * CH, :] = (keep_t[...].astype(F32) + recv_t[...].astype(F32)).astype(BF)


def spread_kernel(owner, pieces, pos, half, *refs):
    spat1, spat2, time1, time2, stage, sems = refs[-6:]
    targets = [(spat2, time1), (spat1, time2)]
    rows = 3 * CH

    def copies(at):
        space, time = targets[at]
        for slot, piece in enumerate(pieces):
            target = space.at[pl.ds(piece * rows, rows)] if piece < 3 else time
            source = stage.at[pl.ds(slot * rows, rows)]
            yield pltpu.make_async_copy(source, target, sems.at[slot])

    for at in range(2):

        @pl.when((pos[0] ^ owner) == at)
        def _():
            for slot, copy in enumerate(copies(at)):
                part = slice(slot * rows, (slot + 1) * rows)
                stage[part, :] = half[part, :].astype(F32)
                copy.start()
            for copy in copies(at):
                copy.wait()


def input_kernel(first_grad, w1, out, wide):
    fill_windows(wide, first_grad[...])
    out[...] = back_from(wide, w1).astype(BF)


def swap_cores(values):
    return lax.ppermute(values, "core", [(0, 1), (1, 0)])


def swap_frames(values):
    blocks = values.reshape(PIX // COLS, COLS, CH)
    return lax.all_to_all(blocks, FRAME_AXES, 0, 0, tiled=True).reshape(PIX, CH)


def scatter_sum(values, axes, count):
    parts = values.reshape(count, -1, CH)
    arrived = lax.all_to_all(parts, axes, 0, 0, tiled=True)
    return jnp.sum(arrived.astype(F32), axis=0).astype(BF)


def gather_all(values, axes, count):
    copies = jnp.broadcast_to(values[None], (count,) + values.shape)
    return lax.all_to_all(copies, axes, 0, 0, tiled=True).reshape(-1, CH)


def body(video, cotangent, w_spat1, w_spat2, w_time1, w_time2):
    pos = lax.axis_index("core").astype(jnp.int32).reshape(1)
    w1, w2, wt1, wt2 = (w.reshape(-1, CH) for w in (w_spat1, w_spat2, w_time1, w_time2))
    rows = PIX // COLS
    slab = ((PIX, CH), BF)
    wide, tall = pltpu.VMEM((PAD, 3 * CH), BF), pltpu.VMEM((PAD, CH), BF)
    frame, lines = pltpu.VMEM((PIX, CH), BF), pltpu.VMEM((rows, COLS, CH), BF)
    both_slopes = pltpu.VMEM((2, PIX, CH), BF)
    space, time = pltpu.VMEM((9 * CH, CH), BF), pltpu.VMEM((3 * CH, CH), BF)
    conv_flops, time_flops = 2 * PIX * 9 * CH * CH, 2 * PIX * 3 * CH * CH

    both, slopes, keep_x, send_x = call(
        forward_kernel,
        [((rows, 2 * COLS, CH), BF), ((2, PIX, CH), BF), slab, slab],
        (pos, video.reshape(PIX, CH), cotangent.reshape(rows, COLS, CH), w1, w2),
        [frame, frame, pltpu.VMEM((rows, 2 * COLS, CH), BF), both_slopes, space, space, wide, pltpu.SemaphoreType.DMA((15,))],
        2 * conv_flops,
        (1, 2, 3, 4),
        (0, 1, 2, 3),
        vmem=60,
    )
    both = lax.all_to_all(both, FRAME_AXES, 0, 0, tiled=True)
    recv_x = swap_cores(send_x)
    act_back, own = call(
        time_kernel,
        [slab, ((4, rows, COLS, CH), BF)],
        (both, wt1, wt2),
        [lines, lines, time, time, lines, lines, frame, tall, tall, tall, pltpu.SemaphoreType.DMA((10,))],
        3 * time_flops,
        (0, 1, 2),
        (0, 1),
        vmem=60,
    )
    act_back = swap_frames(act_back)
    taps = ((3 * CH, CH), BF)
    keep_t, send_t = call(
        time_weights_kernel, [taps, taps], (pos, own.reshape(4, PIX, CH)), (), 2 * time_flops
    )
    act_back, send_t, recv_x = lax.optimization_barrier((act_back, send_t, recv_x))
    recv_t = swap_cores(send_t)
    first_grad, keep_g, send_g = call(
        backward_kernel, [slab, slab, slab], (pos, act_back, slopes, w2), [wide], conv_flops
    )
    recv_g = swap_cores(send_g)
    (partial,) = call(
        own_weights_kernel, [((9 * CH, CH), F32)], (keep_x, keep_g), [wide], conv_flops
    )
    (part,) = call(
        space_weights_kernel,
        [((12 * CH, CH), BF)],
        (partial, recv_x, recv_g, keep_t, recv_t),
        [wide],
        conv_flops,
    )

    part = scatter_sum(part, ("zl", "x", "y"), 32)
    part, first_grad = lax.optimization_barrier((part, first_grad))
    (grad_input,) = call(input_kernel, [slab], (first_grad, w1), [wide], conv_flops)
    for pairs in (((0, 1), (1, 0), (2, 3), (3, 2)), ((0, 3), (3, 0), (1, 2), (2, 1))):
        arrived = lax.ppermute(part, "zh", pairs)
        arrived, grad_input = lax.optimization_barrier((arrived, grad_input))
        part = (part.astype(F32) + arrived.astype(F32)).astype(BF)
    part = gather_all(part, ("zl", "x", "y"), 32)
    grads = [((9 * CH, CH), F32)] * 2 + [((3 * CH, CH), F32)] * 2
    outs = []
    for owner, pieces in ((0, (0, 1, 2, 3)), (1, (0, 1)), (1, (2, 3))):
        piece = part[pieces[0] * 3 * CH : (pieces[-1] + 1) * 3 * CH]
        piece = swap_cores(piece) if owner else piece
        outs = call(
            functools.partial(spread_kernel, owner, pieces),
            grads,
            (pos, piece, *outs),
            [
                pltpu.VMEM((len(pieces) * 3 * CH, CH), F32),
                pltpu.SemaphoreType.DMA((len(pieces),)),
            ],
            0,
            (2, 3, 4, 5) if owner else (),
            (0, 1, 2, 3),
            {2: 0, 3: 1, 4: 2, 5: 3} if owner else None,
        )
    return (
        grad_input.reshape(video.shape),
        outs[0].reshape(w_spat1.shape),
        outs[1].reshape(w_spat2.shape),
        outs[2].reshape(w_time1.shape),
        outs[3].reshape(w_time2.shape),
    )


def solution(mesh):
    fine = Mesh(mesh.devices.reshape(4, 2, 4, 4, 2), ("zh", "zl", "x", "y", "core"))
    frames = P(("y", "core"), FRAME_AXES, None, None, None)
    return jax.shard_map(
        body,
        mesh=fine,
        in_specs=(frames, frames, P(), P(), P(), P()),
        out_specs=(frames, P(), P(), P(), P()),
        check_vma=False,
    )
```
